32 devices in a mesh: fsdp: 2 (over y), blk: 4 (over x, core), ulysses: 4 (over z).
Axes of the slice: x: 2, y: 2, z: 4, core: 2. Of those that a mesh axis runs over, the one named last changes fastest.
Arguments:
- tokens: bfloat16 [8192, 768], P(('fsdp', 'blk', 'ulysses')), may hold values from -6 to 6
- positions: int32 [8192], P(('fsdp', 'blk', 'ulysses')), may hold values from 0 to 4095, as said below
- cotangent: bfloat16 [8192, 768], P(('fsdp', 'blk', 'ulysses')), may hold values from -6 to 6
- ln1_gain: bfloat16 [768], P('fsdp'), may hold values from 0.099609375 to 1.8984375
- ln1_bias: bfloat16 [768], P('fsdp'), may hold values from -3 to 3
- ln2_gain: bfloat16 [768], P('fsdp'), may hold values from 0.099609375 to 1.8984375
- ln2_bias: bfloat16 [768], P('fsdp'), may hold values from -3 to 3
- qkv_weight: bfloat16 [768, 2304], P('fsdp'), may hold values from -0.21875 to 0.21875
- qkv_bias: bfloat16 [2304], P('fsdp'), may hold values from -2 to 2
- out_weight: bfloat16 [768, 768], P('fsdp'), may hold values from -3 to 3
- out_bias: bfloat16 [768], P('fsdp'), may hold values from -2 to 2
- up_weight: bfloat16 [768, 3072], P('fsdp'), may hold values from -0.21875 to 0.21875
- up_bias: bfloat16 [3072], P('fsdp'), may hold values from -2 to 2
- down_weight: bfloat16 [3072, 768], P('fsdp'), may hold values from -0.109375 to 0.109375
- down_bias: bfloat16 [768], P('fsdp'), may hold values from -2 to 2
Outputs:
- output: bfloat16 [8192, 768], P(('fsdp', 'blk', 'ulysses'))
- input_grad: bfloat16 [8192, 768], P(('fsdp', 'blk', 'ulysses'))
- ln1_gain_grad: float32 [768], P('fsdp')
- ln1_bias_grad: float32 [768], P('fsdp')
- ln2_gain_grad: float32 [768], P('fsdp')
- ln2_bias_grad: float32 [768], P('fsdp')
- qkv_weight_grad: float32 [768, 2304], P('fsdp')
- qkv_bias_grad: float32 [2304], P('fsdp')
- out_weight_grad: float32 [768, 768], P('fsdp')
- out_bias_grad: float32 [768], P('fsdp')
- up_weight_grad: float32 [768, 3072], P('fsdp')
- up_bias_grad: float32 [3072], P('fsdp')
- down_weight_grad: float32 [3072, 768], P('fsdp')
- down_bias_grad: float32 [768], P('fsdp')
The draws below stay inside these ranges and needn't reach their ends.
Inputs may be any that keep to these rules, and one draw needn't show every extreme that they name: Each sequence of 4096 tokens holds every position from 0 once; positions run in blocks of 128 consecutive ascending values, and the order of the blocks within a sequence is drawn.
All inputs are finite; a program needn't handle non-finite values.
Results may differ from the reference program's by a relative error of at most 0.018.
Values may be sent and summed in bfloat16 or wider, within the bound.
No kernel may reach another device: no remote copies, remote signals or barrier semaphores. Data moves between devices by JAX's collectives and lax.ppermute only.
A program may use at most 128 MiB of HBM per device.

```python
import jax
import jax.numpy as jnp
from jax import lax

D = 768
HEADS = 12
HEAD = 64
ROT = 16
FF = 3072
SEQ_LEN = 4096
STRETCH = 128
TOKENS = 8192
N_FSDP = 2


def draw_positions(key, part):
    key = jax.random.fold_in(key, 5)
    pieces = SEQ_LEN // STRETCH
    seq_keys = jax.random.split(key, N_FSDP)
    orders = jax.vmap(lambda k: jax.random.permutation(k, pieces))(seq_keys)
    within = jnp.arange(STRETCH, dtype=jnp.int32)
    return (orders.astype(jnp.int32)[:, :, None] * STRETCH + within[None, None, :]).reshape(-1).astype(jnp.int32)


def level_of(stream_key, dims, shards, smallest, top_value):
    loudness, own = 1.0, jax.random.fold_in(stream_key, 6)
    for position, parts in shards:
        draws = jnp.exp(jax.random.uniform(jax.random.fold_in(own, position), (parts,), jnp.float32, smallest / len(shards), top_value / len(shards)))
        loudness = loudness * jnp.repeat(draws, dims[position] // parts).reshape([-1 if axis == position else 1 for axis in range(len(dims))])
    return loudness


def noise(own_key, extent, width, limit, shards=(), kind=jnp.bfloat16):
    values = width * jax.random.normal(own_key, extent, jnp.float32)
    if shards:
        values = values * level_of(own_key, extent, shards, -0.22, 0.18)
    return jnp.clip(values, -limit, limit).astype(kind)


def setup_inputs(seed: int = 0) -> dict:
    streams_of = jax.random.split(jax.random.key(seed), 16)
    tokens = noise(streams_of[0], (TOKENS, D), 1.0, 6.0, ((0, 32),))
    positions = draw_positions(jax.random.fold_in(streams_of[15], 71), 0)
    cotangent = noise(streams_of[2], (TOKENS, D), 1.0, 6.0, ((0, 32),))
    ln1_gain = jnp.clip(1.0 + 0.18 * jax.random.normal(streams_of[3], (D,), jnp.float32), 0.099609375, 1.8984375).astype(jnp.bfloat16)
    ln1_bias = noise(streams_of[4], (D,), 0.3, 3.0, ((0, 2),))
    ln2_gain = jnp.clip(1.0 + 0.18 * jax.random.normal(streams_of[5], (D,), jnp.float32), 0.099609375, 1.8984375).astype(jnp.bfloat16)
    ln2_bias = noise(streams_of[6], (D,), 0.3, 3.0, ((0, 2),))
    qkv_weight = noise(streams_of[7], (D, 3 * D), D ** -0.5, 0.21875, ((0, 2),))
    qkv_bias = noise(streams_of[8], (3 * D,), 0.2, 2.0, ((0, 2),))
    out_weight = noise(streams_of[9], (D, D), (max(1, D // 192)) ** -0.5, 3.0, ((0, 2),))
    out_bias = noise(streams_of[10], (D,), 0.2, 2.0, ((0, 2),))
    up_weight = noise(streams_of[11], (D, FF), D ** -0.5, 0.21875, ((0, 2),))
    up_bias = noise(streams_of[12], (FF,), 0.2, 2.0, ((0, 2),))
    down_weight = noise(streams_of[13], (FF, D), FF ** -0.5, 0.109375, ((0, 2),))
    down_bias = noise(streams_of[14], (D,), 0.2, 2.0, ((0, 2),))
    return dict(tokens=tokens, positions=positions, cotangent=cotangent, ln1_gain=ln1_gain, ln1_bias=ln1_bias, ln2_gain=ln2_gain, ln2_bias=ln2_bias, qkv_weight=qkv_weight, qkv_bias=qkv_bias, out_weight=out_weight, out_bias=out_bias, up_weight=up_weight, up_bias=up_bias, down_weight=down_weight, down_bias=down_bias)


@jax.custom_vjp
def low(v):
    return lax.optimization_barrier(v.astype(jnp.bfloat16)).astype(jnp.float32)

@jax.custom_vjp
def low_back(v):
    return v

def low_keep(v):
    return (low(v), None)

def low_pass(kept, grad):
    return (grad,)

def back_keep(v):
    return (v, None)

def back_low(kept, grad):
    return (low(grad),)
low.defvjp(low_keep, low_pass)
low_back.defvjp(back_keep, back_low)

def layer_norm(values, gain, shift):
    center = lax.optimization_barrier(jnp.mean(values, -1, keepdims=True))
    offset = values - center
    spread = lax.optimization_barrier(jnp.mean(offset * offset, -1, keepdims=True))
    return offset * lax.rsqrt(spread + 1e-05) * gain + shift

def rotate(values, places):
    count = values.shape[0]
    cols = values.shape[1]
    heads = values.reshape(count, cols // HEAD, HEAD)
    halfway = ROT // 2
    freqs = 10000.0 ** (-(jnp.arange(halfway, dtype=jnp.float32) * 2.0) / ROT)
    angles = places.astype(jnp.float32)[:, None] * freqs[None, :]
    cosine = jnp.cos(angles)[:, None, :]
    sine = jnp.sin(angles)[:, None, :]
    first = heads[..., :halfway]
    second = heads[..., halfway:ROT]
    turned = jnp.concatenate([first * cosine - second * sine, second * cosine + first * sine, heads[..., ROT:]], -1)
    return turned.reshape(count, cols)

def product(left, right):
    return jnp.dot(left, right, precision=lax.Precision.HIGHEST)

def attention(queries, key_rows, value_rows, places):
    model_width = queries.shape[1]
    q_heads = queries.reshape(SEQ_LEN, HEADS, HEAD)
    k_heads = key_rows.reshape(SEQ_LEN, HEADS, HEAD)
    v_heads = value_rows.reshape(SEQ_LEN, HEADS, HEAD)
    block_len = min(512, SEQ_LEN)
    blocks = SEQ_LEN // block_len

    def one_block(q_block, q_places):
        scores = jnp.einsum('qhd,khd->hqk', q_block, k_heads, precision=lax.Precision.HIGHEST) * HEAD ** (-0.5)
        scores = low_back(scores)
        allowed = places[None, :] <= q_places[:, None]
        scores = jnp.where(allowed[None], scores, -1e+30)
        log_total = jax.nn.logsumexp(scores, -1, keepdims=True)
        weights = low(jnp.exp(scores - log_total))
        return jnp.einsum('hqk,khd->qhd', weights, v_heads, precision=lax.Precision.HIGHEST)
    checked = jax.checkpoint(one_block)
    result = lax.map(lambda block_pair: checked(block_pair[0], block_pair[1]), (q_heads.reshape(blocks, block_len, HEADS, HEAD), places.reshape(blocks, block_len)))
    return result.reshape(SEQ_LEN, model_width)

def layer(x_rows, places, params):
    ln1_g, ln1_b, ln2_g, ln2_b, w_qkv, b_qkv, w_out, b_out, w_up, b_up, w_down, b_down = params
    normed = low(layer_norm(x_rows, ln1_g, ln1_b))
    joined = product(normed, w_qkv) + b_qkv
    queries = low(rotate(low_back(joined[:, :D]), places))
    keys_rot = low(rotate(low_back(joined[:, D:2 * D]), places))
    values_in = low(low_back(joined[:, 2 * D:]))
    mixed = low(low_back(attention(queries, keys_rot, values_in, places)))
    attn_out = product(mixed, w_out) + b_out
    normed_two = low(layer_norm(x_rows, ln2_g, ln2_b))
    hidden = low_back(product(normed_two, w_up) + b_up)
    active = low(jax.nn.gelu(hidden, approximate=False))
    return x_rows + attn_out + product(active, w_down) + b_down

def reference(tokens, positions, cotangent, ln1_gain, ln1_bias, ln2_gain, ln2_bias, qkv_weight, qkv_bias, out_weight, out_bias, up_weight, up_bias, down_weight, down_bias):
    params = tuple((w.astype(jnp.float32) for w in (ln1_gain, ln1_bias, ln2_gain, ln2_bias, qkv_weight, qkv_bias, out_weight, out_bias, up_weight, up_bias, down_weight, down_bias)))
    inputs = tokens.astype(jnp.float32).reshape(N_FSDP, SEQ_LEN, D)
    places = positions.reshape(N_FSDP, SEQ_LEN)
    pulled = cotangent.astype(jnp.float32).reshape(N_FSDP, SEQ_LEN, D)

    def per_sequence(totals, item):
        x_rows, where_at, pull_in = item
        result, pullback = jax.vjp(lambda rows_in, *weights: layer(rows_in, where_at, weights), x_rows, *params)
        grads = pullback(pull_in)
        totals = tuple((a + b for a, b in zip(totals, grads[1:])))
        return (totals, (result.astype(jnp.bfloat16), grads[0].astype(jnp.bfloat16)))
    zeros = tuple((jnp.zeros_like(w) for w in params))
    totals, (outputs, input_grads) = lax.scan(per_sequence, zeros, (inputs, places, pulled))
    return (outputs.reshape(TOKENS, D), input_grads.reshape(TOKENS, D), totals[0], totals[1], totals[2], totals[3], totals[4], totals[5], totals[6], totals[7], totals[8], totals[9], totals[10], totals[11])
```

```python
import jax
import jax.numpy as jnp
from jax import lax
from jax.experimental import pallas as pl
from jax.experimental.pallas import tpu as pltpu
from jax.sharding import PartitionSpec as P

HEAD = 64
ROT = 16
STRETCH = 128
CHUNK = 2
BIG_NEG = -1e30

f32 = jnp.float32
bf16 = jnp.bfloat16


def layer_norm(values, gain, shift):
    center = jnp.mean(values, -1, keepdims=True)
    offset = values - center
    spread = jnp.mean(offset * offset, -1, keepdims=True)
    return offset * lax.rsqrt(spread + 1e-05) * gain + shift


def gelu_exact(values):
    return jax.nn.gelu(values, approximate=False)


def swap(values, axis, bits):
    count = lax.axis_size(axis)
    return lax.ppermute(values, axis, [(i, i ^ bits) for i in range(count)])


def bit_of(axis, bit):
    return (lax.axis_index(axis) // bit) % 2


def in_order(bit, mine, other, axis=0):
    return jnp.concatenate([jnp.where(bit == 0, mine, other), jnp.where(bit == 0, other, mine)], axis)


def by_device(pieces, index):
    step = 1
    while step < len(pieces):
        odd = (index // step) % 2 == 1
        pieces = [jnp.where(odd, pieces[i ^ step], pieces[i]) for i in range(len(pieces))]
        step *= 2
    return pieces


def add_half(halves, axis, bit):
    which = bit_of(axis, bit)
    got = swap(jnp.where(which == 0, halves[1], halves[0]), axis, bit)
    kept = jnp.where(which == 0, halves[0], halves[1])
    return (kept.astype(f32) + got.astype(f32)).astype(bf16)


def halves_of(values, axis):
    half = values.shape[axis] // 2
    return (
        lax.slice_in_dim(values, 0, half, axis=axis),
        lax.slice_in_dim(values, half, 2 * half, axis=axis),
    )


def share_half(values, axis, bit, dim):
    return in_order(bit_of(axis, bit), values, swap(values, axis, bit), dim)


def gather_small(shard):
    if lax.axis_size("fsdp") != 2:
        return lax.all_gather(shard[None], "fsdp", axis=0, tiled=True)
    return in_order(lax.axis_index("fsdp"), shard[None], swap(shard[None], "fsdp", 1))


def other_rows(shard):
    quarter = shard.shape[0] // 4
    place = bit_of("blk", 1) * 2 + bit_of("blk", 2)
    part = swap(lax.dynamic_slice_in_dim(shard, place * quarter, quarter), "fsdp", 1)
    return share_half(share_half(part, "blk", 2, 0), "blk", 1, 0)


def gather_rows(shard):
    if lax.axis_size("fsdp") != 2:
        return lax.all_gather(shard, "fsdp", axis=0, tiled=True)
    return in_order(lax.axis_index("fsdp"), shard, other_rows(shard))


def attend_kernel(rank, q_ref, g_ref, kv_ref, o_ref, dq_ref, dkv_ref, rows, lanes, sums, probs, order):
    n_keys = rank.shape[0]
    own = q_ref.shape[-1] // STRETCH
    wide = 2 * STRETCH
    span = CHUNK * STRETCH

    for t in range(n_keys):
        i, at = t // own, (t % own) * STRETCH
        both = jnp.concatenate(
            [kv_ref[i, 0, :, at : at + STRETCH], kv_ref[i, 1, :, at : at + STRETCH]], 0
        )
        place = rank[t]
        lanes[place] = both
        rows[place] = both.T
    sums[...] = jnp.zeros_like(sums)
    for a in range(own):
        before = jnp.int32(0)
        for b in range(own):
            before += (rank[b] < rank[a]).astype(jnp.int32)
        order[before] = a

    def side(j, part):
        return jnp.concatenate(
            [lanes[j * CHUNK + i, part * HEAD : (part + 1) * HEAD, :] for i in range(CHUNK)], 1
        )

    def keys(j):
        return rows[pl.ds(j * CHUNK, CHUNK)].reshape(span, 2 * HEAD)

    def pair(p, carry):
        a, b = order[2 * p], order[2 * p + 1]
        ra, rb = rank[a], rank[b]
        at_a = pl.ds(pl.multiple_of(a * STRETCH, STRETCH), STRETCH)
        at_b = pl.ds(pl.multiple_of(b * STRETCH, STRETCH), STRETCH)
        q = jnp.concatenate([q_ref[:, at_a], q_ref[:, at_b]], 1)
        g = jnp.concatenate([g_ref[:, at_a], g_ref[:, at_b]], 1)
        none = jnp.zeros_like(q)
        q_low = jnp.concatenate([q, none], 0)
        g_high = jnp.concatenate([none, g], 0)
        lane = lax.broadcasted_iota(jnp.int32, (1, wide), 1)
        q_place = jnp.where(lane < STRETCH, ra * STRETCH + lane, rb * STRETCH + lane - STRETCH)
        clear = ra // CHUNK
        total = (rb + CHUNK) // CHUNK

        def score(j, top, masked):
            s = jnp.dot(keys(j), q_low, preferred_element_type=f32)
            if masked:
                k_place = j * span + lax.broadcasted_iota(jnp.int32, (span, 1), 0)
                s = jnp.where(k_place <= q_place, s, BIG_NEG)
            probs[j] = s
            return jnp.maximum(top, jnp.max(s.reshape(span // 8, 8, wide), 0))

        top = jnp.full((8, wide), BIG_NEG, f32)
        top = lax.fori_loop(0, clear, lambda j, v: score(j, v, False), top)
        top = lax.fori_loop(clear, total, lambda j, v: score(j, v, True), top)
        top = jnp.max(top, 0, keepdims=True)

        def weigh(j, state):
            count, out = state
            weight = jnp.exp(probs[j] - top)
            probs[j] = weight
            count = count + jnp.sum(weight.reshape(span // 8, 8, wide), 0)
            out = out + jnp.dot(side(j, 1), weight.astype(bf16), preferred_element_type=f32)
            return count, out

        count, out = lax.fori_loop(
            0, total, weigh, (jnp.zeros((8, wide), f32), jnp.zeros((HEAD, wide), f32))
        )
        inverse = 1.0 / jnp.sum(count, 0, keepdims=True)
        out = out * inverse
        delta = jnp.sum(out * g.astype(f32), 0, keepdims=True)
        o_ref[:, at_a] = out[:, :STRETCH].astype(bf16)
        o_ref[:, at_b] = out[:, STRETCH:].astype(bf16)
        right = jnp.concatenate(
            [jnp.concatenate([g, none], 0).T, jnp.concatenate([none, q], 0).T], 0
        )

        def back(j, d_q):
            weight = probs[j] * inverse
            d_weight = jnp.dot(keys(j), g_high, preferred_element_type=f32)
            d_score = (weight * (d_weight - delta)).astype(bf16)
            left = jnp.concatenate([weight.astype(bf16), d_score], 1)
            sums[pl.ds(j * CHUNK, CHUNK)] += jnp.dot(
                left, right, preferred_element_type=f32
            ).reshape(CHUNK, STRETCH, 2 * HEAD)
            return d_q + jnp.dot(side(j, 0), d_score, preferred_element_type=f32)

        d_q = lax.fori_loop(0, total, back, jnp.zeros((HEAD, wide), f32))
        d_q = d_q * HEAD ** (-0.5)
        dq_ref[:, at_a] = d_q[:, :STRETCH]
        dq_ref[:, at_b] = d_q[:, STRETCH:]
        return carry

    lax.fori_loop(0, own // 2, pair, 0)
    for t in range(n_keys):
        i, at = t // own, (t % own) * STRETCH
        turned = sums[rank[t]].T.astype(bf16)
        dkv_ref[i, 1, :, at : at + STRETCH] = turned[:HEAD]
        dkv_ref[i, 0, :, at : at + STRETCH] = turned[HEAD:]


def attend(ranks, q, g, kv):
    heads, _, count = q.shape
    devices = kv.shape[0]
    n_keys = devices * count // STRETCH
    pairs = heads * 4 * HEAD * count * count * devices
    q_spec = pl.BlockSpec((None, HEAD, count), lambda h, *_: (h, 0, 0))
    kv_spec = pl.BlockSpec((devices, 2, None, HEAD, count), lambda h, *_: (0, 0, h, 0, 0))
    return pl.pallas_call(
        attend_kernel,
        grid_spec=pltpu.PrefetchScalarGridSpec(
            num_scalar_prefetch=1,
            grid=(heads,),
            in_specs=[q_spec, q_spec, kv_spec],
            out_specs=[q_spec, q_spec, kv_spec],
            scratch_shapes=[
                pltpu.VMEM((n_keys, STRETCH, 2 * HEAD), bf16),
                pltpu.VMEM((n_keys, 2 * HEAD, STRETCH), bf16),
                pltpu.VMEM((n_keys, STRETCH, 2 * HEAD), f32),
                pltpu.VMEM((n_keys // CHUNK, CHUNK * STRETCH, 2 * STRETCH), f32),
                pltpu.SMEM((count // STRETCH,), jnp.int32),
            ],
        ),
        out_shape=[
            jax.ShapeDtypeStruct(q.shape, bf16),
            jax.ShapeDtypeStruct(q.shape, f32),
            jax.ShapeDtypeStruct(kv.shape, bf16),
        ],
        compiler_params=pltpu.CompilerParams(vmem_limit_bytes=40 * 2**20),
        cost_estimate=pl.CostEstimate(
            flops=2 * pairs, bytes_accessed=4 * kv.size, transcendentals=pairs // 512
        ),
        name="attend",
    )(ranks, q, g, kv)


def angles_of(places):
    halfway = ROT // 2
    freqs = 10000.0 ** (-(jnp.arange(halfway, dtype=f32) * 2.0) / ROT)
    angles = freqs[:, None] * places.astype(f32)[None, :]
    return jnp.cos(angles), jnp.sin(angles)


def rotate(heads, cosine, sine):
    halfway = ROT // 2
    first = heads[:, :halfway]
    second = heads[:, halfway:ROT]
    return jnp.concatenate(
        [first * cosine - second * sine, second * cosine + first * sine, heads[:, ROT:]], 1
    )


def around(values):
    return [values] + [swap(values, "ulysses", j) for j in range(1, lax.axis_size("ulysses"))]


def mlp_pair(x, e, gain, shift, up_weight, up_bias, down_weight):
    side = lax.axis_index("fsdp")
    rows, width = x.shape
    units = up_weight.shape[1] // 2
    x_both = jnp.concatenate([x, swap(x, "fsdp", 1)], 0)
    e_both = jnp.concatenate([e, swap(e, "fsdp", 1)], 0)
    left, right = up_weight[:, :units], up_weight[:, units:]
    mine = jnp.where(side == 0, left, right)
    theirs = jnp.where(side == 0, right, left)
    up = in_order(side, mine, other_rows(theirs))
    normed = layer_norm(x_both.astype(f32), gain, shift).astype(bf16)
    hidden = jnp.dot(normed, up, preferred_element_type=f32) + up_bias.astype(f32)
    active_f, pull_gelu = jax.vjp(gelu_exact, hidden)
    active = active_f.astype(bf16)
    part = jnp.dot(active, down_weight, preferred_element_type=f32)
    out = part[:rows] + swap(part[rows:].astype(bf16), "fsdp", 1).astype(f32)
    d_active = jnp.einsum("td,fd->tf", e_both, down_weight, preferred_element_type=f32)
    d_hidden = pull_gelu(d_active)[0].astype(bf16)
    g_up_bias = jnp.sum(d_hidden.astype(f32), 0)
    d_part = jnp.einsum("tf,df->td", d_hidden, up, preferred_element_type=f32)
    d_normed = d_part[:rows] + swap(d_part[rows:].astype(bf16), "fsdp", 1).astype(f32)
    g_up = jnp.einsum(
        "td,tcf->cdf", normed, d_hidden.reshape(2 * rows, 2, units // 2), preferred_element_type=f32
    ).astype(bf16)
    g_down = jnp.einsum("tf,td->fd", active, e_both, preferred_element_type=f32).astype(bf16)
    g_down = g_down.reshape(2, units // 2, width)
    pieces = jnp.stack([g_up, g_down], 1).reshape(2, 2, 2, width // 2, width)
    sums = add_half((pieces[0], pieces[1]), "blk", 1)
    sums = add_half(halves_of(sums, 2), "blk", 2)
    sums = add_half(halves_of(sums, 2), "ulysses", 1)
    sums = add_half(halves_of(sums, 2), "ulysses", 2)
    got = swap(jnp.where(side == 0, sums[0, 1], sums[0, 0]), "fsdp", 1)
    kept = jnp.where(side == 0, sums[0, 0], sums[0, 1])
    sums = jnp.concatenate([in_order(side, kept[None], got[None]), sums[1]], 0)
    sums = share_half(sums, "ulysses", 2, 1)
    sums = share_half(sums, "ulysses", 1, 1)
    sums = share_half(sums, "blk", 2, 1)
    sums = share_half(sums[None], "blk", 1, 0).astype(f32)
    g_up = jnp.concatenate([sums[c, f] for f in range(2) for c in range(2)], 1)
    g_down = sums[:, 2:].reshape(2 * width, width)
    full_bias = jnp.where(side == 0, jnp.concatenate([g_up_bias, 0 * g_up_bias]), jnp.concatenate([0 * g_up_bias, g_up_bias]))
    return out, d_normed, g_up, g_down, full_bias


def mlp_gathered(x, e, gain, shift, up_weight, up_bias, down_weight):
    up, down = gather_rows(up_weight), gather_rows(down_weight)
    bias = gather_small(up_bias).reshape(-1)
    normed = layer_norm(x.astype(f32), gain, shift).astype(bf16)
    hidden = jnp.dot(normed, up, preferred_element_type=f32) + bias.astype(f32)
    active_f, pull_gelu = jax.vjp(gelu_exact, hidden)
    active = active_f.astype(bf16)
    out = jnp.dot(active, down, preferred_element_type=f32)
    g_down = jnp.einsum("tf,td->fd", active, e, preferred_element_type=f32)
    d_active = jnp.einsum("td,fd->tf", e, down, preferred_element_type=f32)
    d_hidden = pull_gelu(d_active)[0].astype(bf16)
    g_up = jnp.einsum("td,tf->df", normed, d_hidden, preferred_element_type=f32)
    d_normed = jnp.einsum("tf,df->td", d_hidden, up, preferred_element_type=f32)
    g_up, g_down = (
        lax.psum(
            lax.psum_scatter(g.astype(bf16), "fsdp", scatter_dimension=0, tiled=True),
            ("blk", "ulysses"),
        ).astype(f32)
        for g in (g_up, g_down)
    )
    return out, d_normed, g_up, g_down, jnp.sum(d_hidden.astype(f32), 0)


def attention_grads(grads):
    _, cols, width = grads.shape
    groups = lax.axis_size("ulysses")
    if lax.axis_size("fsdp") != 2:
        shards = lax.axis_size("fsdp")
        total = lax.psum(grads, ("blk", "fsdp"))
        total = lax.all_gather(total, "ulysses", axis=1, tiled=True)
        rows = width // shards
        first = lax.axis_index("fsdp") * rows
        g_qkv = lax.dynamic_slice_in_dim(total[:3], first, rows, 2)
        g_out = lax.dynamic_slice_in_dim(total[3], first, rows, 0)
        return g_qkv.reshape(3 * width, rows).T.astype(f32), g_out.astype(f32)
    side = lax.axis_index("fsdp")
    group = lax.axis_index("ulysses")
    half = width // 2
    grads = add_half(halves_of(grads, 1), "blk", 1)
    grads = add_half(halves_of(grads, 1), "blk", 2)
    rows = grads.shape[1]
    low, high = grads[:, :, :half], grads[:, :, half:]
    kept = jnp.where(side == 0, low[:3], high[:3])
    sent = jnp.where(side == 0, high[:3], low[:3])
    whole = jnp.stack([low[3], high[3]])
    kept = jnp.concatenate([kept, whole])
    got = swap(jnp.concatenate([sent, whole]), "fsdp", 1)
    kept = (kept.astype(f32) + got.astype(f32)).astype(bf16)[None]
    for bit in (1, 2):
        kept = share_half(kept, "ulysses", bit, 0)
    of_qkv = kept[:, :3].reshape(3 * groups, rows, half)
    of_out = jnp.where(side == 0, kept[: groups // 2, 3:], kept[groups // 2 :, 3:])
    kept = jnp.concatenate([of_qkv, of_out.reshape(groups, rows, half)])
    kept = share_half(kept, "blk", 2, 1)
    kept = share_half(kept, "blk", 1, 1)
    g_qkv = kept[: 3 * groups].reshape(groups, 3, cols, half).transpose(3, 1, 0, 2)
    g_out = kept[3 * groups :].reshape(groups // 2, 2, cols, half).transpose(0, 2, 1, 3)
    return g_qkv.reshape(half, 3 * width).astype(f32), g_out.reshape(half, width).astype(f32)


def sum_everywhere(values):
    for axis in ("blk", "ulysses", "fsdp"):
        step = 1
        while step < lax.axis_size(axis):
            values = values + swap(values, axis, step)
            step *= 2
    return values


def on_device(
    tokens,
    positions,
    cotangent,
    ln1_gain,
    ln1_bias,
    ln2_gain,
    ln2_bias,
    qkv_weight,
    qkv_bias,
    out_weight,
    out_bias,
    up_weight,
    up_bias,
    down_weight,
    down_bias,
):
    count, width = tokens.shape
    groups = lax.axis_size("ulysses")
    group = lax.axis_index("ulysses")
    shards = lax.axis_size("fsdp")
    cols = width // groups
    heads = cols // HEAD
    rows = count * groups

    x_all = jnp.concatenate(around(tokens), 0)
    w_qkv = gather_rows(qkv_weight)
    small = gather_small(
        jnp.concatenate([ln1_gain, ln1_bias, ln2_gain, ln2_bias, out_bias, down_bias, qkv_bias])
    )
    part = width // shards
    ln1_g, ln1_b, ln2_g, ln2_b, b_out, b_down = (
        small[:, i * part : (i + 1) * part].reshape(width).astype(f32) for i in range(6)
    )
    b_qkv = small[:, 6 * part :].reshape(3 * width).astype(f32)
    ranks = positions[::STRETCH] // STRETCH
    for axis in ("ulysses", "blk"):
        step = 1
        while step < lax.axis_size(axis):
            ranks = jnp.concatenate([ranks, swap(ranks, axis, step)])
            step *= 2
    places = (ranks[: rows // STRETCH, None] * STRETCH + jnp.arange(STRETCH)[None, :]).reshape(-1)
    cosine, sine = angles_of(places)
    e_all = jnp.concatenate(around(cotangent), 0)

    if shards == 2:
        mlp = mlp_pair
    else:
        mlp = mlp_gathered
    mlp_out, d_norm_two, g_up, g_down, g_up_bias = mlp(
        tokens, cotangent, ln2_g, ln2_b, up_weight, up_bias, down_weight
    )

    normed = layer_norm(x_all.astype(f32), ln1_g, ln1_b).astype(bf16)
    starts = [i * width + group * cols for i in range(3)]
    w_mine = jnp.concatenate([lax.dynamic_slice_in_dim(w_qkv, s, cols, 1) for s in starts], 1)
    b_mine = jnp.concatenate([lax.dynamic_slice_in_dim(b_qkv, s, cols, 0) for s in starts])
    joined = jnp.einsum("de,td->et", w_mine, normed, preferred_element_type=f32) + b_mine[:, None]
    joined = joined.reshape(3, heads, HEAD, rows)
    queries = (rotate(joined[0], cosine, sine).astype(bf16) * HEAD ** (-0.5)).astype(bf16)
    kv = jnp.stack([rotate(joined[1], cosine, sine).astype(bf16), joined[2].astype(bf16)])
    pieces = {0: kv}
    step = lax.axis_size("blk") // 2
    while step >= 1:
        for i in list(pieces):
            pieces[i ^ step] = swap(pieces[i], "blk", step)
        step //= 2
    kv_all = jnp.stack([pieces[i] for i in range(len(pieces))])

    w_out = gather_rows(out_weight)
    w_out_mine = lax.dynamic_slice_in_dim(w_out, group * cols, cols, 0)
    d_heads = jnp.einsum("ed,td->et", w_out_mine, e_all, preferred_element_type=f32).astype(bf16)
    mixed, d_q, d_kv = attend(ranks, queries, d_heads.reshape(heads, HEAD, rows), kv_all)

    mixed = mixed.reshape(cols, rows)
    back = [mixed[:, j * count : (j + 1) * count] for j in range(groups)]
    back = [back[0]] + [swap(back[j], "ulysses", j) for j in range(1, groups)]
    mixed_mine = jnp.concatenate(by_device(back, group), 0)
    attn_out = jnp.einsum("et,ed->td", mixed_mine, w_out, preferred_element_type=f32)
    x_float = tokens.astype(f32)
    output = (x_float + (attn_out + b_out) + (mlp_out + b_down)).astype(bf16)

    blks = lax.axis_size("blk")
    d_kv = [d_kv[i] for i in range(blks)]
    step = 1
    while step < blks:
        sent = [swap(d_kv[i], "blk", step) for i in range(step, blks, 2 * step)]
        kept = [d_kv[i] for i in range(0, blks, 2 * step)]
        total = [a.astype(f32) + b.astype(f32) for a, b in zip(kept, sent)]
        step *= 2
        if step < blks:
            total = [a.astype(bf16) for a in total]
        d_kv = [total[i // step] if i % step == 0 else None for i in range(blks)]
    d_kv = d_kv[0]
    d_joined = jnp.concatenate(
        [
            rotate(d_q, cosine, -sine).astype(bf16),
            rotate(d_kv[0], cosine, -sine).astype(bf16),
            d_kv[1].astype(bf16),
        ],
        0,
    ).reshape(3 * cols, rows)
    g_bias_mine = jnp.sum(d_joined.astype(f32), 1)
    g_qkv = jnp.dot(d_joined, normed, preferred_element_type=f32).astype(bf16)
    g_out = jnp.dot(mixed, e_all, preferred_element_type=f32).astype(bf16)
    g_qkv, g_out = attention_grads(
        jnp.concatenate([g_qkv.reshape(3, cols, width), g_out[None]])
    )

    back = [d_joined[:, j * count : (j + 1) * count] for j in range(groups)]
    back = [back[0]] + [swap(back[j], "ulysses", j) for j in range(1, groups)]
    back = by_device(back, group)
    d_mine = jnp.concatenate([back[z][i * cols : (i + 1) * cols] for i in range(3) for z in range(groups)], 0)
    d_norm_one = jnp.einsum("et,de->td", d_mine, w_qkv, preferred_element_type=f32)
    _, pull_one = jax.vjp(layer_norm, x_float, ln1_g, ln1_b)
    _, pull_two = jax.vjp(layer_norm, x_float, ln2_g, ln2_b)
    d_x_one, g_ln1_g, g_ln1_b = pull_one(d_norm_one)
    d_x_two, g_ln2_g, g_ln2_b = pull_two(d_norm_two)
    e_float = cotangent.astype(f32)
    input_grad = (e_float + d_x_one + d_x_two).astype(bf16)

    g_qkv_bias = jnp.zeros((3, groups, cols), f32)
    g_qkv_bias = lax.dynamic_update_slice(g_qkv_bias, g_bias_mine.reshape(3, 1, cols), (0, group, 0))
    vectors = [g_ln1_g, g_ln1_b, g_ln2_g, g_ln2_b, jnp.sum(e_float, 0), g_qkv_bias.reshape(-1), g_up_bias]
    summed = sum_everywhere(jnp.concatenate(vectors))
    results, start = [], 0
    for vector in vectors:
        mine = vector.shape[0] // shards
        results.append(lax.dynamic_slice_in_dim(summed, start + lax.axis_index("fsdp") * mine, mine))
        start += vector.shape[0]
    g_ln1_g, g_ln1_b, g_ln2_g, g_ln2_b, g_e, g_qkv_bias, g_up_bias = results
    return (
        output,
        input_grad,
        g_ln1_g,
        g_ln1_b,
        g_ln2_g,
        g_ln2_b,
        g_qkv,
        g_qkv_bias,
        g_out,
        g_e,
        g_up,
        g_up_bias,
        g_down,
        g_e,
    )


def solution(mesh):
    rows = P(("fsdp", "blk", "ulysses"), None)
    split, matrix = P("fsdp"), P("fsdp", None)
    return jax.shard_map(
        on_device,
        mesh=mesh,
        in_specs=(
            rows,
            P(("fsdp", "blk", "ulysses")),
            rows,
            split,
            split,
            split,
            split,
            matrix,
            split,
            matrix,
            split,
            matrix,
            split,
            matrix,
            split,
        ),
        out_specs=(
            rows,
            rows,
            split,
            split,
            split,
            split,
            matrix,
            split,
            matrix,
            split,
            matrix,
            split,
            matrix,
            split,
        ),
        check_vma=False,
    )
```

```python
import jax
import jax.numpy as jnp
from jax import lax
from jax.experimental import pallas as pl
from jax.experimental.pallas import tpu as pltpu
from jax.sharding import PartitionSpec as P

HEAD = 64
ROT = 16
STRETCH = 128
CHUNK = 8
BIG_NEG = -1e30

f32 = jnp.float32
bf16 = jnp.bfloat16


def layer_norm(values, gain, shift):
    center = jnp.mean(values, -1, keepdims=True)
    offset = values - center
    spread = jnp.mean(offset * offset, -1, keepdims=True)
    return offset * lax.rsqrt(spread + 1e-05) * gain + shift


def gelu_exact(values):
    return jax.nn.gelu(values, approximate=False)


def swap(values, axis, bits):
    count = lax.axis_size(axis)
    return lax.ppermute(values, axis, [(i, i ^ bits) for i in range(count)])


def after(values, *earlier):
    return lax.optimization_barrier((values, earlier))[0]


def bit_of(axis, bit):
    return (lax.axis_index(axis) // bit) % 2


def in_order(bit, mine, other, axis=0):
    return jnp.concatenate([jnp.where(bit == 0, mine, other), jnp.where(bit == 0, other, mine)], axis)


def by_device(pieces, index):
    step = 1
    while step < len(pieces):
        odd = (index // step) % 2 == 1
        pieces = [jnp.where(odd, pieces[i ^ step], pieces[i]) for i in range(len(pieces))]
        step *= 2
    return pieces


def add_half(halves, axis, bit):
    which = bit_of(axis, bit)
    got = swap(jnp.where(which == 0, halves[1], halves[0]), axis, bit)
    kept = jnp.where(which == 0, halves[0], halves[1])
    return (kept.astype(f32) + got.astype(f32)).astype(bf16)


def halves_of(values, axis):
    half = values.shape[axis] // 2
    return (
        lax.slice_in_dim(values, 0, half, axis=axis),
        lax.slice_in_dim(values, half, 2 * half, axis=axis),
    )


def share_half(values, axis, bit, dim):
    return in_order(bit_of(axis, bit), values, swap(values, axis, bit), dim)


def gather_small(shard):
    if lax.axis_size("fsdp") != 2:
        return lax.all_gather(shard[None], "fsdp", axis=0, tiled=True)
    return in_order(lax.axis_index("fsdp"), shard[None], swap(shard[None], "fsdp", 1))


def other_quarter(shard, *earlier):
    quarter = shard.shape[0] // 4
    place = bit_of("blk", 1) * 2 + bit_of("blk", 2)
    return swap(after(lax.dynamic_slice_in_dim(shard, place * quarter, quarter), *earlier), "fsdp", 1)


def whole_shard(part):
    return share_half(share_half(part, "blk", 2, 0), "blk", 1, 0)


def both_shards(shard, part):
    return in_order(lax.axis_index("fsdp"), shard, whole_shard(part))


def attend_kernel(rank, q_ref, g_ref, kv_ref, o_ref, dq_ref, keep_ref, send_ref, rows, lanes, sums, probs, order):
    heads = range(q_ref.shape[0])
    n_keys = rank.shape[0]
    own = q_ref.shape[-1] // STRETCH
    wide = 2 * STRETCH
    span = CHUNK * STRETCH

    for t in range(n_keys):
        i, at = t // own, (t % own) * STRETCH
        place = rank[t]
        for h in heads:
            both = jnp.concatenate(
                [kv_ref[i, 0, h, :, at : at + STRETCH], kv_ref[i, 1, h, :, at : at + STRETCH]], 0
            )
            lanes[h, place] = both
            rows[h, place] = both.T
            sums[h, t] = jnp.zeros((STRETCH, 2 * HEAD), f32)
    for a in range(own):
        before = jnp.int32(0)
        for b in range(own):
            before += (rank[b] < rank[a]).astype(jnp.int32)
        order[before] = a

    def side(h, j, part):
        first = part * HEAD
        return jnp.concatenate(
            [lanes[h, j * CHUNK + i, first : first + HEAD, :] for i in range(CHUNK)], 1
        )

    def keys(h, j):
        return rows[h, pl.ds(j * CHUNK, CHUNK)].reshape(span, 2 * HEAD)

    def pair(p, carry):
        a, b = order[2 * p], order[2 * p + 1]
        ra, rb = rank[a], rank[b]
        at_a = pl.ds(pl.multiple_of(a * STRETCH, STRETCH), STRETCH)
        at_b = pl.ds(pl.multiple_of(b * STRETCH, STRETCH), STRETCH)
        q = [jnp.concatenate([q_ref[h, :, at_a], q_ref[h, :, at_b]], 1) for h in heads]
        g = [jnp.concatenate([g_ref[h, :, at_a], g_ref[h, :, at_b]], 1) for h in heads]
        none = jnp.zeros_like(q[0])
        q_low = [jnp.concatenate([v, none], 0) for v in q]
        g_high = [jnp.concatenate([none, v], 0) for v in g]
        lane = lax.broadcasted_iota(jnp.int32, (1, wide), 1)
        q_place = jnp.where(lane < STRETCH, ra * STRETCH + lane, rb * STRETCH + lane - STRETCH)
        clear = ra // CHUNK
        total = (rb + CHUNK) // CHUNK

        def score(j, tops, masked):
            result = []
            for h in heads:
                s = jnp.dot(keys(h, j), q_low[h], preferred_element_type=f32)
                if masked:
                    k_place = j * span + lax.broadcasted_iota(jnp.int32, (span, 1), 0)
                    s = jnp.where(k_place <= q_place, s, BIG_NEG)
                probs[h, j] = s
                result.append(jnp.maximum(tops[h], jnp.max(s.reshape(span // 8, 8, wide), 0)))
            return tuple(result)

        tops = tuple(jnp.full((8, wide), BIG_NEG, f32) for _ in heads)
        tops = lax.fori_loop(0, clear, lambda j, v: score(j, v, False), tops)
        tops = lax.fori_loop(clear, total, lambda j, v: score(j, v, True), tops)
        tops = [jnp.max(v, 0, keepdims=True) for v in tops]

        def weigh(j, state):
            result = []
            for h in heads:
                count, out = state[h]
                weight = jnp.exp(probs[h, j] - tops[h])
                probs[h, j] = weight
                count = count + jnp.sum(weight.reshape(span // 8, 8, wide), 0)
                out = out + jnp.dot(side(h, j, 1), weight.astype(bf16), preferred_element_type=f32)
                result.append((count, out))
            return tuple(result)

        state = tuple((jnp.zeros((8, wide), f32), jnp.zeros((HEAD, wide), f32)) for _ in heads)
        state = lax.fori_loop(0, total, weigh, state)
        inverse, delta, right = [], [], []
        for h in heads:
            count, out = state[h]
            inverse.append(1.0 / jnp.sum(count, 0, keepdims=True))
            out = out * inverse[h]
            delta.append(jnp.sum(out * g[h].astype(f32), 0, keepdims=True))
            o_ref[h, :, at_a] = out[:, :STRETCH].astype(bf16)
            o_ref[h, :, at_b] = out[:, STRETCH:].astype(bf16)
            top = jnp.concatenate([g[h], none], 0).T
            right.append(jnp.concatenate([top, jnp.concatenate([none, q[h]], 0).T], 0))

        def back(j, d_q):
            result = []
            for h in heads:
                weight = probs[h, j] * inverse[h]
                d_weight = jnp.dot(keys(h, j), g_high[h], preferred_element_type=f32)
                d_score = (weight * (d_weight - delta[h])).astype(bf16)
                left = jnp.concatenate([weight.astype(bf16), d_score], 1)
                sums[h, pl.ds(j * CHUNK, CHUNK)] += jnp.dot(
                    left, right[h], preferred_element_type=f32
                ).reshape(CHUNK, STRETCH, 2 * HEAD)
                result.append(d_q[h] + jnp.dot(side(h, j, 0), d_score, preferred_element_type=f32))
            return tuple(result)

        d_q = lax.fori_loop(0, total, back, tuple(jnp.zeros((HEAD, wide), f32) for _ in heads))
        for h in heads:
            scaled = d_q[h] * HEAD ** (-0.5)
            dq_ref[h, :, at_a] = scaled[:, :STRETCH]
            dq_ref[h, :, at_b] = scaled[:, STRETCH:]
        return carry

    lax.fori_loop(0, own // 2, pair, 0)
    for t in range(n_keys):
        i, at = t // own, (t % own) * STRETCH
        to = keep_ref if i % 2 == 0 else send_ref
        for h in heads:
            turned = sums[h, rank[t]].T.astype(bf16)
            to[i // 2, 1, h, :, at : at + STRETCH] = turned[:HEAD]
            to[i // 2, 0, h, :, at : at + STRETCH] = turned[HEAD:]


def attend(ranks, q, g, kv):
    heads, _, count = q.shape
    devices = kv.shape[0]
    n_keys = devices * count // STRETCH
    pairs = heads * 4 * HEAD * count * count * devices
    q_spec = pl.BlockSpec(q.shape, lambda i, *_: (0, 0, 0))
    kv_spec = pl.BlockSpec(kv.shape, lambda i, *_: (0, 0, 0, 0, 0))
    half = (devices // 2,) + kv.shape[1:]
    half_spec = pl.BlockSpec(half, lambda i, *_: (0, 0, 0, 0, 0))
    return pl.pallas_call(
        attend_kernel,
        grid_spec=pltpu.PrefetchScalarGridSpec(
            num_scalar_prefetch=1,
            grid=(1,),
            in_specs=[q_spec, q_spec, kv_spec],
            out_specs=[q_spec, q_spec, half_spec, half_spec],
            scratch_shapes=[
                pltpu.VMEM((heads, n_keys, STRETCH, 2 * HEAD), bf16),
                pltpu.VMEM((heads, n_keys, 2 * HEAD, STRETCH), bf16),
                pltpu.VMEM((heads, n_keys, STRETCH, 2 * HEAD), f32),
                pltpu.VMEM((heads, n_keys // CHUNK, CHUNK * STRETCH, 2 * STRETCH), f32),
                pltpu.SMEM((count // STRETCH,), jnp.int32),
            ],
        ),
        out_shape=[
            jax.ShapeDtypeStruct(q.shape, bf16),
            jax.ShapeDtypeStruct(q.shape, f32),
            jax.ShapeDtypeStruct(half, bf16),
            jax.ShapeDtypeStruct(half, bf16),
        ],
        compiler_params=pltpu.CompilerParams(vmem_limit_bytes=56 * 2**20),
        cost_estimate=pl.CostEstimate(
            flops=12 * pairs, bytes_accessed=4 * kv.size, transcendentals=pairs // 512
        ),
        name="attend",
    )(ranks, q, g, kv)


def angles_of(places):
    halfway = ROT // 2
    freqs = 10000.0 ** (-(jnp.arange(halfway, dtype=f32) * 2.0) / ROT)
    angles = freqs[:, None] * places.astype(f32)[None, :]
    return jnp.cos(angles), jnp.sin(angles)


def rotate(heads, cosine, sine):
    halfway = ROT // 2
    first = heads[:, :halfway]
    second = heads[:, halfway:ROT]
    return jnp.concatenate(
        [first * cosine - second * sine, second * cosine + first * sine, heads[:, ROT:]], 1
    )


def around(values):
    return [values] + [swap(values, "ulysses", j) for j in range(1, lax.axis_size("ulysses"))]


def units_of(up_weight, side):
    units = up_weight.shape[1] // 2
    return jnp.where(side == 0, up_weight[:, :units], up_weight[:, units:])


def mlp_pair(x_both, e_both, gain, shift, up, up_bias, down_weight):
    side = lax.axis_index("fsdp")
    rows, width = x_both.shape[0] // 2, x_both.shape[1]
    units = up.shape[1]
    normed = layer_norm(x_both.astype(f32), gain, shift).astype(bf16)
    hidden = jnp.dot(normed, up, preferred_element_type=f32) + up_bias.astype(f32)
    active_f, pull_gelu = jax.vjp(gelu_exact, hidden)
    active = active_f.astype(bf16)
    part = jnp.dot(active, down_weight, preferred_element_type=f32)
    out = part[:rows] + swap(part[rows:].astype(bf16), "fsdp", 1).astype(f32)
    d_active = jnp.einsum("td,fd->tf", e_both, down_weight, preferred_element_type=f32)
    d_hidden = pull_gelu(d_active)[0].astype(bf16)
    g_up_bias = jnp.sum(d_hidden.astype(f32), 0)
    d_part = jnp.einsum("tf,df->td", d_hidden, up, preferred_element_type=f32)
    d_normed = d_part[:rows] + swap(d_part[rows:].astype(bf16), "fsdp", 1).astype(f32)
    g_up = jnp.einsum(
        "td,tcf->cdf", normed, d_hidden.reshape(2 * rows, 2, units // 2), preferred_element_type=f32
    ).astype(bf16)
    g_down = jnp.einsum("tf,td->fd", active, e_both, preferred_element_type=f32).astype(bf16)
    g_down = g_down.reshape(2, units // 2, width)
    pieces = jnp.stack([g_up, g_down], 1).reshape(2, 2, 2, width // 2, width)
    first = add_half((pieces[0], pieces[1]), "blk", 1)
    sums = add_half(halves_of(first, 2), "blk", 2)
    sums = add_half(halves_of(sums, 2), "ulysses", 1)
    sums = add_half(halves_of(sums, 2), "ulysses", 2)
    got = swap(jnp.where(side == 0, sums[0, 1], sums[0, 0]), "fsdp", 1)
    kept = jnp.where(side == 0, sums[0, 0], sums[0, 1])
    sums = jnp.concatenate([in_order(side, kept[None], got[None]), sums[1]], 0)
    sums = share_half(sums, "ulysses", 2, 1)
    sums = share_half(sums, "ulysses", 1, 1)
    sums = share_half(sums, "blk", 2, 1)
    sums = share_half(sums[None], "blk", 1, 0).astype(f32)
    g_up = jnp.concatenate([sums[c, f] for f in range(2) for c in range(2)], 1)
    g_down = sums[:, 2:].reshape(2 * width, width)
    none = jnp.zeros_like(g_up_bias)
    g_up_bias = jnp.concatenate([jnp.where(side == 0, g_up_bias, none), jnp.where(side == 0, none, g_up_bias)])
    return out, d_normed, g_up, g_down, g_up_bias, first


def mlp_gathered(x, e, gain, shift, up, bias, down):
    normed = layer_norm(x.astype(f32), gain, shift).astype(bf16)
    hidden = jnp.dot(normed, up, preferred_element_type=f32) + bias.astype(f32)
    active_f, pull_gelu = jax.vjp(gelu_exact, hidden)
    active = active_f.astype(bf16)
    out = jnp.dot(active, down, preferred_element_type=f32)
    g_down = jnp.einsum("tf,td->fd", active, e, preferred_element_type=f32)
    d_active = jnp.einsum("td,fd->tf", e, down, preferred_element_type=f32)
    d_hidden = pull_gelu(d_active)[0].astype(bf16)
    g_up = jnp.einsum("td,tf->df", normed, d_hidden, preferred_element_type=f32)
    d_normed = jnp.einsum("tf,df->td", d_hidden, up, preferred_element_type=f32)
    g_up, g_down = (
        lax.psum(
            lax.psum_scatter(g.astype(bf16), "fsdp", scatter_dimension=0, tiled=True),
            ("blk", "ulysses"),
        ).astype(f32)
        for g in (g_up, g_down)
    )
    return out, d_normed, g_up, g_down, jnp.sum(d_hidden.astype(f32), 0), d_hidden


def attention_grads(grads):
    _, cols, width = grads.shape
    groups = lax.axis_size("ulysses")
    if lax.axis_size("fsdp") != 2:
        shards = lax.axis_size("fsdp")
        total = lax.psum(grads, ("blk", "fsdp"))
        total = lax.all_gather(total, "ulysses", axis=1, tiled=True)
        rows = width // shards
        first = lax.axis_index("fsdp") * rows
        g_qkv = lax.dynamic_slice_in_dim(total[:3], first, rows, 2)
        g_out = lax.dynamic_slice_in_dim(total[3], first, rows, 0)
        return g_qkv.reshape(3 * width, rows).T.astype(f32), g_out.astype(f32)
    side = lax.axis_index("fsdp")
    group = lax.axis_index("ulysses")
    half = width // 2
    grads = add_half(halves_of(grads, 1), "blk", 1)
    grads = add_half(halves_of(grads, 1), "blk", 2)
    rows = grads.shape[1]
    low, high = grads[:, :, :half], grads[:, :, half:]
    kept = jnp.where(side == 0, low[:3], high[:3])
    sent = jnp.where(side == 0, high[:3], low[:3])
    whole = jnp.stack([low[3], high[3]])
    kept = jnp.concatenate([kept, whole])
    got = swap(jnp.concatenate([sent, whole]), "fsdp", 1)
    kept = (kept.astype(f32) + got.astype(f32)).astype(bf16)[None]
    for bit in (1, 2):
        kept = share_half(kept, "ulysses", bit, 0)
    of_qkv = kept[:, :3].reshape(3 * groups, rows, half)
    of_out = jnp.where(side == 0, kept[: groups // 2, 3:], kept[groups // 2 :, 3:])
    kept = jnp.concatenate([of_qkv, of_out.reshape(groups, rows, half)])
    kept = share_half(kept, "blk", 2, 1)
    kept = share_half(kept, "blk", 1, 1)
    g_qkv = kept[: 3 * groups].reshape(groups, 3, cols, half).transpose(3, 1, 0, 2)
    g_out = kept[3 * groups :].reshape(groups // 2, 2, cols, half).transpose(0, 2, 1, 3)
    return g_qkv.reshape(half, 3 * width).astype(f32), g_out.reshape(half, width).astype(f32)


def sum_everywhere(values):
    for axis in ("blk", "ulysses", "fsdp"):
        step = 1
        while step < lax.axis_size(axis):
            values = values + swap(values, axis, step)
            step *= 2
    return values


def on_device(
    tokens,
    positions,
    cotangent,
    ln1_gain,
    ln1_bias,
    ln2_gain,
    ln2_bias,
    qkv_weight,
    qkv_bias,
    out_weight,
    out_bias,
    up_weight,
    up_bias,
    down_weight,
    down_bias,
):
    count, width = tokens.shape
    groups = lax.axis_size("ulysses")
    group = lax.axis_index("ulysses")
    shards = lax.axis_size("fsdp")
    cols = width // groups
    heads = cols // HEAD
    rows = count * groups

    ranks = (positions[::STRETCH] // STRETCH).astype(bf16)[None]
    ranks = jnp.pad(ranks, ((0, 15), (0, width - ranks.shape[1])))
    x_all = around(jnp.concatenate([tokens, ranks]))
    ranks = jnp.concatenate([v[count, : count // STRETCH] for v in x_all]).astype(jnp.int32)
    x_all = jnp.concatenate([v[:count] for v in x_all], 0)
    step = 1
    while step < lax.axis_size("blk"):
        ranks = jnp.concatenate([ranks, swap(ranks, "blk", step)])
        step *= 2
    places = (ranks[: rows // STRETCH, None] * STRETCH + jnp.arange(STRETCH)[None, :]).reshape(-1)
    cosine, sine = angles_of(places)

    small = gather_small(
        jnp.concatenate([ln1_gain, ln1_bias, ln2_gain, ln2_bias, out_bias, down_bias, qkv_bias])
    )
    part = width // shards
    ln1_g, ln1_b, ln2_g, ln2_b, b_out, b_down = (
        small[:, i * part : (i + 1) * part].reshape(width).astype(f32) for i in range(6)
    )
    b_qkv = small[:, 6 * part :].reshape(3 * width).astype(f32)
    if shards == 2:
        side = lax.axis_index("fsdp")
        part_qkv = other_quarter(qkv_weight)
        x_e = swap(after(jnp.stack([tokens, cotangent]), part_qkv), "fsdp", 1)
        half_up = jnp.concatenate([units_of(up_weight, 1 - side), out_weight], 1)
        part_up = other_quarter(half_up, x_e)
        w_qkv = both_shards(qkv_weight, part_qkv)
        half_up = jnp.concatenate([units_of(up_weight, side), out_weight], 1)
        half_up = both_shards(half_up, part_up)
        w_up, w_out = half_up[:, :-width], half_up[:, -width:]
        x_mlp = jnp.concatenate([tokens, x_e[0]])
        e_mlp = jnp.concatenate([cotangent, x_e[1]])
        b_up, w_down, mlp = up_bias, down_weight, mlp_pair
    else:
        w_qkv, w_up, w_out, w_down = (
            lax.all_gather(w, "fsdp", axis=0, tiled=True)
            for w in (qkv_weight, up_weight, out_weight, down_weight)
        )
        b_up = gather_small(up_bias).reshape(-1)
        x_mlp, e_mlp, mlp = tokens, cotangent, mlp_gathered

    normed = layer_norm(x_all.astype(f32), ln1_g, ln1_b).astype(bf16)
    starts = [i * width + group * cols for i in range(3)]
    w_mine = jnp.concatenate([lax.dynamic_slice_in_dim(w_qkv, s, cols, 1) for s in starts], 1)
    b_mine = jnp.concatenate([lax.dynamic_slice_in_dim(b_qkv, s, cols, 0) for s in starts])
    joined = jnp.einsum("de,td->et", w_mine, normed, preferred_element_type=f32) + b_mine[:, None]
    joined = joined.reshape(3, heads, HEAD, rows)
    queries = (rotate(joined[0], cosine, sine).astype(bf16) * HEAD ** (-0.5)).astype(bf16)
    kv = jnp.stack([rotate(joined[1], cosine, sine).astype(bf16), joined[2].astype(bf16)])
    pieces = {0: kv}
    step = lax.axis_size("blk") // 2
    while step >= 1:
        for i in list(pieces):
            pieces[i ^ step] = swap(pieces[i], "blk", step)
        step //= 2
    kv_all = jnp.stack([pieces[i] for i in range(len(pieces))])

    x_mlp, w_up = after((x_mlp, w_up), kv)
    mlp_out, d_norm_two, g_up, g_down, g_up_bias, begun = mlp(
        x_mlp, e_mlp, ln2_g, ln2_b, w_up, b_up, w_down
    )

    e_all = jnp.concatenate(around(after(cotangent, x_all)), 0)
    w_out_mine = lax.dynamic_slice_in_dim(w_out, group * cols, cols, 0)
    d_heads = jnp.einsum("ed,td->et", w_out_mine, e_all, preferred_element_type=f32).astype(bf16)
    d_heads = after(d_heads, begun)
    mixed, d_q, kept, sent = attend(ranks, queries, d_heads.reshape(heads, HEAD, rows), kv_all)

    mixed = mixed.reshape(cols, rows)
    back = [mixed[:, j * count : (j + 1) * count] for j in range(groups)]
    back = [back[0]] + [swap(back[j], "ulysses", j) for j in range(1, groups)]
    mixed_mine = jnp.concatenate(by_device(back, group), 0)
    attn_out = jnp.einsum("et,ed->td", mixed_mine, w_out, preferred_element_type=f32)
    x_float = tokens.astype(f32)
    output = (x_float + (attn_out + b_out) + (mlp_out + b_down)).astype(bf16)

    total = kept.astype(f32) + swap(sent, "blk", 1).astype(f32)
    step = 1
    while total.shape[0] > 1:
        step *= 2
        sent = swap(total[1::2].astype(bf16), "blk", step)
        total = total[0::2] + sent.astype(f32)
    d_kv = total[0]
    d_joined = jnp.concatenate(
        [
            rotate(d_q, cosine, -sine).astype(bf16),
            rotate(d_kv[0], cosine, -sine).astype(bf16),
            d_kv[1].astype(bf16),
        ],
        0,
    ).reshape(3 * cols, rows)
    g_bias_mine = jnp.sum(d_joined.astype(f32), 1)
    g_qkv = jnp.dot(d_joined, normed, preferred_element_type=f32).astype(bf16)
    g_out = jnp.dot(mixed, e_all, preferred_element_type=f32).astype(bf16)
    g_qkv, g_out = attention_grads(
        jnp.concatenate([g_qkv.reshape(3, cols, width), g_out[None]])
    )

    back = [d_joined[:, j * count : (j + 1) * count] for j in range(groups)]
    back = [back[0]] + [swap(back[j], "ulysses", j) for j in range(1, groups)]
    back = by_device(back, group)
    d_mine = jnp.concatenate([back[z][i * cols : (i + 1) * cols] for i in range(3) for z in range(groups)], 0)
    d_norm_one = jnp.einsum("et,de->td", d_mine, w_qkv, preferred_element_type=f32)
    _, pull_one = jax.vjp(layer_norm, x_float, ln1_g, ln1_b)
    _, pull_two = jax.vjp(layer_norm, x_float, ln2_g, ln2_b)
    d_x_one, g_ln1_g, g_ln1_b = pull_one(d_norm_one)
    d_x_two, g_ln2_g, g_ln2_b = pull_two(d_norm_two)
    e_float = cotangent.astype(f32)
    input_grad = (e_float + d_x_one + d_x_two).astype(bf16)

    g_qkv_bias = jnp.zeros((3, groups, cols), f32)
    g_qkv_bias = lax.dynamic_update_slice(g_qkv_bias, g_bias_mine.reshape(3, 1, cols), (0, group, 0))
    vectors = [g_ln1_g, g_ln1_b, g_ln2_g, g_ln2_b, jnp.sum(e_float, 0), g_qkv_bias.reshape(-1), g_up_bias]
    summed = sum_everywhere(jnp.concatenate(vectors))
    results, start = [], 0
    for vector in vectors:
        mine = vector.shape[0] // shards
        results.append(lax.dynamic_slice_in_dim(summed, start + lax.axis_index("fsdp") * mine, mine))
        start += vector.shape[0]
    g_ln1_g, g_ln1_b, g_ln2_g, g_ln2_b, g_e, g_qkv_bias, g_up_bias = results
    return (
        output,
        input_grad,
        g_ln1_g,
        g_ln1_b,
        g_ln2_g,
        g_ln2_b,
        g_qkv,
        g_qkv_bias,
        g_out,
        g_e,
        g_up,
        g_up_bias,
        g_down,
        g_e,
    )


def solution(mesh):
    rows = P(("fsdp", "blk", "ulysses"), None)
    split, matrix = P("fsdp"), P("fsdp", None)
    return jax.shard_map(
        on_device,
        mesh=mesh,
        in_specs=(
            rows,
            P(("fsdp", "blk", "ulysses")),
            rows,
            split,
            split,
            split,
            split,
            matrix,
            split,
            matrix,
            split,
            matrix,
            split,
            matrix,
            split,
        ),
        out_specs=(
            rows,
            rows,
            split,
            split,
            split,
            split,
            matrix,
            split,
            matrix,
            split,
            matrix,
            split,
            matrix,
            split,
        ),
        check_vma=False,
    )
```

```python
import jax
import jax.numpy as jnp
from jax import lax
from jax.experimental import pallas as pl
from jax.experimental.pallas import tpu as pltpu
from jax.sharding import PartitionSpec as P

HEAD = 64
ROT = 16
STRETCH = 128
CHUNK = 8
BIG_NEG = -1e30

f32 = jnp.float32
bf16 = jnp.bfloat16


def layer_norm(values, gain, shift):
    center = jnp.mean(values, -1, keepdims=True)
    offset = values - center
    spread = jnp.mean(offset * offset, -1, keepdims=True)
    return offset * lax.rsqrt(spread + 1e-05) * gain + shift


def gelu_exact(values):
    return jax.nn.gelu(values, approximate=False)


def swap(values, axis, bits):
    count = lax.axis_size(axis)
    return lax.ppermute(values, axis, [(i, i ^ bits) for i in range(count)])


def after(values, *earlier):
    return lax.optimization_barrier((values, earlier))[0]


def bit_of(axis, bit):
    return (lax.axis_index(axis) // bit) % 2


def in_order(bit, mine, other, axis=0):
    return jnp.concatenate([jnp.where(bit == 0, mine, other), jnp.where(bit == 0, other, mine)], axis)


def by_device(pieces, index):
    step = 1
    while step < len(pieces):
        odd = (index // step) % 2 == 1
        pieces = [jnp.where(odd, pieces[i ^ step], pieces[i]) for i in range(len(pieces))]
        step *= 2
    return pieces


def add_half(halves, axis, bit):
    which = bit_of(axis, bit)
    got = swap(jnp.where(which == 0, halves[1], halves[0]), axis, bit)
    kept = jnp.where(which == 0, halves[0], halves[1])
    return (kept.astype(f32) + got.astype(f32)).astype(bf16)


def halves_of(values, axis):
    half = values.shape[axis] // 2
    return (
        lax.slice_in_dim(values, 0, half, axis=axis),
        lax.slice_in_dim(values, half, 2 * half, axis=axis),
    )


def share_half(values, axis, bit, dim):
    return in_order(bit_of(axis, bit), values, swap(values, axis, bit), dim)


def gather_small(shard):
    if lax.axis_size("fsdp") != 2:
        return lax.all_gather(shard[None], "fsdp", axis=0, tiled=True)
    return in_order(lax.axis_index("fsdp"), shard[None], swap(shard[None], "fsdp", 1))


def quarter_of(shard):
    quarter = shard.shape[0] // 4
    place = bit_of("blk", 1) * 2 + bit_of("blk", 2)
    return lax.dynamic_slice_in_dim(shard, place * quarter, quarter)


def both_shards(shard, half):
    return in_order(lax.axis_index("fsdp"), shard, share_half(half, "blk", 1, 0))


def attend_kernel(rank, q_ref, g_ref, kv_ref, o_ref, dq_ref, keep_ref, send_ref, rows, lanes, sums, probs, order):
    heads = range(q_ref.shape[0])
    n_keys = rank.shape[0]
    own = q_ref.shape[-1] // STRETCH
    wide = 2 * STRETCH
    span = CHUNK * STRETCH

    for t in range(n_keys):
        i, at = t // own, (t % own) * STRETCH
        place = rank[t]
        for h in heads:
            both = jnp.concatenate(
                [kv_ref[i, 0, h, :, at : at + STRETCH], kv_ref[i, 1, h, :, at : at + STRETCH]], 0
            )
            lanes[h, place] = both
            rows[h, place] = both.T
            sums[h, t] = jnp.zeros((STRETCH, 2 * HEAD), f32)
    for a in range(own):
        before = jnp.int32(0)
        for b in range(own):
            before += (rank[b] < rank[a]).astype(jnp.int32)
        order[before] = a

    def side(h, j, part):
        first = part * HEAD
        return jnp.concatenate(
            [lanes[h, j * CHUNK + i, first : first + HEAD, :] for i in range(CHUNK)], 1
        )

    def keys(h, j):
        return rows[h, pl.ds(j * CHUNK, CHUNK)].reshape(span, 2 * HEAD)

    def pair(p, carry):
        a, b = order[2 * p], order[2 * p + 1]
        ra, rb = rank[a], rank[b]
        at_a = pl.ds(pl.multiple_of(a * STRETCH, STRETCH), STRETCH)
        at_b = pl.ds(pl.multiple_of(b * STRETCH, STRETCH), STRETCH)
        q = [jnp.concatenate([q_ref[h, :, at_a], q_ref[h, :, at_b]], 1) for h in heads]
        g = [jnp.concatenate([g_ref[h, :, at_a], g_ref[h, :, at_b]], 1) for h in heads]
        none = jnp.zeros_like(q[0])
        q_low = [jnp.concatenate([v, none], 0) for v in q]
        g_high = [jnp.concatenate([none, v], 0) for v in g]
        lane = lax.broadcasted_iota(jnp.int32, (1, wide), 1)
        q_place = jnp.where(lane < STRETCH, ra * STRETCH + lane, rb * STRETCH + lane - STRETCH)
        clear = ra // CHUNK
        total = (rb + CHUNK) // CHUNK

        def score(j, tops, masked):
            result = []
            for h in heads:
                s = jnp.dot(keys(h, j), q_low[h], preferred_element_type=f32)
                if masked:
                    k_place = j * span + lax.broadcasted_iota(jnp.int32, (span, 1), 0)
                    s = jnp.where(k_place <= q_place, s, BIG_NEG)
                probs[h, j] = s
                result.append(jnp.maximum(tops[h], jnp.max(s.reshape(span // 8, 8, wide), 0)))
            return tuple(result)

        tops = tuple(jnp.full((8, wide), BIG_NEG, f32) for _ in heads)
        tops = lax.fori_loop(0, clear, lambda j, v: score(j, v, False), tops)
        tops = lax.fori_loop(clear, total, lambda j, v: score(j, v, True), tops)
        tops = [jnp.max(v, 0, keepdims=True) for v in tops]

        def weigh(j, state):
            result = []
            for h in heads:
                count, out = state[h]
                weight = jnp.exp(probs[h, j] - tops[h])
                probs[h, j] = weight
                count = count + jnp.sum(weight.reshape(span // 8, 8, wide), 0)
                out = out + jnp.dot(side(h, j, 1), weight.astype(bf16), preferred_element_type=f32)
                result.append((count, out))
            return tuple(result)

        state = tuple((jnp.zeros((8, wide), f32), jnp.zeros((HEAD, wide), f32)) for _ in heads)
        state = lax.fori_loop(0, total, weigh, state)
        inverse, delta, right = [], [], []
        for h in heads:
            count, out = state[h]
            inverse.append(1.0 / jnp.sum(count, 0, keepdims=True))
            out = out * inverse[h]
            delta.append(jnp.sum(out * g[h].astype(f32), 0, keepdims=True))
            o_ref[h, :, at_a] = out[:, :STRETCH].astype(bf16)
            o_ref[h, :, at_b] = out[:, STRETCH:].astype(bf16)
            top = jnp.concatenate([g[h], none], 0).T
            right.append(jnp.concatenate([top, jnp.concatenate([none, q[h]], 0).T], 0))

        def back(j, d_q):
            result = []
            for h in heads:
                weight = probs[h, j] * inverse[h]
                d_weight = jnp.dot(keys(h, j), g_high[h], preferred_element_type=f32)
                d_score = (weight * (d_weight - delta[h])).astype(bf16)
                left = jnp.concatenate([weight.astype(bf16), d_score], 1)
                sums[h, pl.ds(j * CHUNK, CHUNK)] += jnp.dot(
                    left, right[h], preferred_element_type=f32
                ).reshape(CHUNK, STRETCH, 2 * HEAD)
                result.append(d_q[h] + jnp.dot(side(h, j, 0), d_score, preferred_element_type=f32))
            return tuple(result)

        d_q = lax.fori_loop(0, total, back, tuple(jnp.zeros((HEAD, wide), f32) for _ in heads))
        for h in heads:
            scaled = d_q[h] * HEAD ** (-0.5)
            dq_ref[h, :, at_a] = scaled[:, :STRETCH]
            dq_ref[h, :, at_b] = scaled[:, STRETCH:]
        return carry

    lax.fori_loop(0, own // 2, pair, 0)
    for t in range(n_keys):
        i, at = t // own, (t % own) * STRETCH
        to = keep_ref if i % 2 == 0 else send_ref
        for h in heads:
            turned = sums[h, rank[t]].T.astype(bf16)
            to[i // 2, 1, h, :, at : at + STRETCH] = turned[:HEAD]
            to[i // 2, 0, h, :, at : at + STRETCH] = turned[HEAD:]


def attend(ranks, q, g, kv):
    heads, _, count = q.shape
    devices = kv.shape[0]
    n_keys = devices * count // STRETCH
    pairs = heads * 4 * HEAD * count * count * devices
    q_spec = pl.BlockSpec(q.shape, lambda i, *_: (0, 0, 0))
    kv_spec = pl.BlockSpec(kv.shape, lambda i, *_: (0, 0, 0, 0, 0))
    half = (devices // 2,) + kv.shape[1:]
    half_spec = pl.BlockSpec(half, lambda i, *_: (0, 0, 0, 0, 0))
    return pl.pallas_call(
        attend_kernel,
        grid_spec=pltpu.PrefetchScalarGridSpec(
            num_scalar_prefetch=1,
            grid=(1,),
            in_specs=[q_spec, q_spec, kv_spec],
            out_specs=[q_spec, q_spec, half_spec, half_spec],
            scratch_shapes=[
                pltpu.VMEM((heads, n_keys, STRETCH, 2 * HEAD), bf16),
                pltpu.VMEM((heads, n_keys, 2 * HEAD, STRETCH), bf16),
                pltpu.VMEM((heads, n_keys, STRETCH, 2 * HEAD), f32),
                pltpu.VMEM((heads, n_keys // CHUNK, CHUNK * STRETCH, 2 * STRETCH), f32),
                pltpu.SMEM((count // STRETCH,), jnp.int32),
            ],
        ),
        out_shape=[
            jax.ShapeDtypeStruct(q.shape, bf16),
            jax.ShapeDtypeStruct(q.shape, f32),
            jax.ShapeDtypeStruct(half, bf16),
            jax.ShapeDtypeStruct(half, bf16),
        ],
        compiler_params=pltpu.CompilerParams(vmem_limit_bytes=56 * 2**20),
        cost_estimate=pl.CostEstimate(
            flops=12 * pairs, bytes_accessed=4 * kv.size, transcendentals=pairs // 512
        ),
        name="attend",
    )(ranks, q, g, kv)


def angles_of(places):
    halfway = ROT // 2
    freqs = 10000.0 ** (-(jnp.arange(halfway, dtype=f32) * 2.0) / ROT)
    angles = freqs[:, None] * places.astype(f32)[None, :]
    return jnp.cos(angles), jnp.sin(angles)


def rotate(heads, cosine, sine):
    halfway = ROT // 2
    first = heads[:, :halfway]
    second = heads[:, halfway:ROT]
    return jnp.concatenate(
        [first * cosine - second * sine, second * cosine + first * sine, heads[:, ROT:]], 1
    )


def around(values):
    return [values] + [swap(values, "ulysses", j) for j in range(1, lax.axis_size("ulysses"))]


def to_tokens(values):
    groups = lax.axis_size("ulysses")
    count = values.shape[1] // groups
    pieces = [values[:, j * count : (j + 1) * count] for j in range(groups)]
    return [pieces[0]] + [swap(pieces[j], "ulysses", j) for j in range(1, groups)]


def units_of(up_weight, side):
    units = up_weight.shape[1] // 2
    return jnp.where(side == 0, up_weight[:, :units], up_weight[:, units:])


def mlp_pair(x_both, e_both, gain, shift, up, up_bias, down_weight, *meanwhile):
    side = lax.axis_index("fsdp")
    rows, width = x_both.shape[0] // 2, x_both.shape[1]
    units = up.shape[1]
    normed = layer_norm(x_both.astype(f32), gain, shift).astype(bf16)
    hidden = jnp.dot(normed, up, preferred_element_type=f32) + up_bias.astype(f32)
    active_f, pull_gelu = jax.vjp(gelu_exact, hidden)
    active = active_f.astype(bf16)
    part = jnp.dot(active, down_weight, preferred_element_type=f32)
    out = part[:rows] + swap(part[rows:].astype(bf16), "fsdp", 1).astype(f32)
    d_active = jnp.einsum("td,fd->tf", e_both, down_weight, preferred_element_type=f32)
    d_hidden = pull_gelu(d_active)[0].astype(bf16)
    g_up_bias = jnp.sum(d_hidden.astype(f32), 0)
    d_part = jnp.einsum("tf,df->td", d_hidden, up, preferred_element_type=f32)
    d_normed = d_part[:rows] + swap(d_part[rows:].astype(bf16), "fsdp", 1).astype(f32)
    active, d_hidden = after((active, d_hidden), *meanwhile)
    g_up = jnp.einsum(
        "td,tcf->cdf", normed, d_hidden.reshape(2 * rows, 2, units // 2), preferred_element_type=f32
    ).astype(bf16)
    g_down = jnp.einsum("tf,td->fd", active, e_both, preferred_element_type=f32).astype(bf16)
    g_down = g_down.reshape(2, units // 2, width)
    pieces = jnp.stack([g_up, g_down], 1).reshape(2, 2, 2, width // 2, width)
    first = add_half((pieces[0], pieces[1]), "blk", 1)
    sums = add_half(halves_of(first, 2), "blk", 2)
    sums = add_half(halves_of(sums, 2), "ulysses", 1)
    sums = add_half(halves_of(sums, 2), "ulysses", 2)
    got = swap(jnp.where(side == 0, sums[0, 1], sums[0, 0]), "fsdp", 1)
    kept = jnp.where(side == 0, sums[0, 0], sums[0, 1])
    sums = jnp.concatenate([in_order(side, kept[None], got[None]), sums[1]], 0)
    sums = share_half(sums, "ulysses", 2, 1)
    sums = share_half(sums, "ulysses", 1, 1)
    sums = share_half(sums, "blk", 2, 1)
    sums = share_half(sums[None], "blk", 1, 0).astype(f32)
    g_up = jnp.concatenate([sums[c, f] for f in range(2) for c in range(2)], 1)
    g_down = sums[:, 2:].reshape(2 * width, width)
    none = jnp.zeros_like(g_up_bias)
    g_up_bias = jnp.concatenate([jnp.where(side == 0, g_up_bias, none), jnp.where(side == 0, none, g_up_bias)])
    return out, d_normed, g_up, g_down, g_up_bias, first


def mlp_gathered(x, e, gain, shift, up, bias, down, *meanwhile):
    normed = layer_norm(x.astype(f32), gain, shift).astype(bf16)
    hidden = jnp.dot(normed, up, preferred_element_type=f32) + bias.astype(f32)
    active_f, pull_gelu = jax.vjp(gelu_exact, hidden)
    active = active_f.astype(bf16)
    out = jnp.dot(active, down, preferred_element_type=f32)
    g_down = jnp.einsum("tf,td->fd", active, e, preferred_element_type=f32)
    d_active = jnp.einsum("td,fd->tf", e, down, preferred_element_type=f32)
    d_hidden = pull_gelu(d_active)[0].astype(bf16)
    g_up = jnp.einsum("td,tf->df", normed, d_hidden, preferred_element_type=f32)
    d_normed = jnp.einsum("tf,df->td", d_hidden, up, preferred_element_type=f32)
    g_up, g_down = (
        lax.psum(
            lax.psum_scatter(g.astype(bf16), "fsdp", scatter_dimension=0, tiled=True),
            ("blk", "ulysses"),
        ).astype(f32)
        for g in (g_up, g_down)
    )
    return out, d_normed, g_up, g_down, jnp.sum(d_hidden.astype(f32), 0), d_hidden


def attention_grads(grads):
    _, cols, width = grads.shape
    groups = lax.axis_size("ulysses")
    if lax.axis_size("fsdp") != 2:
        shards = lax.axis_size("fsdp")
        total = lax.psum(grads, ("blk", "fsdp"))
        total = lax.all_gather(total, "ulysses", axis=1, tiled=True)
        rows = width // shards
        first = lax.axis_index("fsdp") * rows
        g_qkv = lax.dynamic_slice_in_dim(total[:3], first, rows, 2)
        g_out = lax.dynamic_slice_in_dim(total[3], first, rows, 0)
        return g_qkv.reshape(3 * width, rows).T.astype(f32), g_out.astype(f32), total
    side = lax.axis_index("fsdp")
    group = lax.axis_index("ulysses")
    half = width // 2
    grads = add_half(halves_of(grads, 1), "blk", 1)
    grads = add_half(halves_of(grads, 1), "blk", 2)
    begun, rows = grads, grads.shape[1]
    low, high = grads[:, :, :half], grads[:, :, half:]
    kept = jnp.where(side == 0, low[:3], high[:3])
    sent = jnp.where(side == 0, high[:3], low[:3])
    whole = jnp.stack([low[3], high[3]])
    kept = jnp.concatenate([kept, whole])
    got = swap(jnp.concatenate([sent, whole]), "fsdp", 1)
    kept = (kept.astype(f32) + got.astype(f32)).astype(bf16)[None]
    for bit in (1, 2):
        kept = share_half(kept, "ulysses", bit, 0)
    of_qkv = kept[:, :3].reshape(3 * groups, rows, half)
    of_out = jnp.where(side == 0, kept[: groups // 2, 3:], kept[groups // 2 :, 3:])
    kept = jnp.concatenate([of_qkv, of_out.reshape(groups, rows, half)])
    kept = share_half(kept, "blk", 2, 1)
    kept = share_half(kept, "blk", 1, 1)
    g_qkv = kept[: 3 * groups].reshape(groups, 3, cols, half).transpose(3, 1, 0, 2)
    g_out = kept[3 * groups :].reshape(groups // 2, 2, cols, half).transpose(0, 2, 1, 3)
    return g_qkv.reshape(half, 3 * width).astype(f32), g_out.reshape(half, width).astype(f32), begun


def sum_everywhere(values):
    for axis in ("blk", "ulysses", "fsdp"):
        step = 1
        while step < lax.axis_size(axis):
            values = values + swap(values, axis, step)
            step *= 2
    return values


def on_device(
    tokens,
    positions,
    cotangent,
    ln1_gain,
    ln1_bias,
    ln2_gain,
    ln2_bias,
    qkv_weight,
    qkv_bias,
    out_weight,
    out_bias,
    up_weight,
    up_bias,
    down_weight,
    down_bias,
):
    count, width = tokens.shape
    groups = lax.axis_size("ulysses")
    group = lax.axis_index("ulysses")
    shards = lax.axis_size("fsdp")
    cols = width // groups
    heads = cols // HEAD
    rows = count * groups

    ranks = (positions[::STRETCH] // STRETCH).astype(bf16)[None]
    ranks = jnp.pad(ranks, ((0, 15), (0, width - ranks.shape[1])))
    x_ranks = jnp.concatenate([tokens, ranks])
    if shards == 2:
        side = lax.axis_index("fsdp")
        quarter = quarter_of(qkv_weight)
        x_ranks, quarter = after((x_ranks, quarter))
        part_qkv = swap(quarter, "fsdp", 1)
        half_up = jnp.concatenate([units_of(up_weight, 1 - side), out_weight], 1)
        part_up = swap(after(quarter_of(half_up), part_qkv), "fsdp", 1)
        x_e = swap(after(jnp.stack([tokens, cotangent]), part_up), "fsdp", 1)
        w_qkv = both_shards(qkv_weight, share_half(part_qkv, "blk", 2, 0))
        half_up = share_half(part_up, "blk", 2, 0)
        x_all = after(around(x_ranks), w_qkv, half_up)
        mine = jnp.concatenate([units_of(up_weight, side), out_weight], 1)
        half_up = both_shards(mine, half_up)
        w_up, w_out = half_up[:, :-width], half_up[:, -width:]
        x_mlp = jnp.concatenate([tokens, x_e[0]])
        e_mlp = jnp.concatenate([cotangent, x_e[1]])
        b_up, w_down, mlp = up_bias, down_weight, mlp_pair
    else:
        x_all = around(x_ranks)
        w_qkv, w_up, w_out, w_down = (
            lax.all_gather(w, "fsdp", axis=0, tiled=True)
            for w in (qkv_weight, up_weight, out_weight, down_weight)
        )
        b_up = gather_small(up_bias).reshape(-1)
        x_mlp, e_mlp, mlp = tokens, cotangent, mlp_gathered
    ranks = jnp.concatenate([v[count, : count // STRETCH] for v in x_all]).astype(jnp.int32)
    x_all = jnp.concatenate([v[:count] for v in x_all], 0)
    step = 1
    while step < lax.axis_size("blk"):
        ranks = jnp.concatenate([ranks, swap(ranks, "blk", step)])
        step *= 2
    places = (ranks[: rows // STRETCH, None] * STRETCH + jnp.arange(STRETCH)[None, :]).reshape(-1)
    cosine, sine = angles_of(places)

    small = gather_small(
        jnp.concatenate([ln1_gain, ln1_bias, ln2_gain, ln2_bias, out_bias, down_bias, qkv_bias])
    )
    part = width // shards
    ln1_g, ln1_b, ln2_g, ln2_b, b_out, b_down = (
        small[:, i * part : (i + 1) * part].reshape(width).astype(f32) for i in range(6)
    )
    b_qkv = small[:, 6 * part :].reshape(3 * width).astype(f32)
    normed = layer_norm(x_all.astype(f32), ln1_g, ln1_b).astype(bf16)
    starts = [i * width + group * cols for i in range(3)]
    w_mine = jnp.concatenate([lax.dynamic_slice_in_dim(w_qkv, s, cols, 1) for s in starts], 1)
    b_mine = jnp.concatenate([lax.dynamic_slice_in_dim(b_qkv, s, cols, 0) for s in starts])
    joined = jnp.einsum("de,td->et", w_mine, normed, preferred_element_type=f32) + b_mine[:, None]
    joined = joined.reshape(3, heads, HEAD, rows)
    queries = (rotate(joined[0], cosine, sine).astype(bf16) * HEAD ** (-0.5)).astype(bf16)
    kv = jnp.stack([rotate(joined[1], cosine, sine).astype(bf16), joined[2].astype(bf16)])
    kv, ranks = after((kv, ranks))
    pieces = {0: kv}
    step = lax.axis_size("blk") // 2
    while step >= 1:
        for i in list(pieces):
            pieces[i ^ step] = swap(pieces[i], "blk", step)
        step //= 2
    kv_all = jnp.stack([pieces[i] for i in range(len(pieces))])

    d_mixed = jnp.einsum("ed,td->et", w_out, cotangent, preferred_element_type=f32).astype(bf16)
    d_heads = [lax.dynamic_slice_in_dim(d_mixed, (group ^ j) * cols, cols) for j in range(groups)]
    d_heads = [d_heads[0]] + [swap(d_heads[j], "ulysses", j) for j in range(1, groups)]
    d_heads = jnp.concatenate(d_heads, 1).reshape(heads, HEAD, rows)

    x_mlp, w_up = after((x_mlp, w_up), kv, d_mixed)
    mlp_out, d_norm_two, g_up, g_down, g_up_bias, begun = mlp(
        x_mlp, e_mlp, ln2_g, ln2_b, w_up, b_up, w_down, pieces[lax.axis_size("blk") // 2]
    )

    e_around = around(after(cotangent, begun))
    d_heads = after(d_heads, begun)
    mixed, d_q, kept, sent = attend(ranks, queries, d_heads, kv_all)

    total = kept.astype(f32) + swap(sent, "blk", 1).astype(f32)
    d_q = rotate(d_q, cosine, -sine).astype(bf16).reshape(cols, rows)
    back_q = to_tokens(after(d_q, total))
    step = 1
    while total.shape[0] > 1:
        step *= 2
        sent = swap(total[1::2].astype(bf16), "blk", step)
        total = total[0::2] + sent.astype(f32)
    mixed = mixed.reshape(cols, rows)
    e_all = jnp.concatenate(e_around, 0)
    g_out = jnp.dot(mixed, e_all, preferred_element_type=f32).astype(bf16)
    d_kv = jnp.concatenate([rotate(total[0, 0], cosine, -sine), total[0, 1]])
    d_kv = d_kv.astype(bf16).reshape(2 * cols, rows)
    d_joined = jnp.concatenate([d_q, d_kv])
    g_bias_mine = jnp.sum(d_joined.astype(f32), 1)
    g_qkv = jnp.dot(d_joined, normed, preferred_element_type=f32).astype(bf16)
    back_kv = to_tokens(d_kv)
    g_qkv, g_out, begun = attention_grads(
        jnp.concatenate([g_qkv.reshape(3, cols, width), g_out[None]])
    )
    back_q, back_kv = after((back_q, back_kv), begun)
    back_q, back_kv = by_device(back_q, group), by_device(back_kv, group)
    d_mine = jnp.concatenate(
        back_q + [v[:cols] for v in back_kv] + [v[cols:] for v in back_kv], 0
    )
    d_norm_one = jnp.einsum("et,de->td", d_mine, w_qkv, preferred_element_type=f32)
    x_float = tokens.astype(f32)
    _, pull_one = jax.vjp(layer_norm, x_float, ln1_g, ln1_b)
    _, pull_two = jax.vjp(layer_norm, x_float, ln2_g, ln2_b)
    d_x_one, g_ln1_g, g_ln1_b = pull_one(d_norm_one)
    d_x_two, g_ln2_g, g_ln2_b = pull_two(d_norm_two)
    e_float = cotangent.astype(f32)

    back = by_device(to_tokens(after(mixed, back_kv)), group)
    attn_out = jnp.einsum("et,ed->td", jnp.concatenate(back, 0), w_out, preferred_element_type=f32)
    output = (x_float + (attn_out + b_out) + (mlp_out + b_down)).astype(bf16)
    input_grad = (e_float + d_x_one + d_x_two).astype(bf16)

    g_qkv_bias = jnp.zeros((3, groups, cols), f32)
    g_qkv_bias = lax.dynamic_update_slice(g_qkv_bias, g_bias_mine.reshape(3, 1, cols), (0, group, 0))
    vectors = [g_ln1_g, g_ln1_b, g_ln2_g, g_ln2_b, jnp.sum(e_float, 0), g_qkv_bias.reshape(-1), g_up_bias]
    summed = sum_everywhere(jnp.concatenate(vectors))
    results, start = [], 0
    for vector in vectors:
        mine = vector.shape[0] // shards
        results.append(lax.dynamic_slice_in_dim(summed, start + lax.axis_index("fsdp") * mine, mine))
        start += vector.shape[0]
    g_ln1_g, g_ln1_b, g_ln2_g, g_ln2_b, g_e, g_qkv_bias, g_up_bias = results
    return (
        output,
        input_grad,
        g_ln1_g,
        g_ln1_b,
        g_ln2_g,
        g_ln2_b,
        g_qkv,
        g_qkv_bias,
        g_out,
        g_e,
        g_up,
        g_up_bias,
        g_down,
        g_e,
    )


def solution(mesh):
    rows = P(("fsdp", "blk", "ulysses"), None)
    split, matrix = P("fsdp"), P("fsdp", None)
    return jax.shard_map(
        on_device,
        mesh=mesh,
        in_specs=(
            rows,
            P(("fsdp", "blk", "ulysses")),
            rows,
            split,
            split,
            split,
            split,
            matrix,
            split,
            matrix,
            split,
            matrix,
            split,
            matrix,
            split,
        ),
        out_specs=(
            rows,
            rows,
            split,
            split,
            split,
            split,
            matrix,
            split,
            matrix,
            split,
            matrix,
            split,
            matrix,
            split,
        ),
        check_vma=False,
    )
```

```python
import jax
import jax.numpy as jnp
import numpy as np
from jax import lax
from jax.experimental import pallas as pl
from jax.experimental.pallas import tpu as pltpu
from jax.sharding import PartitionSpec as P

HEAD = 64
ROT = 16
STRETCH = 128
CHUNK = 8
BIG_NEG = -1e30

f32 = jnp.float32
bf16 = jnp.bfloat16


def layer_norm(values, gain, shift):
    center = jnp.mean(values, -1, keepdims=True)
    offset = values - center
    spread = jnp.mean(offset * offset, -1, keepdims=True)
    return offset * lax.rsqrt(spread + 1e-05) * gain + shift


def gelu_exact(values):
    return jax.nn.gelu(values, approximate=False)


def swap(values, axis, bits):
    count = lax.axis_size(axis)
    return lax.ppermute(values, axis, [(i, i ^ bits) for i in range(count)])


def after(values, *earlier):
    return lax.optimization_barrier((values, earlier))[0]


def bit_of(axis, bit):
    return (lax.axis_index(axis) // bit) % 2


def in_order(bit, mine, other, axis=0):
    return jnp.concatenate([jnp.where(bit == 0, mine, other), jnp.where(bit == 0, other, mine)], axis)


def by_device(pieces, index):
    step = 1
    while step < len(pieces):
        odd = (index // step) % 2 == 1
        pieces = [jnp.where(odd, pieces[i ^ step], pieces[i]) for i in range(len(pieces))]
        step *= 2
    return pieces


def add_half(halves, axis, bit):
    which = bit_of(axis, bit)
    got = swap(jnp.where(which == 0, halves[1], halves[0]), axis, bit)
    kept = jnp.where(which == 0, halves[0], halves[1])
    return (kept.astype(f32) + got.astype(f32)).astype(bf16)


def halves_of(values, axis):
    half = values.shape[axis] // 2
    return (
        lax.slice_in_dim(values, 0, half, axis=axis),
        lax.slice_in_dim(values, half, 2 * half, axis=axis),
    )


def share_half(values, axis, bit, dim):
    return in_order(bit_of(axis, bit), values, swap(values, axis, bit), dim)


def gather_small(shard):
    if lax.axis_size("fsdp") != 2:
        return lax.all_gather(shard[None], "fsdp", axis=0, tiled=True)
    return in_order(lax.axis_index("fsdp"), shard[None], swap(shard[None], "fsdp", 1))


def quarter_of(shard):
    quarter = shard.shape[0] // 4
    place = bit_of("blk", 1) * 2 + bit_of("blk", 2)
    return lax.dynamic_slice_in_dim(shard, place * quarter, quarter)


def both_shards(shard, half):
    return in_order(lax.axis_index("fsdp"), shard, share_half(half, "blk", 1, 0))


def attend_kernel(rank, q_ref, g_ref, *refs):
    kv_refs = refs[:-9]
    o_ref, dq_ref, keep_ref, send_ref, rows, lanes, sums, probs, order = refs[-9:]
    heads = range(q_ref.shape[0])
    cols = q_ref.shape[0] * HEAD
    n_keys = rank.shape[0]
    own = q_ref.shape[-1] // STRETCH
    wide = 2 * STRETCH
    span = CHUNK * STRETCH

    for t in range(n_keys):
        i, at = t // own, (t % own) * STRETCH
        place = rank[t]
        for h in heads:
            both = jnp.concatenate(
                [
                    kv_refs[i][first : first + HEAD, at : at + STRETCH]
                    for first in (h * HEAD, cols + h * HEAD)
                ],
                0,
            )
            lanes[h, place] = both
            rows[h, place] = both.T
            sums[h, t] = jnp.zeros((STRETCH, 2 * HEAD), f32)
    for a in range(own):
        before = jnp.int32(0)
        for b in range(own):
            before += (rank[b] < rank[a]).astype(jnp.int32)
        order[before] = a

    def side(h, j, part):
        first = part * HEAD
        return jnp.concatenate(
            [lanes[h, j * CHUNK + i, first : first + HEAD, :] for i in range(CHUNK)], 1
        )

    def keys(h, j):
        return rows[h, pl.ds(j * CHUNK, CHUNK)].reshape(span, 2 * HEAD)

    def pair(p, carry):
        a, b = order[2 * p], order[2 * p + 1]
        ra, rb = rank[a], rank[b]
        at_a = pl.ds(pl.multiple_of(a * STRETCH, STRETCH), STRETCH)
        at_b = pl.ds(pl.multiple_of(b * STRETCH, STRETCH), STRETCH)
        q = [jnp.concatenate([q_ref[h, :, at_a], q_ref[h, :, at_b]], 1) for h in heads]
        g = [jnp.concatenate([g_ref[h, :, at_a], g_ref[h, :, at_b]], 1) for h in heads]
        none = jnp.zeros_like(q[0])
        q_low = [jnp.concatenate([v, none], 0) for v in q]
        g_high = [jnp.concatenate([none, v], 0) for v in g]
        lane = lax.broadcasted_iota(jnp.int32, (1, wide), 1)
        q_place = jnp.where(lane < STRETCH, ra * STRETCH + lane, rb * STRETCH + lane - STRETCH)
        clear = ra // CHUNK
        total = (rb + CHUNK) // CHUNK

        def score(j, tops, masked):
            result = []
            for h in heads:
                s = jnp.dot(keys(h, j), q_low[h], preferred_element_type=f32)
                if masked:
                    k_place = j * span + lax.broadcasted_iota(jnp.int32, (span, 1), 0)
                    s = jnp.where(k_place <= q_place, s, BIG_NEG)
                probs[h, j] = s
                result.append(jnp.maximum(tops[h], jnp.max(s.reshape(span // 8, 8, wide), 0)))
            return tuple(result)

        tops = tuple(jnp.full((8, wide), BIG_NEG, f32) for _ in heads)
        tops = lax.fori_loop(0, clear, lambda j, v: score(j, v, False), tops)
        tops = lax.fori_loop(clear, total, lambda j, v: score(j, v, True), tops)
        tops = [jnp.max(v, 0, keepdims=True) for v in tops]

        def weigh(j, state):
            result = []
            for h in heads:
                count, out = state[h]
                weight = jnp.exp(probs[h, j] - tops[h])
                probs[h, j] = weight
                count = count + jnp.sum(weight.reshape(span // 8, 8, wide), 0)
                out = out + jnp.dot(side(h, j, 1), weight.astype(bf16), preferred_element_type=f32)
                result.append((count, out))
            return tuple(result)

        state = tuple((jnp.zeros((8, wide), f32), jnp.zeros((HEAD, wide), f32)) for _ in heads)
        state = lax.fori_loop(0, total, weigh, state)
        inverse, delta, right = [], [], []
        for h in heads:
            count, out = state[h]
            inverse.append(1.0 / jnp.sum(count, 0, keepdims=True))
            out = out * inverse[h]
            delta.append(jnp.sum(out * g[h].astype(f32), 0, keepdims=True))
            o_ref[h, :, at_a] = out[:, :STRETCH].astype(bf16)
            o_ref[h, :, at_b] = out[:, STRETCH:].astype(bf16)
            top = jnp.concatenate([g[h], none], 0).T
            right.append(jnp.concatenate([top, jnp.concatenate([none, q[h]], 0).T], 0))

        def back(j, d_q):
            result = []
            for h in heads:
                weight = probs[h, j] * inverse[h]
                d_weight = jnp.dot(keys(h, j), g_high[h], preferred_element_type=f32)
                d_score = (weight * (d_weight - delta[h])).astype(bf16)
                left = jnp.concatenate([weight.astype(bf16), d_score], 1)
                sums[h, pl.ds(j * CHUNK, CHUNK)] += jnp.dot(
                    left, right[h], preferred_element_type=f32
                ).reshape(CHUNK, STRETCH, 2 * HEAD)
                result.append(d_q[h] + jnp.dot(side(h, j, 0), d_score, preferred_element_type=f32))
            return tuple(result)

        d_q = lax.fori_loop(0, total, back, tuple(jnp.zeros((HEAD, wide), f32) for _ in heads))
        for h in heads:
            scaled = d_q[h] * HEAD ** (-0.5)
            dq_ref[h, :, at_a] = scaled[:, :STRETCH]
            dq_ref[h, :, at_b] = scaled[:, STRETCH:]
        return carry

    lax.fori_loop(0, own // 2, pair, 0)
    for t in range(n_keys):
        i, at = t // own, (t % own) * STRETCH
        to = keep_ref if i % 2 == 0 else send_ref
        for h in heads:
            turned = sums[h, rank[t]].T.astype(bf16)
            first = h * HEAD
            to[i // 2, cols + first : cols + first + HEAD, at : at + STRETCH] = turned[:HEAD]
            to[i // 2, first : first + HEAD, at : at + STRETCH] = turned[HEAD:]


def attend(ranks, q, g, kv):
    heads, _, count = q.shape
    devices = len(kv)
    n_keys = devices * count // STRETCH
    pairs = heads * 4 * HEAD * count * count * devices
    half = (devices // 2, 2 * heads * HEAD, count)
    q_spec = pl.BlockSpec(q.shape, lambda i, *_: (0, 0, 0))
    half_spec = pl.BlockSpec(half, lambda i, *_: (0, 0, 0))
    return pl.pallas_call(
        attend_kernel,
        grid_spec=pltpu.PrefetchScalarGridSpec(
            num_scalar_prefetch=1,
            grid=(1,),
            in_specs=[q_spec, q_spec] + [pl.BlockSpec(v.shape, lambda i, *_: (0, 0)) for v in kv],
            out_specs=[q_spec, q_spec, half_spec, half_spec],
            scratch_shapes=[
                pltpu.VMEM((heads, n_keys, STRETCH, 2 * HEAD), bf16),
                pltpu.VMEM((heads, n_keys, 2 * HEAD, STRETCH), bf16),
                pltpu.VMEM((heads, n_keys, STRETCH, 2 * HEAD), f32),
                pltpu.VMEM((heads, n_keys // CHUNK, CHUNK * STRETCH, 2 * STRETCH), f32),
                pltpu.SMEM((count // STRETCH,), jnp.int32),
            ],
        ),
        out_shape=[
            jax.ShapeDtypeStruct(q.shape, bf16),
            jax.ShapeDtypeStruct(q.shape, f32),
            jax.ShapeDtypeStruct(half, bf16),
            jax.ShapeDtypeStruct(half, bf16),
        ],
        compiler_params=pltpu.CompilerParams(vmem_limit_bytes=56 * 2**20),
        cost_estimate=pl.CostEstimate(
            flops=12 * pairs, bytes_accessed=16 * q.size * devices, transcendentals=pairs // 512
        ),
        name="attend",
    )(ranks, q, g, *kv)


def prepare_kernel(freqs, gain, shift, weight, bias, *refs):
    groups = len(refs) - 5
    x_refs = refs[:groups]
    normed_ref, q_ref, kv_ref, cos_ref, sin_ref = refs[groups:]
    count = normed_ref.shape[0] // groups
    cols = q_ref.shape[0]
    halfway = ROT // 2
    blocks = count // STRETCH
    lane = lax.broadcasted_iota(jnp.int32, (1, STRETCH), 1).astype(f32)
    kv_ref[2 * cols :, :] = jnp.zeros((kv_ref.shape[0] - 2 * cols, kv_ref.shape[1]), bf16)
    spots = lax.broadcasted_iota(jnp.int32, (1, STRETCH), 1)
    table = jnp.zeros((1, STRETCH), f32)
    for i, x_ref in enumerate(x_refs):
        at = i * count
        normed = layer_norm(x_ref[:count].astype(f32), gain[...], shift[...]).astype(bf16)
        normed_ref[at : at + count] = normed
        joined = jnp.dot(normed, weight[...], preferred_element_type=f32) + bias[...]
        joined = joined.T
        ranks = x_ref[count : count + 16, :STRETCH].astype(f32)[:1]
        places = []
        for b in range(blocks):
            rank = jnp.sum(jnp.where(spots == b, ranks, 0.0), 1, keepdims=True)
            places.append(rank * STRETCH + lane)
            table = jnp.where(spots == i * blocks + b, rank, table)
        angles = freqs[...] * jnp.concatenate(places, 1)
        cosine, sine = jnp.cos(angles), jnp.sin(angles)
        cos_ref[:, at : at + count] = cosine
        sin_ref[:, at : at + count] = sine
        for to, first, scale in ((q_ref, 0, HEAD ** (-0.5)), (kv_ref, cols, 1.0)):
            for h in range(cols // HEAD):
                low = first + h * HEAD
                one = joined[low : low + halfway]
                two = joined[low + halfway : low + ROT]
                rest = joined[low + ROT : low + HEAD]
                turned = jnp.concatenate(
                    [one * cosine - two * sine, two * cosine + one * sine, rest], 0
                ).astype(bf16)
                to[h * HEAD : (h + 1) * HEAD, at : at + count] = turned * jnp.bfloat16(scale)
        kv_ref[cols : 2 * cols, at : at + count] = joined[2 * cols :].astype(bf16)
    kv_ref[2 * cols :, :STRETCH] = jnp.broadcast_to(table, (16, STRETCH)).astype(bf16)


def prepare(gain, shift, weight, bias, x_all, count):
    width = weight.shape[0]
    cols = weight.shape[1] // 3
    rows = count * len(x_all)
    halfway = ROT // 2
    freqs = jnp.asarray(10000.0 ** (-np.arange(halfway) * 2.0 / ROT), f32)[:, None]
    return pl.pallas_call(
        prepare_kernel,
        out_shape=[
            jax.ShapeDtypeStruct((rows, width), bf16),
            jax.ShapeDtypeStruct((cols, rows), bf16),
            jax.ShapeDtypeStruct((2 * cols + 16, rows), bf16),
            jax.ShapeDtypeStruct((ROT // 2, rows), f32),
            jax.ShapeDtypeStruct((ROT // 2, rows), f32),
        ],
        compiler_params=pltpu.CompilerParams(vmem_limit_bytes=40 * 2**20),
        cost_estimate=pl.CostEstimate(
            flops=6 * cols * rows * width, bytes_accessed=8 * rows * width, transcendentals=0
        ),
        name="prepare",
    )(freqs, gain[None], shift[None], weight, bias[None], *x_all)


def rotate(heads, cosine, sine):
    halfway = ROT // 2
    first = heads[:, :halfway]
    second = heads[:, halfway:ROT]
    return jnp.concatenate(
        [first * cosine - second * sine, second * cosine + first * sine, heads[:, ROT:]], 1
    )


def around(values):
    return [values] + [swap(values, "ulysses", j) for j in range(1, lax.axis_size("ulysses"))]


def to_tokens(values):
    groups = lax.axis_size("ulysses")
    count = values.shape[1] // groups
    pieces = [values[:, j * count : (j + 1) * count] for j in range(groups)]
    return [pieces[0]] + [swap(pieces[j], "ulysses", j) for j in range(1, groups)]


def units_of(up_weight, side):
    units = up_weight.shape[1] // 2
    return jnp.where(side == 0, up_weight[:, :units], up_weight[:, units:])


def mlp_pair(x_both, e_both, gain, shift, up, up_bias, down_weight, *meanwhile):
    side = lax.axis_index("fsdp")
    rows, width = x_both.shape[0] // 2, x_both.shape[1]
    units = up.shape[1]
    normed = layer_norm(x_both.astype(f32), gain, shift).astype(bf16)
    hidden = jnp.dot(normed, up, preferred_element_type=f32) + up_bias.astype(f32)
    active_f, pull_gelu = jax.vjp(gelu_exact, hidden)
    active = active_f.astype(bf16)
    part = jnp.dot(active, down_weight, preferred_element_type=f32)
    out = part[:rows] + swap(part[rows:].astype(bf16), "fsdp", 1).astype(f32)
    d_active = jnp.einsum("td,fd->tf", e_both, down_weight, preferred_element_type=f32)
    d_hidden = pull_gelu(d_active)[0].astype(bf16)
    g_up_bias = jnp.sum(d_hidden.astype(f32), 0)
    d_part = jnp.einsum("tf,df->td", d_hidden, up, preferred_element_type=f32)
    d_normed = d_part[:rows] + swap(d_part[rows:].astype(bf16), "fsdp", 1).astype(f32)
    active, d_hidden = after((active, d_hidden), *meanwhile)
    g_up = jnp.einsum(
        "td,tcf->cdf", normed, d_hidden.reshape(2 * rows, 2, units // 2), preferred_element_type=f32
    ).astype(bf16)
    g_down = jnp.einsum("tf,td->fd", active, e_both, preferred_element_type=f32).astype(bf16)
    g_down = g_down.reshape(2, units // 2, width)
    pieces = jnp.stack([g_up, g_down], 1).reshape(2, 2, 2, width // 2, width)
    first = add_half((pieces[0], pieces[1]), "blk", 1)
    sums = add_half(halves_of(first, 2), "blk", 2)
    side, none = lax.axis_index("fsdp"), jnp.zeros_like(g_up_bias)
    g_up_bias = jnp.concatenate([jnp.where(side == 0, g_up_bias, none), jnp.where(side == 0, none, g_up_bias)])
    return out, d_normed, first, sums, g_up_bias


def finish_pair(sums, earlier):
    side = lax.axis_index("fsdp")
    sums = after(sums, earlier)
    sums = add_half(halves_of(sums, 2), "ulysses", 1)
    sums = add_half(halves_of(sums, 2), "ulysses", 2)
    got = swap(jnp.where(side == 0, sums[0, 1], sums[0, 0]), "fsdp", 1)
    kept = jnp.where(side == 0, sums[0, 0], sums[0, 1])
    sums = jnp.concatenate([in_order(side, kept[None], got[None]), sums[1]], 0)
    sums = share_half(sums, "ulysses", 2, 1)
    sums = share_half(sums, "ulysses", 1, 1)
    sums = share_half(sums, "blk", 2, 1)
    return place_mlp(bit_of("blk", 1), sums, swap(sums, "blk", 1))


def place_mlp_kernel(which, mine, other, up_ref, down_ref):
    width = mine.shape[-1]
    for c, ref in ((which[0], mine), (1 - which[0], other)):
        for f in range(2):
            at = pl.multiple_of((2 * f + c) * width, STRETCH)
            up_ref[:, pl.ds(at, width)] = ref[f].astype(f32)
            down_ref[c, f] = ref[2 + f].astype(f32)


def place_mlp(which, mine, other):
    _, rows, width = mine.shape
    step = rows // 4
    whole = pl.BlockSpec((4, step, width), lambda i, *_: (0, i, 0))
    up, down = pl.pallas_call(
        place_mlp_kernel,
        grid_spec=pltpu.PrefetchScalarGridSpec(
            num_scalar_prefetch=1,
            grid=(4,),
            in_specs=[whole, whole],
            out_specs=[
                pl.BlockSpec((step, 4 * width), lambda i, *_: (i, 0)),
                pl.BlockSpec((2, 2, step, width), lambda i, *_: (0, 0, i, 0)),
            ],
        ),
        out_shape=[
            jax.ShapeDtypeStruct((rows, 4 * width), f32),
            jax.ShapeDtypeStruct((2, 2, rows, width), f32),
        ],
        compiler_params=pltpu.CompilerParams(vmem_limit_bytes=32 * 2**20),
        cost_estimate=pl.CostEstimate(flops=0, bytes_accessed=12 * mine.size, transcendentals=0),
        name="place_mlp",
    )(which[None], mine, other)
    return up, down.reshape(4 * rows, width)


def place_qkv_kernel(which, mine, other, qkv_ref, out_ref):
    first = which[0] == 0
    rows, half = mine.shape[1:]
    width = 2 * half
    groups = mine.shape[0] // 4
    for t in range(3):
        blocks = []
        for z in range(groups):
            a, b = mine[3 * z + t], other[3 * z + t]
            blocks += [jnp.where(first, a, b), jnp.where(first, b, a)]
        qkv_ref[:, t * width : (t + 1) * width] = jnp.concatenate(blocks, 0).astype(f32).T
    for z in range(groups // 2):
        for side in range(2):
            a, b = mine[3 * groups + 2 * z + side], other[3 * groups + 2 * z + side]
            at = 2 * z * rows
            both = jnp.concatenate([jnp.where(first, a, b), jnp.where(first, b, a)], 0)
            out_ref[at : at + 2 * rows, side * half : (side + 1) * half] = both.astype(f32)


def place_qkv(which, mine, other):
    _, rows, half = mine.shape
    groups = mine.shape[0] // 4
    return pl.pallas_call(
        place_qkv_kernel,
        grid_spec=pltpu.PrefetchScalarGridSpec(
            num_scalar_prefetch=1,
            grid=(1,),
            in_specs=[pl.BlockSpec(mine.shape, lambda i, *_: (0, 0, 0))] * 2,
            out_specs=[
                pl.BlockSpec((half, 6 * half), lambda i, *_: (0, 0)),
                pl.BlockSpec((groups * rows, 2 * half), lambda i, *_: (0, 0)),
            ],
        ),
        out_shape=[
            jax.ShapeDtypeStruct((half, 6 * half), f32),
            jax.ShapeDtypeStruct((groups * rows, 2 * half), f32),
        ],
        compiler_params=pltpu.CompilerParams(vmem_limit_bytes=40 * 2**20),
        cost_estimate=pl.CostEstimate(flops=0, bytes_accessed=12 * mine.size, transcendentals=0),
        name="place_qkv",
    )(which[None], mine, other)


def mlp_gathered(x, e, gain, shift, up, bias, down, *meanwhile):
    normed = layer_norm(x.astype(f32), gain, shift).astype(bf16)
    hidden = jnp.dot(normed, up, preferred_element_type=f32) + bias.astype(f32)
    active_f, pull_gelu = jax.vjp(gelu_exact, hidden)
    active = active_f.astype(bf16)
    out = jnp.dot(active, down, preferred_element_type=f32)
    g_down = jnp.einsum("tf,td->fd", active, e, preferred_element_type=f32)
    d_active = jnp.einsum("td,fd->tf", e, down, preferred_element_type=f32)
    d_hidden = pull_gelu(d_active)[0].astype(bf16)
    g_up = jnp.einsum("td,tf->df", normed, d_hidden, preferred_element_type=f32)
    d_normed = jnp.einsum("tf,df->td", d_hidden, up, preferred_element_type=f32)
    g_up, g_down = (
        lax.psum(
            lax.psum_scatter(g.astype(bf16), "fsdp", scatter_dimension=0, tiled=True),
            ("blk", "ulysses"),
        ).astype(f32)
        for g in (g_up, g_down)
    )
    return out, d_normed, d_hidden, (g_up, g_down), jnp.sum(d_hidden.astype(f32), 0)


def attention_grads(grads):
    _, cols, width = grads.shape
    groups = lax.axis_size("ulysses")
    if lax.axis_size("fsdp") != 2:
        shards = lax.axis_size("fsdp")
        total = lax.psum(grads, ("blk", "fsdp"))
        total = lax.all_gather(total, "ulysses", axis=1, tiled=True)
        rows = width // shards
        first = lax.axis_index("fsdp") * rows
        g_qkv = lax.dynamic_slice_in_dim(total[:3], first, rows, 2)
        g_out = lax.dynamic_slice_in_dim(total[3], first, rows, 0)
        return g_qkv.reshape(3 * width, rows).T.astype(f32), g_out.astype(f32), total
    side = lax.axis_index("fsdp")
    group = lax.axis_index("ulysses")
    half = width // 2
    grads = add_half(halves_of(grads, 1), "blk", 1)
    grads = add_half(halves_of(grads, 1), "blk", 2)
    begun, rows = grads, grads.shape[1]
    low, high = grads[:, :, :half], grads[:, :, half:]
    kept = jnp.where(side == 0, low[:3], high[:3])
    sent = jnp.where(side == 0, high[:3], low[:3])
    whole = jnp.stack([low[3], high[3]])
    kept = jnp.concatenate([kept, whole])
    got = swap(jnp.concatenate([sent, whole]), "fsdp", 1)
    kept = (kept.astype(f32) + got.astype(f32)).astype(bf16)
    kept = jnp.stack(by_device(around(kept), group))
    of_qkv = kept[:, :3].reshape(3 * groups, rows, half)
    of_out = jnp.where(side == 0, kept[: groups // 2, 3:], kept[groups // 2 :, 3:])
    kept = jnp.concatenate([of_qkv, of_out.reshape(groups, rows, half)])
    kept = share_half(kept, "blk", 2, 1)
    g_qkv, g_out = place_qkv(bit_of("blk", 1), kept, swap(kept, "blk", 1))
    return g_qkv, g_out, begun


def sum_everywhere(values):
    for axis in ("blk", "ulysses", "fsdp"):
        step = 1
        while step < lax.axis_size(axis):
            values = values + swap(values, axis, step)
            step *= 2
    return values


def on_device(
    tokens,
    positions,
    cotangent,
    ln1_gain,
    ln1_bias,
    ln2_gain,
    ln2_bias,
    qkv_weight,
    qkv_bias,
    out_weight,
    out_bias,
    up_weight,
    up_bias,
    down_weight,
    down_bias,
):
    count, width = tokens.shape
    groups = lax.axis_size("ulysses")
    group = lax.axis_index("ulysses")
    shards = lax.axis_size("fsdp")
    cols = width // groups
    heads = cols // HEAD
    rows = count * groups

    ranks = (positions[::STRETCH] // STRETCH).astype(bf16)[None]
    ranks = jnp.pad(ranks, ((0, 15), (0, width - ranks.shape[1])))
    x_ranks = jnp.concatenate([tokens, ranks])
    if shards == 2:
        side = lax.axis_index("fsdp")
        quarter = quarter_of(qkv_weight)
        x_ranks, quarter = after((x_ranks, quarter))
        part_qkv = swap(quarter, "fsdp", 1)
        half_up = jnp.concatenate([units_of(up_weight, 1 - side), out_weight], 1)
        part_up = swap(after(quarter_of(half_up), part_qkv), "fsdp", 1)
        x_e = swap(after(jnp.stack([tokens, cotangent]), part_up), "fsdp", 1)
        w_qkv = both_shards(qkv_weight, share_half(part_qkv, "blk", 2, 0))
        half_up = share_half(part_up, "blk", 2, 0)
        begun = half_up
        x_all = around(x_ranks)
        mine = jnp.concatenate([units_of(up_weight, side), out_weight], 1)
        half_up = both_shards(mine, half_up)
        w_up, w_out = half_up[:, :-width], half_up[:, -width:]
        x_mlp = jnp.concatenate([tokens, x_e[0]])
        e_mlp = jnp.concatenate([cotangent, x_e[1]])
        b_up, w_down, mlp, finish = up_bias, down_weight, mlp_pair, finish_pair
    else:
        x_all, begun = around(x_ranks), x_ranks
        w_qkv, w_up, w_out, w_down = (
            lax.all_gather(w, "fsdp", axis=0, tiled=True)
            for w in (qkv_weight, up_weight, out_weight, down_weight)
        )
        b_up = gather_small(up_bias).reshape(-1)
        x_mlp, e_mlp, mlp, finish = tokens, cotangent, mlp_gathered, lambda v, _: v
    small = gather_small(
        jnp.concatenate([ln1_gain, ln1_bias, ln2_gain, ln2_bias, out_bias, down_bias, qkv_bias])
    )
    part = width // shards
    ln1_g, ln1_b, ln2_g, ln2_b, b_out, b_down = (
        small[:, i * part : (i + 1) * part].reshape(width).astype(f32) for i in range(6)
    )
    b_qkv = small[:, 6 * part :].reshape(3 * width).astype(f32)
    starts = [i * width + group * cols for i in range(3)]
    w_mine = jnp.concatenate([lax.dynamic_slice_in_dim(w_qkv, v, cols, 1) for v in starts], 1)
    b_mine = jnp.concatenate([lax.dynamic_slice_in_dim(b_qkv, v, cols, 0) for v in starts])
    x_all = after(x_all, w_mine, begun)
    normed, queries, kv, cosine, sine = prepare(ln1_g, ln1_b, w_mine, b_mine, x_all, count)
    queries = queries.reshape(heads, HEAD, rows)
    pieces = {0: kv}
    step = lax.axis_size("blk") // 2
    while step >= 1:
        for i in list(pieces):
            pieces[i ^ step] = swap(pieces[i], "blk", step)
        step //= 2
    kv_all = [pieces[i] for i in range(len(pieces))]
    ranks = jnp.concatenate([v[2 * cols, : rows // STRETCH] for v in kv_all]).astype(jnp.int32)

    d_mixed = jnp.einsum("ed,td->et", w_out, cotangent, preferred_element_type=f32).astype(bf16)
    d_heads = [lax.dynamic_slice_in_dim(d_mixed, (group ^ j) * cols, cols) for j in range(groups)]
    d_heads = [d_heads[0]] + [swap(d_heads[j], "ulysses", j) for j in range(1, groups)]
    d_heads = jnp.concatenate(d_heads, 1).reshape(heads, HEAD, rows)

    x_mlp, w_up = after((x_mlp, w_up), kv, d_mixed)
    mlp_out, d_norm_two, begun, terms, g_up_bias = mlp(
        x_mlp, e_mlp, ln2_g, ln2_b, w_up, b_up, w_down, pieces[lax.axis_size("blk") // 2], d_heads
    )

    e_around = around(after(cotangent, begun))
    d_heads = after(d_heads, begun)
    mixed, d_q, kept, sent = attend(ranks, queries, d_heads, kv_all)

    sent, e_around = after((sent, e_around))
    total = kept.astype(f32) + swap(sent, "blk", 1).astype(f32)
    g_up, g_down = finish(terms, total)
    d_q = rotate(d_q, cosine, -sine).astype(bf16).reshape(cols, rows)
    back_q = to_tokens(after(d_q, total))
    step = 1
    while total.shape[0] > 1:
        step *= 2
        sent = swap(total[1::2].astype(bf16), "blk", step)
        total = total[0::2] + sent.astype(f32)
    mixed = mixed.reshape(cols, rows)
    e_all = jnp.concatenate(e_around, 0)
    g_out = jnp.dot(mixed, e_all, preferred_element_type=f32).astype(bf16)
    d_k = rotate(total[0, :cols].reshape(heads, HEAD, rows), cosine, -sine).reshape(cols, rows)
    d_kv = jnp.concatenate([d_k, total[0, cols:]]).astype(bf16)
    d_joined = jnp.concatenate([d_q, d_kv])
    g_bias_mine = jnp.sum(d_joined.astype(f32), 1)
    g_qkv = jnp.dot(d_joined, normed, preferred_element_type=f32).astype(bf16)
    back_kv = to_tokens(d_kv)
    grads = jnp.concatenate([g_qkv.reshape(3, cols, width), g_out[None]])
    g_qkv, g_out, begun = attention_grads(grads)
    back_q, back_kv = after((back_q, back_kv), begun)
    back_q, back_kv = by_device(back_q, group), by_device(back_kv, group)
    d_mine = jnp.concatenate(
        back_q + [v[:cols] for v in back_kv] + [v[cols:] for v in back_kv], 0
    )
    d_norm_one = jnp.einsum("et,de->td", d_mine, w_qkv, preferred_element_type=f32)
    x_float = tokens.astype(f32)
    _, pull_one = jax.vjp(layer_norm, x_float, ln1_g, ln1_b)
    _, pull_two = jax.vjp(layer_norm, x_float, ln2_g, ln2_b)
    d_x_one, g_ln1_g, g_ln1_b = pull_one(d_norm_one)
    d_x_two, g_ln2_g, g_ln2_b = pull_two(d_norm_two)
    e_float = cotangent.astype(f32)

    back = by_device(to_tokens(after(mixed, back_kv)), group)
    attn_out = jnp.einsum("et,ed->td", jnp.concatenate(back, 0), w_out, preferred_element_type=f32)
    output = (x_float + (attn_out + b_out) + (mlp_out + b_down)).astype(bf16)
    input_grad = (e_float + d_x_one + d_x_two).astype(bf16)

    g_qkv_bias = jnp.zeros((3, groups, cols), f32)
    g_qkv_bias = lax.dynamic_update_slice(g_qkv_bias, g_bias_mine.reshape(3, 1, cols), (0, group, 0))
    vectors = [g_ln1_g, g_ln1_b, g_ln2_g, g_ln2_b, jnp.sum(e_float, 0), g_qkv_bias.reshape(-1), g_up_bias]
    summed = sum_everywhere(jnp.concatenate(vectors))
    results, start = [], 0
    for vector in vectors:
        mine = vector.shape[0] // shards
        results.append(lax.dynamic_slice_in_dim(summed, start + lax.axis_index("fsdp") * mine, mine))
        start += vector.shape[0]
    g_ln1_g, g_ln1_b, g_ln2_g, g_ln2_b, g_e, g_qkv_bias, g_up_bias = results
    return (
        output,
        input_grad,
        g_ln1_g,
        g_ln1_b,
        g_ln2_g,
        g_ln2_b,
        g_qkv,
        g_qkv_bias,
        g_out,
        g_e,
        g_up,
        g_up_bias,
        g_down,
        g_e,
    )


def solution(mesh):
    rows = P(("fsdp", "blk", "ulysses"), None)
    split, matrix = P("fsdp"), P("fsdp", None)
    return jax.shard_map(
        on_device,
        mesh=mesh,
        in_specs=(
            rows,
            P(("fsdp", "blk", "ulysses")),
            rows,
            split,
            split,
            split,
            split,
            matrix,
            split,
            matrix,
            split,
            matrix,
            split,
            matrix,
            split,
        ),
        out_specs=(
            rows,
            rows,
            split,
            split,
            split,
            split,
            matrix,
            split,
            matrix,
            split,
            matrix,
            split,
            matrix,
            split,
        ),
        check_vma=False,
    )
```

```python
import jax
import jax.numpy as jnp
import numpy as np
from jax import lax
from jax.experimental import pallas as pl
from jax.experimental.pallas import tpu as pltpu
from jax.sharding import PartitionSpec as P

HEAD = 64
ROT = 16
STRETCH = 128
CHUNK = 8
BIG_NEG = -1e30

f32 = jnp.float32
bf16 = jnp.bfloat16


def layer_norm(values, gain, shift):
    center = jnp.mean(values, -1, keepdims=True)
    offset = values - center
    spread = jnp.mean(offset * offset, -1, keepdims=True)
    return offset * lax.rsqrt(spread + 1e-05) * gain + shift


def gelu_exact(values):
    return jax.nn.gelu(values, approximate=False)


def swap(values, axis, bits):
    count = lax.axis_size(axis)
    return lax.ppermute(values, axis, [(i, i ^ bits) for i in range(count)])


def after(values, *earlier):
    return lax.optimization_barrier((values, earlier))[0]


def bit_of(axis, bit):
    return (lax.axis_index(axis) // bit) % 2


def in_order(bit, mine, other, axis=0):
    return jnp.concatenate([jnp.where(bit == 0, mine, other), jnp.where(bit == 0, other, mine)], axis)


def by_device(pieces, index):
    step = 1
    while step < len(pieces):
        odd = (index // step) % 2 == 1
        pieces = [jnp.where(odd, pieces[i ^ step], pieces[i]) for i in range(len(pieces))]
        step *= 2
    return pieces


def add_half(halves, axis, bit):
    which = bit_of(axis, bit)
    got = swap(jnp.where(which == 0, halves[1], halves[0]), axis, bit)
    kept = jnp.where(which == 0, halves[0], halves[1])
    return (kept.astype(f32) + got.astype(f32)).astype(bf16)


def halves_of(values, axis):
    half = values.shape[axis] // 2
    return (
        lax.slice_in_dim(values, 0, half, axis=axis),
        lax.slice_in_dim(values, half, 2 * half, axis=axis),
    )


def share_half(values, axis, bit, dim):
    return in_order(bit_of(axis, bit), values, swap(values, axis, bit), dim)


def gather_small(shard):
    if lax.axis_size("fsdp") != 2:
        return lax.all_gather(shard[None], "fsdp", axis=0, tiled=True)
    return in_order(lax.axis_index("fsdp"), shard[None], swap(shard[None], "fsdp", 1))


def quarter_of(shard):
    quarter = shard.shape[0] // 4
    place = bit_of("blk", 1) * 2 + bit_of("blk", 2)
    return lax.dynamic_slice_in_dim(shard, place * quarter, quarter)


def both_shards(shard, half):
    return in_order(lax.axis_index("fsdp"), shard, share_half(half, "blk", 1, 0))


def attend_kernel(rank, q_ref, g_ref, *refs):
    kv_refs = refs[:-9]
    o_ref, dq_ref, keep_ref, send_ref, rows, lanes, sums, probs, order = refs[-9:]
    heads = range(q_ref.shape[0])
    cols = q_ref.shape[0] * HEAD
    n_keys = rank.shape[0]
    own = q_ref.shape[-1] // STRETCH
    wide = 2 * STRETCH
    span = CHUNK * STRETCH

    for t in range(n_keys):
        i, at = t // own, (t % own) * STRETCH
        place = rank[t]
        for h in heads:
            both = jnp.concatenate(
                [
                    kv_refs[i][first : first + HEAD, at : at + STRETCH]
                    for first in (h * HEAD, cols + h * HEAD)
                ],
                0,
            )
            lanes[h, place] = both
            rows[h, place] = both.T
            sums[h, t] = jnp.zeros((STRETCH, 2 * HEAD), f32)
    for a in range(own):
        before = jnp.int32(0)
        for b in range(own):
            before += (rank[b] < rank[a]).astype(jnp.int32)
        order[before] = a

    def side(h, j, part):
        first = part * HEAD
        return jnp.concatenate(
            [lanes[h, j * CHUNK + i, first : first + HEAD, :] for i in range(CHUNK)], 1
        )

    def keys(h, j):
        return rows[h, pl.ds(j * CHUNK, CHUNK)].reshape(span, 2 * HEAD)

    def pair(p, carry):
        a, b = order[2 * p], order[2 * p + 1]
        ra, rb = rank[a], rank[b]
        at_a = pl.ds(pl.multiple_of(a * STRETCH, STRETCH), STRETCH)
        at_b = pl.ds(pl.multiple_of(b * STRETCH, STRETCH), STRETCH)
        q = [jnp.concatenate([q_ref[h, :, at_a], q_ref[h, :, at_b]], 1) for h in heads]
        g = [jnp.concatenate([g_ref[h, :, at_a], g_ref[h, :, at_b]], 1) for h in heads]
        none = jnp.zeros_like(q[0])
        q_low = [jnp.concatenate([v, none], 0) for v in q]
        g_high = [jnp.concatenate([none, v], 0) for v in g]
        lane = lax.broadcasted_iota(jnp.int32, (1, wide), 1)
        q_place = jnp.where(lane < STRETCH, ra * STRETCH + lane, rb * STRETCH + lane - STRETCH)
        clear = ra // CHUNK
        total = (rb + CHUNK) // CHUNK

        def score(j, tops, masked):
            result = []
            for h in heads:
                s = jnp.dot(keys(h, j), q_low[h], preferred_element_type=f32)
                if masked:
                    k_place = j * span + lax.broadcasted_iota(jnp.int32, (span, 1), 0)
                    s = jnp.where(k_place <= q_place, s, BIG_NEG)
                probs[h, j] = s
                result.append(jnp.maximum(tops[h], jnp.max(s.reshape(span // 8, 8, wide), 0)))
            return tuple(result)

        tops = tuple(jnp.full((8, wide), BIG_NEG, f32) for _ in heads)
        tops = lax.fori_loop(0, clear, lambda j, v: score(j, v, False), tops)
        tops = lax.fori_loop(clear, total, lambda j, v: score(j, v, True), tops)
        tops = [jnp.max(v, 0, keepdims=True) for v in tops]

        def weigh(j, state):
            result = []
            for h in heads:
                count, out = state[h]
                weight = jnp.exp(probs[h, j] - tops[h])
                probs[h, j] = weight
                count = count + jnp.sum(weight.reshape(span // 8, 8, wide), 0)
                out = out + jnp.dot(side(h, j, 1), weight.astype(bf16), preferred_element_type=f32)
                result.append((count, out))
            return tuple(result)

        state = tuple((jnp.zeros((8, wide), f32), jnp.zeros((HEAD, wide), f32)) for _ in heads)
        state = lax.fori_loop(0, total, weigh, state)
        inverse, delta, right = [], [], []
        for h in heads:
            count, out = state[h]
            inverse.append(1.0 / jnp.sum(count, 0, keepdims=True))
            out = out * inverse[h]
            delta.append(jnp.sum(out * g[h].astype(f32), 0, keepdims=True))
            o_ref[h, :, at_a] = out[:, :STRETCH].astype(bf16)
            o_ref[h, :, at_b] = out[:, STRETCH:].astype(bf16)
            top = jnp.concatenate([g[h], none], 0).T
            right.append(jnp.concatenate([top, jnp.concatenate([none, q[h]], 0).T], 0))

        def back(j, d_q):
            result = []
            for h in heads:
                weight = probs[h, j] * inverse[h]
                d_weight = jnp.dot(keys(h, j), g_high[h], preferred_element_type=f32)
                d_score = (weight * (d_weight - delta[h])).astype(bf16)
                left = jnp.concatenate([weight.astype(bf16), d_score], 1)
                sums[h, pl.ds(j * CHUNK, CHUNK)] += jnp.dot(
                    left, right[h], preferred_element_type=f32
                ).reshape(CHUNK, STRETCH, 2 * HEAD)
                result.append(d_q[h] + jnp.dot(side(h, j, 0), d_score, preferred_element_type=f32))
            return tuple(result)

        d_q = lax.fori_loop(0, total, back, tuple(jnp.zeros((HEAD, wide), f32) for _ in heads))
        for h in heads:
            scaled = d_q[h] * HEAD ** (-0.5)
            dq_ref[h, :, at_a] = scaled[:, :STRETCH]
            dq_ref[h, :, at_b] = scaled[:, STRETCH:]
        return carry

    lax.fori_loop(0, own // 2, pair, 0)
    for t in range(n_keys):
        i, at = t // own, (t % own) * STRETCH
        to = keep_ref if i % 2 == 0 else send_ref
        for h in heads:
            turned = sums[h, rank[t]].T.astype(bf16)
            first = h * HEAD
            to[i // 2, cols + first : cols + first + HEAD, at : at + STRETCH] = turned[:HEAD]
            to[i // 2, first : first + HEAD, at : at + STRETCH] = turned[HEAD:]


def attend(ranks, q, g, kv):
    heads, _, count = q.shape
    devices = len(kv)
    n_keys = devices * count // STRETCH
    pairs = heads * 4 * HEAD * count * count * devices
    half = (devices // 2, 2 * heads * HEAD, count)
    q_spec = pl.BlockSpec(q.shape, lambda i, *_: (0, 0, 0))
    half_spec = pl.BlockSpec(half, lambda i, *_: (0, 0, 0))
    return pl.pallas_call(
        attend_kernel,
        grid_spec=pltpu.PrefetchScalarGridSpec(
            num_scalar_prefetch=1,
            grid=(1,),
            in_specs=[q_spec, q_spec] + [pl.BlockSpec(v.shape, lambda i, *_: (0, 0)) for v in kv],
            out_specs=[q_spec, q_spec, half_spec, half_spec],
            scratch_shapes=[
                pltpu.VMEM((heads, n_keys, STRETCH, 2 * HEAD), bf16),
                pltpu.VMEM((heads, n_keys, 2 * HEAD, STRETCH), bf16),
                pltpu.VMEM((heads, n_keys, STRETCH, 2 * HEAD), f32),
                pltpu.VMEM((heads, n_keys // CHUNK, CHUNK * STRETCH, 2 * STRETCH), f32),
                pltpu.SMEM((count // STRETCH,), jnp.int32),
            ],
        ),
        out_shape=[
            jax.ShapeDtypeStruct(q.shape, bf16),
            jax.ShapeDtypeStruct(q.shape, f32),
            jax.ShapeDtypeStruct(half, bf16),
            jax.ShapeDtypeStruct(half, bf16),
        ],
        compiler_params=pltpu.CompilerParams(vmem_limit_bytes=56 * 2**20),
        cost_estimate=pl.CostEstimate(
            flops=12 * pairs, bytes_accessed=16 * q.size * devices, transcendentals=pairs // 512
        ),
        name="attend",
    )(ranks, q, g, *kv)


def prepare_kernel(freqs, gain, shift, weight, bias, *refs):
    groups = len(refs) - 5
    x_refs = refs[:groups]
    normed_ref, q_ref, kv_ref, cos_ref, sin_ref = refs[groups:]
    count = normed_ref.shape[0] // groups
    cols = q_ref.shape[0]
    halfway = ROT // 2
    blocks = count // STRETCH
    lane = lax.broadcasted_iota(jnp.int32, (1, STRETCH), 1).astype(f32)
    kv_ref[2 * cols :, :] = jnp.zeros((kv_ref.shape[0] - 2 * cols, kv_ref.shape[1]), bf16)
    spots = lax.broadcasted_iota(jnp.int32, (1, STRETCH), 1)
    table = jnp.zeros((1, STRETCH), f32)
    for i, x_ref in enumerate(x_refs):
        at = i * count
        normed = layer_norm(x_ref[:count].astype(f32), gain[...], shift[...]).astype(bf16)
        normed_ref[at : at + count] = normed
        joined = jnp.dot(normed, weight[...], preferred_element_type=f32) + bias[...]
        joined = joined.T
        ranks = x_ref[count : count + 16, :STRETCH].astype(f32)[:1]
        places = []
        for b in range(blocks):
            rank = jnp.sum(jnp.where(spots == b, ranks, 0.0), 1, keepdims=True)
            places.append(rank * STRETCH + lane)
            table = jnp.where(spots == i * blocks + b, rank, table)
        angles = freqs[...] * jnp.concatenate(places, 1)
        cosine, sine = jnp.cos(angles), jnp.sin(angles)
        cos_ref[:, at : at + count] = cosine
        sin_ref[:, at : at + count] = sine
        for to, first, scale in ((q_ref, 0, HEAD ** (-0.5)), (kv_ref, cols, 1.0)):
            for h in range(cols // HEAD):
                low = first + h * HEAD
                one = joined[low : low + halfway]
                two = joined[low + halfway : low + ROT]
                rest = joined[low + ROT : low + HEAD]
                turned = jnp.concatenate(
                    [one * cosine - two * sine, two * cosine + one * sine, rest], 0
                ).astype(bf16)
                to[h * HEAD : (h + 1) * HEAD, at : at + count] = turned * jnp.bfloat16(scale)
        kv_ref[cols : 2 * cols, at : at + count] = joined[2 * cols :].astype(bf16)
    kv_ref[2 * cols :, :STRETCH] = jnp.broadcast_to(table, (16, STRETCH)).astype(bf16)


def prepare(gain, shift, weight, bias, x_all, count):
    width = weight.shape[0]
    cols = weight.shape[1] // 3
    rows = count * len(x_all)
    halfway = ROT // 2
    freqs = jnp.asarray(10000.0 ** (-np.arange(halfway) * 2.0 / ROT), f32)[:, None]
    return pl.pallas_call(
        prepare_kernel,
        out_shape=[
            jax.ShapeDtypeStruct((rows, width), bf16),
            jax.ShapeDtypeStruct((cols, rows), bf16),
            jax.ShapeDtypeStruct((2 * cols + 16, rows), bf16),
            jax.ShapeDtypeStruct((ROT // 2, rows), f32),
            jax.ShapeDtypeStruct((ROT // 2, rows), f32),
        ],
        compiler_params=pltpu.CompilerParams(vmem_limit_bytes=40 * 2**20),
        cost_estimate=pl.CostEstimate(
            flops=6 * cols * rows * width, bytes_accessed=8 * rows * width, transcendentals=0
        ),
        name="prepare",
    )(freqs, gain[None], shift[None], weight, bias[None], *x_all)


def rotate(heads, cosine, sine):
    halfway = ROT // 2
    first = heads[:, :halfway]
    second = heads[:, halfway:ROT]
    return jnp.concatenate(
        [first * cosine - second * sine, second * cosine + first * sine, heads[:, ROT:]], 1
    )


def around(values):
    return [values] + [swap(values, "ulysses", j) for j in range(1, lax.axis_size("ulysses"))]


def to_tokens(values):
    groups = lax.axis_size("ulysses")
    count = values.shape[1] // groups
    pieces = [values[:, j * count : (j + 1) * count] for j in range(groups)]
    return [pieces[0]] + [swap(pieces[j], "ulysses", j) for j in range(1, groups)]


def units_of(up_weight, side):
    units = up_weight.shape[1] // 2
    return jnp.where(side == 0, up_weight[:, :units], up_weight[:, units:])


def mlp_pair(x_both, e_both, gain, shift, up, up_bias, down_weight, *meanwhile):
    side = lax.axis_index("fsdp")
    rows, width = x_both.shape[0] // 2, x_both.shape[1]
    units = up.shape[1]
    normed = layer_norm(x_both.astype(f32), gain, shift).astype(bf16)
    hidden = jnp.dot(normed, up, preferred_element_type=f32) + up_bias.astype(f32)
    active_f, pull_gelu = jax.vjp(gelu_exact, hidden)
    active = active_f.astype(bf16)
    part = jnp.dot(active, down_weight, preferred_element_type=f32)
    out = part[:rows] + swap(part[rows:].astype(bf16), "fsdp", 1).astype(f32)
    d_active = jnp.einsum("td,fd->tf", e_both, down_weight, preferred_element_type=f32)
    d_hidden = pull_gelu(d_active)[0].astype(bf16)
    g_up_bias = jnp.sum(d_hidden.astype(f32), 0)
    d_part = jnp.einsum("tf,df->td", d_hidden, up, preferred_element_type=f32)
    d_normed = d_part[:rows] + swap(d_part[rows:].astype(bf16), "fsdp", 1).astype(f32)
    active, d_hidden = after((active, d_hidden), *meanwhile)
    g_up = jnp.einsum(
        "td,tcf->cdf", normed, d_hidden.reshape(2 * rows, 2, units // 2), preferred_element_type=f32
    ).astype(bf16)
    g_down = jnp.einsum("tf,td->fd", active, e_both, preferred_element_type=f32).astype(bf16)
    g_down = g_down.reshape(2, units // 2, width)
    pieces = jnp.stack([g_up, g_down], 1).reshape(2, 2, 2, width // 2, width)
    first = add_half((pieces[0], pieces[1]), "blk", 1)
    sums = add_half(halves_of(first, 2), "blk", 2)
    side, none = lax.axis_index("fsdp"), jnp.zeros_like(g_up_bias)
    g_up_bias = jnp.concatenate([jnp.where(side == 0, g_up_bias, none), jnp.where(side == 0, none, g_up_bias)])
    return out, d_normed, first, sums, g_up_bias


def finish_pair(sums, earlier):
    side = lax.axis_index("fsdp")
    sums = after(sums, earlier)
    sums = add_half(halves_of(sums, 2), "ulysses", 1)
    sums = add_half(halves_of(sums, 2), "ulysses", 2)
    got = swap(jnp.where(side == 0, sums[0, 1], sums[0, 0]), "fsdp", 1)
    kept = jnp.where(side == 0, sums[0, 0], sums[0, 1])
    sums = jnp.concatenate([in_order(side, kept[None], got[None]), sums[1]], 0)
    sums = share_half(sums, "ulysses", 2, 1)
    sums = share_half(sums, "ulysses", 1, 1)
    sums = share_half(sums, "blk", 2, 1)
    return place_mlp(bit_of("blk", 1), sums, swap(sums, "blk", 1))


def place_mlp_kernel(which, mine, other, up_ref, down_ref):
    width = mine.shape[-1]
    for c, ref in ((which[0], mine), (1 - which[0], other)):
        for f in range(2):
            at = pl.multiple_of((2 * f + c) * width, STRETCH)
            up_ref[:, pl.ds(at, width)] = ref[f].astype(f32)
            down_ref[c, f] = ref[2 + f].astype(f32)


def place_mlp(which, mine, other):
    _, rows, width = mine.shape
    step = rows // 4
    whole = pl.BlockSpec((4, step, width), lambda i, *_: (0, i, 0))
    up, down = pl.pallas_call(
        place_mlp_kernel,
        grid_spec=pltpu.PrefetchScalarGridSpec(
            num_scalar_prefetch=1,
            grid=(4,),
            in_specs=[whole, whole],
            out_specs=[
                pl.BlockSpec((step, 4 * width), lambda i, *_: (i, 0)),
                pl.BlockSpec((2, 2, step, width), lambda i, *_: (0, 0, i, 0)),
            ],
        ),
        out_shape=[
            jax.ShapeDtypeStruct((rows, 4 * width), f32),
            jax.ShapeDtypeStruct((2, 2, rows, width), f32),
        ],
        compiler_params=pltpu.CompilerParams(vmem_limit_bytes=32 * 2**20),
        cost_estimate=pl.CostEstimate(flops=0, bytes_accessed=12 * mine.size, transcendentals=0),
        name="place_mlp",
    )(which[None], mine, other)
    return up, down.reshape(4 * rows, width)


def place_qkv_kernel(which, mine, other, qkv_ref, out_ref):
    first = which[0] == 0
    rows, half = mine.shape[1:]
    width = 2 * half
    groups = mine.shape[0] // 4
    for t in range(3):
        blocks = []
        for z in range(groups):
            a, b = mine[3 * z + t], other[3 * z + t]
            blocks += [jnp.where(first, a, b), jnp.where(first, b, a)]
        qkv_ref[:, t * width : (t + 1) * width] = jnp.concatenate(blocks, 0).astype(f32).T
    for z in range(groups // 2):
        for side in range(2):
            a, b = mine[3 * groups + 2 * z + side], other[3 * groups + 2 * z + side]
            at = 2 * z * rows
            both = jnp.concatenate([jnp.where(first, a, b), jnp.where(first, b, a)], 0)
            out_ref[at : at + 2 * rows, side * half : (side + 1) * half] = both.astype(f32)


def place_qkv(which, mine, other):
    _, rows, half = mine.shape
    groups = mine.shape[0] // 4
    return pl.pallas_call(
        place_qkv_kernel,
        grid_spec=pltpu.PrefetchScalarGridSpec(
            num_scalar_prefetch=1,
            grid=(1,),
            in_specs=[pl.BlockSpec(v.shape, lambda i, *_: (0, 0, 0)) for v in (mine, other)],
            out_specs=[
                pl.BlockSpec((half, 6 * half), lambda i, *_: (0, 0)),
                pl.BlockSpec((groups * rows, 2 * half), lambda i, *_: (0, 0)),
            ],
        ),
        out_shape=[
            jax.ShapeDtypeStruct((half, 6 * half), f32),
            jax.ShapeDtypeStruct((groups * rows, 2 * half), f32),
        ],
        compiler_params=pltpu.CompilerParams(vmem_limit_bytes=40 * 2**20),
        cost_estimate=pl.CostEstimate(flops=0, bytes_accessed=12 * mine.size, transcendentals=0),
        name="place_qkv",
    )(which[None], mine, other)


def mlp_gathered(x, e, gain, shift, up, bias, down, *meanwhile):
    normed = layer_norm(x.astype(f32), gain, shift).astype(bf16)
    hidden = jnp.dot(normed, up, preferred_element_type=f32) + bias.astype(f32)
    active_f, pull_gelu = jax.vjp(gelu_exact, hidden)
    active = active_f.astype(bf16)
    out = jnp.dot(active, down, preferred_element_type=f32)
    g_down = jnp.einsum("tf,td->fd", active, e, preferred_element_type=f32)
    d_active = jnp.einsum("td,fd->tf", e, down, preferred_element_type=f32)
    d_hidden = pull_gelu(d_active)[0].astype(bf16)
    g_up = jnp.einsum("td,tf->df", normed, d_hidden, preferred_element_type=f32)
    d_normed = jnp.einsum("tf,df->td", d_hidden, up, preferred_element_type=f32)
    g_up, g_down = (
        lax.psum(
            lax.psum_scatter(g.astype(bf16), "fsdp", scatter_dimension=0, tiled=True),
            ("blk", "ulysses"),
        ).astype(f32)
        for g in (g_up, g_down)
    )
    return out, d_normed, d_hidden, (g_up, g_down), jnp.sum(d_hidden.astype(f32), 0)


def add_blks(grads):
    if lax.axis_size("fsdp") != 2:
        return lax.psum(grads, "blk")
    return add_half(halves_of(add_half(halves_of(grads, 1), "blk", 1), 1), "blk", 2)


def attention_grads(grads, vector):
    side = lax.axis_index("fsdp")
    group = lax.axis_index("ulysses")
    groups = lax.axis_size("ulysses")
    _, rows, width = grads.shape
    if lax.axis_size("fsdp") != 2:
        total = lax.all_gather(lax.psum(grads, "fsdp"), "ulysses", axis=1, tiled=True)
        part = width // lax.axis_size("fsdp")
        g_qkv = lax.dynamic_slice_in_dim(total[:3], side * part, part, 2)
        g_out = lax.dynamic_slice_in_dim(total[3], side * part, part, 0)
        g_qkv = g_qkv.reshape(3 * width, part).T.astype(f32)
        return g_qkv, g_out.astype(f32), sum_everywhere(vector)
    half = width // 2
    size = vector.shape[0]
    small = jnp.pad(vector.astype(bf16), (0, rows * half - size)).reshape(1, rows, half)
    low, high = grads[:, :, :half], grads[:, :, half:]
    kept = jnp.where(side == 0, low[:3], high[:3])
    sent = jnp.where(side == 0, high[:3], low[:3])
    whole = jnp.stack([low[3], high[3]])
    kept = jnp.concatenate([kept, whole, small])
    got = swap(jnp.concatenate([sent, whole, small]), "fsdp", 1)
    kept = (kept.astype(f32) + got.astype(f32)).astype(bf16)
    kept = by_device(around(kept), group)
    small = sum(v[5:].astype(f32) for v in kept).astype(bf16)
    of_qkv = jnp.concatenate([v[:3] for v in kept])
    of_out = [jnp.where(side == 0, a[3:5], b[3:5]) for a, b in zip(kept[: groups // 2], kept[groups // 2 :])]
    kept = jnp.concatenate([of_qkv] + of_out)
    units = kept.shape[0]
    got = swap(jnp.concatenate([kept, small]), "blk", 2)
    kept = in_order(bit_of("blk", 2), kept, got[:units], 1)
    small = (small.astype(f32) + got[units:].astype(f32)).astype(bf16)
    wide = jnp.pad(small, ((0, 0), (0, rows), (0, 0)))
    got = swap(jnp.concatenate([kept, wide]), "blk", 1)
    small = small.astype(f32) + got[units:, :rows].astype(f32)
    g_qkv, g_out = place_qkv(bit_of("blk", 1), kept, got)
    return g_qkv, g_out, small.reshape(-1)[:size]


def sum_everywhere(values):
    for axis in ("blk", "ulysses", "fsdp"):
        step = 1
        while step < lax.axis_size(axis):
            values = values + swap(values, axis, step)
            step *= 2
    return values


def on_device(
    tokens,
    positions,
    cotangent,
    ln1_gain,
    ln1_bias,
    ln2_gain,
    ln2_bias,
    qkv_weight,
    qkv_bias,
    out_weight,
    out_bias,
    up_weight,
    up_bias,
    down_weight,
    down_bias,
):
    count, width = tokens.shape
    groups = lax.axis_size("ulysses")
    group = lax.axis_index("ulysses")
    shards = lax.axis_size("fsdp")
    cols = width // groups
    heads = cols // HEAD
    rows = count * groups

    ranks = (positions[::STRETCH] // STRETCH).astype(bf16)[None]
    ranks = jnp.pad(ranks, ((0, 15), (0, width - ranks.shape[1])))
    x_ranks = jnp.concatenate([tokens, ranks])
    if shards == 2:
        side = lax.axis_index("fsdp")
        part_qkv = swap(quarter_of(qkv_weight), "fsdp", 1)
        half_up = jnp.concatenate([units_of(up_weight, 1 - side), out_weight], 1)
        part_up = swap(after(quarter_of(half_up), part_qkv), "fsdp", 1)
        x_e = swap(after(jnp.stack([tokens, cotangent]), part_up), "fsdp", 1)
        w_qkv = both_shards(qkv_weight, share_half(part_qkv, "blk", 2, 0))
        half_up = share_half(part_up, "blk", 2, 0)
        x_all = around(x_ranks)
        mine = jnp.concatenate([units_of(up_weight, side), out_weight], 1)
        half_up = both_shards(mine, half_up)
        w_up, w_out = half_up[:, :-width], half_up[:, -width:]
        x_mlp = jnp.concatenate([tokens, x_e[0]])
        e_mlp = jnp.concatenate([cotangent, x_e[1]])
        b_up, w_down, mlp, finish = up_bias, down_weight, mlp_pair, finish_pair
    else:
        x_all, part_qkv = around(x_ranks), x_ranks
        w_qkv, w_up, w_out, w_down = (
            lax.all_gather(w, "fsdp", axis=0, tiled=True)
            for w in (qkv_weight, up_weight, out_weight, down_weight)
        )
        b_up = gather_small(up_bias).reshape(-1)
        x_mlp, e_mlp, mlp, finish = tokens, cotangent, mlp_gathered, lambda v, _: v
    small = jnp.concatenate([ln1_gain, ln1_bias, ln2_gain, ln2_bias, out_bias, down_bias, qkv_bias])
    small = gather_small(after(small, part_qkv))
    part = width // shards
    ln1_g, ln1_b, ln2_g, ln2_b, b_out, b_down = (
        small[:, i * part : (i + 1) * part].reshape(width).astype(f32) for i in range(6)
    )
    b_qkv = small[:, 6 * part :].reshape(3 * width).astype(f32)
    starts = [i * width + group * cols for i in range(3)]
    w_mine = jnp.concatenate([lax.dynamic_slice_in_dim(w_qkv, v, cols, 1) for v in starts], 1)
    b_mine = jnp.concatenate([lax.dynamic_slice_in_dim(b_qkv, v, cols, 0) for v in starts])
    x_all = after(x_all, w_mine)
    normed, queries, kv, cosine, sine = prepare(ln1_g, ln1_b, w_mine, b_mine, x_all, count)
    queries = queries.reshape(heads, HEAD, rows)
    pieces = {0: kv}
    step = lax.axis_size("blk") // 2
    while step >= 1:
        for i in list(pieces):
            pieces[i ^ step] = swap(pieces[i], "blk", step)
        step //= 2
    kv_all = [pieces[i] for i in range(len(pieces))]
    ranks = jnp.concatenate([v[2 * cols, : rows // STRETCH] for v in kv_all]).astype(jnp.int32)

    d_mixed = jnp.einsum("ed,td->et", w_out, after(cotangent, kv), preferred_element_type=f32).astype(bf16)
    d_heads = [lax.dynamic_slice_in_dim(d_mixed, (group ^ j) * cols, cols) for j in range(groups)]
    d_heads = [d_heads[0]] + [swap(d_heads[j], "ulysses", j) for j in range(1, groups)]
    d_heads = jnp.concatenate(d_heads, 1).reshape(heads, HEAD, rows)

    x_mlp, w_up = after((x_mlp, w_up), kv, d_mixed)
    mlp_out, d_norm_two, begun, terms, g_up_bias = mlp(
        x_mlp, e_mlp, ln2_g, ln2_b, w_up, b_up, w_down, pieces[lax.axis_size("blk") // 2], pieces[1], d_heads
    )

    e_around = around(after(cotangent, begun))
    d_heads = after(d_heads, begun)
    mixed, d_q, kept, sent = attend(ranks, queries, d_heads, kv_all)

    sent, e_around, terms, mlp_out, d_norm_two = after((sent, e_around, terms, mlp_out, d_norm_two))
    total = kept.astype(f32) + swap(sent, "blk", 1).astype(f32)
    g_up, g_down = finish(terms, total)
    d_q = rotate(d_q, cosine, -sine).astype(bf16).reshape(cols, rows)
    mixed = mixed.reshape(cols, rows)
    back_q = to_tokens(after(jnp.concatenate([d_q, mixed]), total))
    step = 1
    while total.shape[0] > 1:
        step *= 2
        sent = swap(total[1::2].astype(bf16), "blk", step)
        total = total[0::2] + sent.astype(f32)
    e_all = jnp.concatenate(e_around, 0)
    g_out = jnp.dot(mixed, e_all, preferred_element_type=f32).astype(bf16)
    d_k = rotate(total[0, :cols].reshape(heads, HEAD, rows), cosine, -sine).reshape(cols, rows)
    d_kv = jnp.concatenate([d_k, total[0, cols:]]).astype(bf16)
    d_joined = jnp.concatenate([d_q, d_kv])
    g_bias_mine = jnp.sum(d_joined.astype(f32), 1)
    g_qkv = jnp.dot(d_joined, normed, preferred_element_type=f32).astype(bf16)
    back_kv = to_tokens(d_kv)
    grads = jnp.concatenate([g_qkv.reshape(3, cols, width), g_out[None]])
    grads = add_blks(grads)
    back_q, back_kv = by_device(back_q, group), by_device(back_kv, group)
    d_mine = jnp.concatenate(
        [v[:cols] for v in back_q] + [v[:cols] for v in back_kv] + [v[cols:] for v in back_kv], 0
    )
    d_norm_one = jnp.einsum("et,de->td", d_mine, w_qkv, preferred_element_type=f32)
    x_float = tokens.astype(f32)
    _, pull_one = jax.vjp(layer_norm, x_float, ln1_g, ln1_b)
    _, pull_two = jax.vjp(layer_norm, x_float, ln2_g, ln2_b)
    d_x_one, g_ln1_g, g_ln1_b = pull_one(d_norm_one)
    d_x_two, g_ln2_g, g_ln2_b = pull_two(d_norm_two)
    e_float = cotangent.astype(f32)

    back = jnp.concatenate([v[cols:] for v in back_q], 0)
    attn_out = jnp.einsum("et,ed->td", back, w_out, preferred_element_type=f32)
    output = (x_float + (attn_out + b_out) + (mlp_out + b_down)).astype(bf16)
    input_grad = (e_float + d_x_one + d_x_two).astype(bf16)

    g_qkv_bias = jnp.zeros((3, groups, cols), f32)
    g_qkv_bias = lax.dynamic_update_slice(g_qkv_bias, g_bias_mine.reshape(3, 1, cols), (0, group, 0))
    vectors = [g_ln1_g, g_ln1_b, g_ln2_g, g_ln2_b, jnp.sum(e_float, 0), g_qkv_bias.reshape(-1), g_up_bias]
    g_qkv, g_out, summed = attention_grads(grads, jnp.concatenate(vectors))
    results, start = [], 0
    for vector in vectors:
        mine = vector.shape[0] // shards
        results.append(lax.dynamic_slice_in_dim(summed, start + lax.axis_index("fsdp") * mine, mine))
        start += vector.shape[0]
    g_ln1_g, g_ln1_b, g_ln2_g, g_ln2_b, g_e, g_qkv_bias, g_up_bias = results
    return (
        output,
        input_grad,
        g_ln1_g,
        g_ln1_b,
        g_ln2_g,
        g_ln2_b,
        g_qkv,
        g_qkv_bias,
        g_out,
        g_e,
        g_up,
        g_up_bias,
        g_down,
        g_e,
    )


def solution(mesh):
    rows = P(("fsdp", "blk", "ulysses"), None)
    split, matrix = P("fsdp"), P("fsdp", None)
    return jax.shard_map(
        on_device,
        mesh=mesh,
        in_specs=(
            rows,
            P(("fsdp", "blk", "ulysses")),
            rows,
            split,
            split,
            split,
            split,
            matrix,
            split,
            matrix,
            split,
            matrix,
            split,
            matrix,
            split,
        ),
        out_specs=(
            rows,
            rows,
            split,
            split,
            split,
            split,
            matrix,
            split,
            matrix,
            split,
            matrix,
            split,
            matrix,
            split,
        ),
        check_vma=False,
    )
```

```python
import jax
import jax.numpy as jnp
import numpy as np
from jax import lax
from jax.experimental import pallas as pl
from jax.experimental.pallas import tpu as pltpu
from jax.sharding import PartitionSpec as P

HEAD = 64
ROT = 16
STRETCH = 128
CHUNK = 8
BIG_NEG = -1e30

f32 = jnp.float32
bf16 = jnp.bfloat16


def layer_norm(values, gain, shift):
    center = jnp.mean(values, -1, keepdims=True)
    offset = values - center
    spread = jnp.mean(offset * offset, -1, keepdims=True)
    return offset * lax.rsqrt(spread + 1e-05) * gain + shift


def gelu_exact(values):
    return jax.nn.gelu(values, approximate=False)


def swap(values, axis, bits):
    count = lax.axis_size(axis)
    return lax.ppermute(values, axis, [(i, i ^ bits) for i in range(count)])


def after(values, *earlier):
    return lax.optimization_barrier((values, earlier))[0]


def bit_of(axis, bit):
    return (lax.axis_index(axis) // bit) % 2


def in_order(bit, mine, other, axis=0):
    return jnp.concatenate([jnp.where(bit == 0, mine, other), jnp.where(bit == 0, other, mine)], axis)


def by_device(pieces, index):
    step = 1
    while step < len(pieces):
        odd = (index // step) % 2 == 1
        pieces = [jnp.where(odd, pieces[i ^ step], pieces[i]) for i in range(len(pieces))]
        step *= 2
    return pieces


def add_half(halves, axis, bit):
    which = bit_of(axis, bit)
    got = swap(jnp.where(which == 0, halves[1], halves[0]), axis, bit)
    kept = jnp.where(which == 0, halves[0], halves[1])
    return (kept.astype(f32) + got.astype(f32)).astype(bf16)


def halves_of(values, axis):
    half = values.shape[axis] // 2
    return (
        lax.slice_in_dim(values, 0, half, axis=axis),
        lax.slice_in_dim(values, half, 2 * half, axis=axis),
    )


def share_half(values, axis, bit, dim):
    return in_order(bit_of(axis, bit), values, swap(values, axis, bit), dim)


def gather_small(shard):
    if lax.axis_size("fsdp") != 2:
        return lax.all_gather(shard[None], "fsdp", axis=0, tiled=True)
    return in_order(lax.axis_index("fsdp"), shard[None], swap(shard[None], "fsdp", 1))


def quarter_of(shard):
    quarter = shard.shape[0] // 4
    place = bit_of("blk", 1) * 2 + bit_of("blk", 2)
    return lax.dynamic_slice_in_dim(shard, place * quarter, quarter)


def both_shards(shard, half):
    return in_order(lax.axis_index("fsdp"), shard, share_half(half, "blk", 1, 0))


def attend_kernel(rank, q_ref, g_ref, *refs):
    kv_refs = refs[:-9]
    o_ref, dq_ref, keep_ref, send_ref, rows, lanes, sums, probs, order = refs[-9:]
    heads = range(q_ref.shape[0])
    cols = q_ref.shape[0] * HEAD
    n_keys = rank.shape[0]
    own = q_ref.shape[-1] // STRETCH
    wide = 2 * STRETCH
    span = CHUNK * STRETCH

    for t in range(n_keys):
        i, at = t // own, (t % own) * STRETCH
        place = rank[t]
        for h in heads:
            both = jnp.concatenate(
                [
                    kv_refs[i][first : first + HEAD, at : at + STRETCH]
                    for first in (h * HEAD, cols + h * HEAD)
                ],
                0,
            )
            lanes[h, place] = both
            rows[h, place] = both.T
            sums[h, t] = jnp.zeros((STRETCH, 2 * HEAD), f32)
    for a in range(own):
        before = jnp.int32(0)
        for b in range(own):
            before += (rank[b] < rank[a]).astype(jnp.int32)
        order[before] = a

    def side(h, j, part):
        first = part * HEAD
        return jnp.concatenate(
            [lanes[h, j * CHUNK + i, first : first + HEAD, :] for i in range(CHUNK)], 1
        )

    def keys(h, j):
        return rows[h, pl.ds(j * CHUNK, CHUNK)].reshape(span, 2 * HEAD)

    def pair(p, carry):
        a, b = order[2 * p], order[2 * p + 1]
        ra, rb = rank[a], rank[b]
        at_a = pl.ds(pl.multiple_of(a * STRETCH, STRETCH), STRETCH)
        at_b = pl.ds(pl.multiple_of(b * STRETCH, STRETCH), STRETCH)
        q = [jnp.concatenate([q_ref[h, :, at_a], q_ref[h, :, at_b]], 1) for h in heads]
        g = [jnp.concatenate([g_ref[h, :, at_a], g_ref[h, :, at_b]], 1) for h in heads]
        none = jnp.zeros_like(q[0])
        q_low = [jnp.concatenate([v, none], 0) for v in q]
        g_high = [jnp.concatenate([none, v], 0) for v in g]
        lane = lax.broadcasted_iota(jnp.int32, (1, wide), 1)
        q_place = jnp.where(lane < STRETCH, ra * STRETCH + lane, rb * STRETCH + lane - STRETCH)
        clear = ra // CHUNK
        total = (rb + CHUNK) // CHUNK

        def score(j, tops, masked):
            result = []
            for h in heads:
                s = jnp.dot(keys(h, j), q_low[h], preferred_element_type=f32)
                if masked:
                    k_place = j * span + lax.broadcasted_iota(jnp.int32, (span, 1), 0)
                    s = jnp.where(k_place <= q_place, s, BIG_NEG)
                probs[h, j] = s
                result.append(jnp.maximum(tops[h], jnp.max(s.reshape(span // 8, 8, wide), 0)))
            return tuple(result)

        tops = tuple(jnp.full((8, wide), BIG_NEG, f32) for _ in heads)
        tops = lax.fori_loop(0, clear, lambda j, v: score(j, v, False), tops)
        tops = lax.fori_loop(clear, total, lambda j, v: score(j, v, True), tops)
        tops = [jnp.max(v, 0, keepdims=True) for v in tops]

        def weigh(j, state):
            result = []
            for h in heads:
                count, out = state[h]
                weight = jnp.exp(probs[h, j] - tops[h])
                probs[h, j] = weight
                count = count + jnp.sum(weight.reshape(span // 8, 8, wide), 0)
                out = out + jnp.dot(side(h, j, 1), weight.astype(bf16), preferred_element_type=f32)
                result.append((count, out))
            return tuple(result)

        state = tuple((jnp.zeros((8, wide), f32), jnp.zeros((HEAD, wide), f32)) for _ in heads)
        state = lax.fori_loop(0, total, weigh, state)
        inverse, delta, right = [], [], []
        for h in heads:
            count, out = state[h]
            inverse.append(1.0 / jnp.sum(count, 0, keepdims=True))
            out = out * inverse[h]
            delta.append(jnp.sum(out * g[h].astype(f32), 0, keepdims=True))
            o_ref[h, :, at_a] = out[:, :STRETCH].astype(bf16)
            o_ref[h, :, at_b] = out[:, STRETCH:].astype(bf16)
            top = jnp.concatenate([g[h], none], 0).T
            right.append(jnp.concatenate([top, jnp.concatenate([none, q[h]], 0).T], 0))

        def back(j, d_q):
            result = []
            for h in heads:
                weight = probs[h, j] * inverse[h]
                d_weight = jnp.dot(keys(h, j), g_high[h], preferred_element_type=f32)
                d_score = (weight * (d_weight - delta[h])).astype(bf16)
                left = jnp.concatenate([weight.astype(bf16), d_score], 1)
                sums[h, pl.ds(j * CHUNK, CHUNK)] += jnp.dot(
                    left, right[h], preferred_element_type=f32
                ).reshape(CHUNK, STRETCH, 2 * HEAD)
                result.append(d_q[h] + jnp.dot(side(h, j, 0), d_score, preferred_element_type=f32))
            return tuple(result)

        d_q = lax.fori_loop(0, total, back, tuple(jnp.zeros((HEAD, wide), f32) for _ in heads))
        for h in heads:
            scaled = d_q[h] * HEAD ** (-0.5)
            dq_ref[h, :, at_a] = scaled[:, :STRETCH]
            dq_ref[h, :, at_b] = scaled[:, STRETCH:]
        return carry

    lax.fori_loop(0, own // 2, pair, 0)
    for t in range(n_keys):
        i, at = t // own, (t % own) * STRETCH
        to = keep_ref if i % 2 == 0 else send_ref
        for h in heads:
            turned = sums[h, rank[t]].T.astype(bf16)
            first = h * HEAD
            to[i // 2, cols + first : cols + first + HEAD, at : at + STRETCH] = turned[:HEAD]
            to[i // 2, first : first + HEAD, at : at + STRETCH] = turned[HEAD:]


def attend(ranks, q, g, kv):
    heads, _, count = q.shape
    devices = len(kv)
    n_keys = devices * count // STRETCH
    pairs = heads * 4 * HEAD * count * count * devices
    half = (devices // 2, 2 * heads * HEAD, count)
    q_spec = pl.BlockSpec(q.shape, lambda i, *_: (0, 0, 0))
    half_spec = pl.BlockSpec(half, lambda i, *_: (0, 0, 0))
    return pl.pallas_call(
        attend_kernel,
        grid_spec=pltpu.PrefetchScalarGridSpec(
            num_scalar_prefetch=1,
            grid=(1,),
            in_specs=[q_spec, q_spec] + [pl.BlockSpec(v.shape, lambda i, *_: (0, 0)) for v in kv],
            out_specs=[q_spec, q_spec, half_spec, half_spec],
            scratch_shapes=[
                pltpu.VMEM((heads, n_keys, STRETCH, 2 * HEAD), bf16),
                pltpu.VMEM((heads, n_keys, 2 * HEAD, STRETCH), bf16),
                pltpu.VMEM((heads, n_keys, STRETCH, 2 * HEAD), f32),
                pltpu.VMEM((heads, n_keys // CHUNK, CHUNK * STRETCH, 2 * STRETCH), f32),
                pltpu.SMEM((count // STRETCH,), jnp.int32),
            ],
        ),
        out_shape=[
            jax.ShapeDtypeStruct(q.shape, bf16),
            jax.ShapeDtypeStruct(q.shape, f32),
            jax.ShapeDtypeStruct(half, bf16),
            jax.ShapeDtypeStruct(half, bf16),
        ],
        compiler_params=pltpu.CompilerParams(vmem_limit_bytes=56 * 2**20),
        cost_estimate=pl.CostEstimate(
            flops=12 * pairs, bytes_accessed=16 * q.size * devices, transcendentals=pairs // 512
        ),
        name="attend",
    )(ranks, q, g, *kv)


def prepare_kernel(freqs, gain, shift, weight, bias, *refs):
    groups = len(refs) - 5
    x_refs = refs[:groups]
    normed_ref, q_ref, kv_ref, cos_ref, sin_ref = refs[groups:]
    count = normed_ref.shape[0] // groups
    cols = q_ref.shape[0]
    halfway = ROT // 2
    blocks = count // STRETCH
    lane = lax.broadcasted_iota(jnp.int32, (1, STRETCH), 1).astype(f32)
    kv_ref[2 * cols :, :] = jnp.zeros((kv_ref.shape[0] - 2 * cols, kv_ref.shape[1]), bf16)
    spots = lax.broadcasted_iota(jnp.int32, (1, STRETCH), 1)
    table = jnp.zeros((1, STRETCH), f32)
    for i, x_ref in enumerate(x_refs):
        at = i * count
        normed = layer_norm(x_ref[:count].astype(f32), gain[...], shift[...]).astype(bf16)
        normed_ref[at : at + count] = normed
        joined = jnp.dot(normed, weight[...], preferred_element_type=f32) + bias[...]
        joined = joined.T
        ranks = x_ref[count : count + 16, :STRETCH].astype(f32)[:1]
        places = []
        for b in range(blocks):
            rank = jnp.sum(jnp.where(spots == b, ranks, 0.0), 1, keepdims=True)
            places.append(rank * STRETCH + lane)
            table = jnp.where(spots == i * blocks + b, rank, table)
        angles = freqs[...] * jnp.concatenate(places, 1)
        cosine, sine = jnp.cos(angles), jnp.sin(angles)
        cos_ref[:, at : at + count] = cosine
        sin_ref[:, at : at + count] = sine
        for to, first, scale in ((q_ref, 0, HEAD ** (-0.5)), (kv_ref, cols, 1.0)):
            for h in range(cols // HEAD):
                low = first + h * HEAD
                one = joined[low : low + halfway]
                two = joined[low + halfway : low + ROT]
                rest = joined[low + ROT : low + HEAD]
                turned = jnp.concatenate(
                    [one * cosine - two * sine, two * cosine + one * sine, rest], 0
                ).astype(bf16)
                to[h * HEAD : (h + 1) * HEAD, at : at + count] = turned * jnp.bfloat16(scale)
        kv_ref[cols : 2 * cols, at : at + count] = joined[2 * cols :].astype(bf16)
    kv_ref[2 * cols :, :STRETCH] = jnp.broadcast_to(table, (16, STRETCH)).astype(bf16)


def prepare(gain, shift, weight, bias, x_all, count):
    width = weight.shape[0]
    cols = weight.shape[1] // 3
    rows = count * len(x_all)
    halfway = ROT // 2
    freqs = jnp.asarray(10000.0 ** (-np.arange(halfway) * 2.0 / ROT), f32)[:, None]
    return pl.pallas_call(
        prepare_kernel,
        out_shape=[
            jax.ShapeDtypeStruct((rows, width), bf16),
            jax.ShapeDtypeStruct((cols, rows), bf16),
            jax.ShapeDtypeStruct((2 * cols + 16, rows), bf16),
            jax.ShapeDtypeStruct((ROT // 2, rows), f32),
            jax.ShapeDtypeStruct((ROT // 2, rows), f32),
        ],
        compiler_params=pltpu.CompilerParams(vmem_limit_bytes=40 * 2**20),
        cost_estimate=pl.CostEstimate(
            flops=6 * cols * rows * width, bytes_accessed=8 * rows * width, transcendentals=0
        ),
        name="prepare",
    )(freqs, gain[None], shift[None], weight, bias[None], *x_all)


def rotate(heads, cosine, sine):
    halfway = ROT // 2
    first = heads[:, :halfway]
    second = heads[:, halfway:ROT]
    return jnp.concatenate(
        [first * cosine - second * sine, second * cosine + first * sine, heads[:, ROT:]], 1
    )


def around(values):
    return [values] + [swap(values, "ulysses", j) for j in range(1, lax.axis_size("ulysses"))]


def stacked_terms(lists):
    return [jnp.stack(v) for v in zip(*lists)]


def to_tokens(values):
    groups = lax.axis_size("ulysses")
    count = values.shape[1] // groups
    pieces = [values[:, j * count : (j + 1) * count] for j in range(groups)]
    return [pieces[0]] + [swap(pieces[j], "ulysses", j) for j in range(1, groups)]


def units_of(up_weight, side):
    units = up_weight.shape[1] // 2
    return jnp.where(side == 0, up_weight[:, :units], up_weight[:, units:])


def mlp_pair(x_both, e_both, gain, shift, up, up_bias, down_weight, *meanwhile):
    side = lax.axis_index("fsdp")
    rows, width = x_both.shape[0] // 2, x_both.shape[1]
    units = up.shape[1]
    normed = layer_norm(x_both.astype(f32), gain, shift).astype(bf16)
    hidden = jnp.dot(normed, up, preferred_element_type=f32) + up_bias.astype(f32)
    active_f, pull_gelu = jax.vjp(gelu_exact, hidden)
    active = active_f.astype(bf16)
    part = jnp.dot(active, down_weight, preferred_element_type=f32)
    d_active = jnp.einsum("td,fd->tf", e_both, down_weight, preferred_element_type=f32)
    d_hidden = pull_gelu(d_active)[0].astype(bf16)
    g_up_bias = jnp.sum(d_hidden.astype(f32), 0)
    d_part = jnp.einsum("tf,df->td", d_hidden, up, preferred_element_type=f32)
    sent = jnp.concatenate([part[rows:], d_part[rows:]]).astype(bf16)
    active, d_hidden = after((active, d_hidden), *meanwhile)
    g_up = jnp.einsum(
        "td,tcf->cdf", normed, d_hidden.reshape(2 * rows, 2, units // 2), preferred_element_type=f32
    ).astype(bf16)
    g_down = jnp.einsum("tf,td->fd", active, e_both, preferred_element_type=f32).astype(bf16)
    g_down = g_down.reshape(2, units // 2, width)
    pieces = jnp.stack([g_up, g_down], 1).reshape(2, 2, 2, width // 2, width)
    first = add_half((pieces[0], pieces[1]), "blk", 1)
    got = swap(after(sent, first), "fsdp", 1).astype(f32)
    out, d_normed = part[:rows] + got[:rows], d_part[:rows] + got[rows:]
    sums = add_half(halves_of(first, 2), "blk", 2)
    side, none = lax.axis_index("fsdp"), jnp.zeros_like(g_up_bias)
    g_up_bias = jnp.concatenate([jnp.where(side == 0, g_up_bias, none), jnp.where(side == 0, none, g_up_bias)])
    return out, d_normed, first, sums, g_up_bias


def finish_pair(sums, earlier):
    side = lax.axis_index("fsdp")
    sums = after(sums, earlier)
    sums = add_half(halves_of(sums, 2), "ulysses", 1)
    sums = add_half(halves_of(sums, 2), "ulysses", 2)
    got = swap(jnp.where(side == 0, sums[0, 1], sums[0, 0]), "fsdp", 1)
    kept = jnp.where(side == 0, sums[0, 0], sums[0, 1])
    sums = jnp.concatenate([in_order(side, kept[None], got[None]), sums[1]], 0)
    return share_half(sums, "ulysses", 2, 1)


def spread_pair(sums):
    sums = share_half(sums, "ulysses", 1, 1)
    sums = share_half(sums, "blk", 2, 1)
    return place_mlp(bit_of("blk", 1), sums, swap(sums, "blk", 1))


def place_mlp_kernel(which, mine, other, up_ref, down_ref):
    width = mine.shape[-1]
    for c, ref in ((which[0], mine), (1 - which[0], other)):
        for f in range(2):
            at = pl.multiple_of((2 * f + c) * width, STRETCH)
            up_ref[:, pl.ds(at, width)] = ref[f].astype(f32)
            down_ref[c, f] = ref[2 + f].astype(f32)


def place_mlp(which, mine, other):
    _, rows, width = mine.shape
    step = rows // 4
    whole = pl.BlockSpec((4, step, width), lambda i, *_: (0, i, 0))
    up, down = pl.pallas_call(
        place_mlp_kernel,
        grid_spec=pltpu.PrefetchScalarGridSpec(
            num_scalar_prefetch=1,
            grid=(4,),
            in_specs=[whole, whole],
            out_specs=[
                pl.BlockSpec((step, 4 * width), lambda i, *_: (i, 0)),
                pl.BlockSpec((2, 2, step, width), lambda i, *_: (0, 0, i, 0)),
            ],
        ),
        out_shape=[
            jax.ShapeDtypeStruct((rows, 4 * width), f32),
            jax.ShapeDtypeStruct((2, 2, rows, width), f32),
        ],
        compiler_params=pltpu.CompilerParams(vmem_limit_bytes=32 * 2**20),
        cost_estimate=pl.CostEstimate(flops=0, bytes_accessed=12 * mine.size, transcendentals=0),
        name="place_mlp",
    )(which[None], mine, other)
    return up, down.reshape(4 * rows, width)


def place_qkv_kernel(which, mine, other, qkv_ref, out_ref):
    first = which[0] == 0
    rows, half = mine.shape[1:]
    width = 2 * half
    groups = mine.shape[0] // 4
    for t in range(3):
        blocks = []
        for z in range(groups):
            a, b = mine[3 * z + t], other[3 * z + t]
            blocks += [jnp.where(first, a, b), jnp.where(first, b, a)]
        qkv_ref[:, t * width : (t + 1) * width] = jnp.concatenate(blocks, 0).astype(f32).T
    for z in range(groups // 2):
        for side in range(2):
            a, b = mine[3 * groups + 2 * z + side], other[3 * groups + 2 * z + side]
            at = 2 * z * rows
            both = jnp.concatenate([jnp.where(first, a, b), jnp.where(first, b, a)], 0)
            out_ref[at : at + 2 * rows, side * half : (side + 1) * half] = both.astype(f32)


def place_qkv(which, mine, other):
    _, rows, half = mine.shape
    groups = mine.shape[0] // 4
    return pl.pallas_call(
        place_qkv_kernel,
        grid_spec=pltpu.PrefetchScalarGridSpec(
            num_scalar_prefetch=1,
            grid=(1,),
            in_specs=[pl.BlockSpec(v.shape, lambda i, *_: (0, 0, 0)) for v in (mine, other)],
            out_specs=[
                pl.BlockSpec((half, 6 * half), lambda i, *_: (0, 0)),
                pl.BlockSpec((groups * rows, 2 * half), lambda i, *_: (0, 0)),
            ],
        ),
        out_shape=[
            jax.ShapeDtypeStruct((half, 6 * half), f32),
            jax.ShapeDtypeStruct((groups * rows, 2 * half), f32),
        ],
        compiler_params=pltpu.CompilerParams(vmem_limit_bytes=40 * 2**20),
        cost_estimate=pl.CostEstimate(flops=0, bytes_accessed=12 * mine.size, transcendentals=0),
        name="place_qkv",
    )(which[None], mine, other)


def mlp_gathered(x, e, gain, shift, up, bias, down, *meanwhile):
    normed = layer_norm(x.astype(f32), gain, shift).astype(bf16)
    hidden = jnp.dot(normed, up, preferred_element_type=f32) + bias.astype(f32)
    active_f, pull_gelu = jax.vjp(gelu_exact, hidden)
    active = active_f.astype(bf16)
    out = jnp.dot(active, down, preferred_element_type=f32)
    g_down = jnp.einsum("tf,td->fd", active, e, preferred_element_type=f32)
    d_active = jnp.einsum("td,fd->tf", e, down, preferred_element_type=f32)
    d_hidden = pull_gelu(d_active)[0].astype(bf16)
    g_up = jnp.einsum("td,tf->df", normed, d_hidden, preferred_element_type=f32)
    d_normed = jnp.einsum("tf,df->td", d_hidden, up, preferred_element_type=f32)
    g_up, g_down = (
        lax.psum(
            lax.psum_scatter(g.astype(bf16), "fsdp", scatter_dimension=0, tiled=True),
            ("blk", "ulysses"),
        ).astype(f32)
        for g in (g_up, g_down)
    )
    return out, d_normed, d_hidden, (g_up, g_down), jnp.sum(d_hidden.astype(f32), 0)


def add_blks(grads):
    if lax.axis_size("fsdp") != 2:
        return lax.psum(grads, "blk")
    return add_half(halves_of(add_half(halves_of(grads, 1), "blk", 1), 1), "blk", 2)


def attention_grads(grads, vector, output, g_up):
    side = lax.axis_index("fsdp")
    group = lax.axis_index("ulysses")
    groups = lax.axis_size("ulysses")
    _, rows, width = grads.shape
    if lax.axis_size("fsdp") != 2:
        total = lax.all_gather(lax.psum(grads, "fsdp"), "ulysses", axis=1, tiled=True)
        part = width // lax.axis_size("fsdp")
        g_qkv = lax.dynamic_slice_in_dim(total[:3], side * part, part, 2)
        g_out = lax.dynamic_slice_in_dim(total[3], side * part, part, 0)
        g_qkv = g_qkv.reshape(3 * width, part).T.astype(f32)
        return g_qkv, g_out.astype(f32), sum_everywhere(vector)
    half = width // 2
    size = vector.shape[0]
    small = jnp.pad(vector.astype(bf16), (0, rows * half - size)).reshape(1, rows, half)
    low, high = grads[:, :, :half], grads[:, :, half:]
    kept = jnp.where(side == 0, low[:3], high[:3])
    sent = jnp.where(side == 0, high[:3], low[:3])
    whole = jnp.stack([low[3], high[3]])
    kept = jnp.concatenate([kept, whole, small])
    got = swap(jnp.concatenate([sent, whole, small]), "fsdp", 1)
    kept = (kept.astype(f32) + got.astype(f32)).astype(bf16)
    kept = by_device(around(kept), group)
    small = sum(v[5:].astype(f32) for v in kept).astype(bf16)
    of_qkv = jnp.concatenate([v[:3] for v in kept])
    of_out = [jnp.where(side == 0, a[3:5], b[3:5]) for a, b in zip(kept[: groups // 2], kept[groups // 2 :])]
    kept = jnp.concatenate([of_qkv] + of_out)
    units = kept.shape[0]
    got = after(swap(jnp.concatenate([kept, small]), "blk", 2), output)
    kept = in_order(bit_of("blk", 2), kept, got[:units], 1)
    small = (small.astype(f32) + got[units:].astype(f32)).astype(bf16)
    wide = jnp.pad(small, ((0, 0), (0, rows), (0, 0)))
    got = after(swap(jnp.concatenate([kept, wide]), "blk", 1), g_up)
    small = small.astype(f32) + got[units:, :rows].astype(f32)
    g_qkv, g_out = place_qkv(bit_of("blk", 1), kept, got)
    return g_qkv, g_out, small.reshape(-1)[:size]


def sum_everywhere(values):
    for axis in ("blk", "ulysses", "fsdp"):
        step = 1
        while step < lax.axis_size(axis):
            values = values + swap(values, axis, step)
            step *= 2
    return values


def on_device(
    tokens,
    positions,
    cotangent,
    ln1_gain,
    ln1_bias,
    ln2_gain,
    ln2_bias,
    qkv_weight,
    qkv_bias,
    out_weight,
    out_bias,
    up_weight,
    up_bias,
    down_weight,
    down_bias,
):
    count, width = tokens.shape
    groups = lax.axis_size("ulysses")
    group = lax.axis_index("ulysses")
    shards = lax.axis_size("fsdp")
    cols = width // groups
    heads = cols // HEAD
    rows = count * groups

    ranks = (positions[::STRETCH] // STRETCH).astype(bf16)[None]
    ranks = jnp.pad(ranks, ((0, 15), (0, width - ranks.shape[1])))
    x_ranks = jnp.concatenate([tokens, ranks])
    if shards == 2:
        side = lax.axis_index("fsdp")
        part_qkv = swap(quarter_of(qkv_weight), "fsdp", 1)
        half_up = jnp.concatenate([units_of(up_weight, 1 - side), out_weight], 1)
        part_up = swap(after(quarter_of(half_up), part_qkv), "fsdp", 1)
        x_e = swap(after(jnp.stack([tokens, cotangent]), part_up), "fsdp", 1)
        half_qkv = share_half(part_qkv, "blk", 2, 0)
        w_qkv = both_shards(qkv_weight, half_qkv)
        half_up = share_half(after(part_up, half_qkv), "blk", 2, 0)
        x_all = around(x_ranks)
        mine = jnp.concatenate([units_of(up_weight, side), out_weight], 1)
        half_up = both_shards(mine, half_up)
        w_up, w_out = half_up[:, :-width], half_up[:, -width:]
        x_mlp = jnp.concatenate([tokens, x_e[0]])
        e_mlp = jnp.concatenate([cotangent, x_e[1]])
        b_up, w_down = up_bias, down_weight
        mlp, finish, spread = mlp_pair, finish_pair, spread_pair
    else:
        x_all, part_qkv = around(x_ranks), x_ranks
        w_qkv, w_up, w_out, w_down = (
            lax.all_gather(w, "fsdp", axis=0, tiled=True)
            for w in (qkv_weight, up_weight, out_weight, down_weight)
        )
        b_up = gather_small(up_bias).reshape(-1)
        x_mlp, e_mlp = tokens, cotangent
        mlp, finish, spread = mlp_gathered, lambda v, _: v, lambda v: v
    small = jnp.concatenate([ln1_gain, ln1_bias, ln2_gain, ln2_bias, out_bias, down_bias, qkv_bias])
    small = gather_small(after(small, part_qkv))
    part = width // shards
    ln1_g, ln1_b, ln2_g, ln2_b, b_out, b_down = (
        small[:, i * part : (i + 1) * part].reshape(width).astype(f32) for i in range(6)
    )
    b_qkv = small[:, 6 * part :].reshape(3 * width).astype(f32)
    starts = [i * width + group * cols for i in range(3)]
    w_mine = jnp.concatenate([lax.dynamic_slice_in_dim(w_qkv, v, cols, 1) for v in starts], 1)
    b_mine = jnp.concatenate([lax.dynamic_slice_in_dim(b_qkv, v, cols, 0) for v in starts])
    x_all = after(x_all, w_mine)
    normed, queries, kv, cosine, sine = prepare(ln1_g, ln1_b, w_mine, b_mine, x_all, count)
    queries = queries.reshape(heads, HEAD, rows)
    pieces = {0: kv}
    step = lax.axis_size("blk") // 2
    while step >= 1:
        for i in list(pieces):
            pieces[i ^ step] = swap(pieces[i], "blk", step)
        step //= 2
    kv_all = [pieces[i] for i in range(len(pieces))]
    ranks = jnp.concatenate([v[2 * cols, : rows // STRETCH] for v in kv_all]).astype(jnp.int32)

    d_mixed = jnp.einsum("ed,td->et", w_out, after(cotangent, kv), preferred_element_type=f32).astype(bf16)
    d_heads = [lax.dynamic_slice_in_dim(d_mixed, (group ^ j) * cols, cols) for j in range(groups)]
    d_heads = [d_heads[0]] + [swap(d_heads[j], "ulysses", j) for j in range(1, groups)]
    d_heads = jnp.concatenate(d_heads, 1).reshape(heads, HEAD, rows)

    x_mlp, w_up = after((x_mlp, w_up), kv, d_mixed)
    mlp_out, d_norm_two, begun, terms, g_up_bias = mlp(
        x_mlp, e_mlp, ln2_g, ln2_b, w_up, b_up, w_down, pieces[lax.axis_size("blk") // 2], pieces[1], d_heads
    )

    e_around = around(after(cotangent, begun))
    d_heads = after(d_heads, begun)
    mixed, d_q, kept, sent = attend(ranks, queries, d_heads, kv_all)

    sent, e_around, terms, mlp_out, d_norm_two = after((sent, e_around, terms, mlp_out, d_norm_two))
    got = swap(sent, "blk", 1)
    step, kept = 1, [[kept[i], got[i]] for i in range(kept.shape[0])]
    while len(kept) > 1:
        step *= 2
        sent = sum(v.astype(f32) for v in stacked_terms(kept[1::2])).astype(bf16)
        terms = finish(terms, sent) if step == 2 else terms
        got = swap(sent, "blk", step)
        kept = [kept[2 * i] + [got[i]] for i in range(got.shape[0])]
    total = sum(v.astype(f32) for v in kept[0])
    d_q = rotate(d_q, cosine, -sine).astype(bf16).reshape(cols, rows)
    mixed = mixed.reshape(cols, rows)
    back_q = to_tokens(after(jnp.concatenate([d_q, mixed]), sent))
    e_all = jnp.concatenate(e_around, 0)
    g_out = jnp.dot(mixed, e_all, preferred_element_type=f32).astype(bf16)
    d_k = rotate(total[:cols].reshape(heads, HEAD, rows), cosine, -sine).reshape(cols, rows)
    d_kv = jnp.concatenate([d_k, total[cols:]]).astype(bf16)
    d_joined = jnp.concatenate([d_q, d_kv])
    g_bias_mine = jnp.sum(d_joined.astype(f32), 1)
    g_qkv = jnp.dot(d_joined, normed, preferred_element_type=f32).astype(bf16)
    back_kv = to_tokens(d_kv)
    grads = jnp.concatenate([g_qkv.reshape(3, cols, width), g_out[None]])
    grads = add_blks(grads)
    back_kv = after(back_kv, grads, terms)
    g_up, g_down = spread(terms)
    back_q, back_kv = by_device(back_q, group), by_device(back_kv, group)
    d_mine = jnp.concatenate(
        [v[:cols] for v in back_q] + [v[:cols] for v in back_kv] + [v[cols:] for v in back_kv], 0
    )
    d_norm_one = jnp.einsum("et,de->td", d_mine, w_qkv, preferred_element_type=f32)
    x_float = tokens.astype(f32)
    _, pull_one = jax.vjp(layer_norm, x_float, ln1_g, ln1_b)
    _, pull_two = jax.vjp(layer_norm, x_float, ln2_g, ln2_b)
    d_x_one, g_ln1_g, g_ln1_b = pull_one(d_norm_one)
    d_x_two, g_ln2_g, g_ln2_b = pull_two(d_norm_two)
    e_float = cotangent.astype(f32)

    g_qkv_bias = jnp.zeros((3, groups, cols), f32)
    g_qkv_bias = lax.dynamic_update_slice(g_qkv_bias, g_bias_mine.reshape(3, 1, cols), (0, group, 0))
    vectors = [g_ln1_g, g_ln1_b, g_ln2_g, g_ln2_b, jnp.sum(e_float, 0), g_qkv_bias.reshape(-1), g_up_bias]
    back = jnp.concatenate([v[cols:] for v in back_q], 0)
    attn_out = jnp.einsum("et,ed->td", back, w_out, preferred_element_type=f32)
    output = (x_float + (attn_out + b_out) + (mlp_out + b_down)).astype(bf16)
    input_grad = (e_float + d_x_one + d_x_two).astype(bf16)

    g_qkv, g_out, summed = attention_grads(grads, jnp.concatenate(vectors), output, g_up)
    results, start = [], 0
    for vector in vectors:
        mine = vector.shape[0] // shards
        results.append(lax.dynamic_slice_in_dim(summed, start + lax.axis_index("fsdp") * mine, mine))
        start += vector.shape[0]
    g_ln1_g, g_ln1_b, g_ln2_g, g_ln2_b, g_e, g_qkv_bias, g_up_bias = results
    return (
        output,
        input_grad,
        g_ln1_g,
        g_ln1_b,
        g_ln2_g,
        g_ln2_b,
        g_qkv,
        g_qkv_bias,
        g_out,
        g_e,
        g_up,
        g_up_bias,
        g_down,
        g_e,
    )


def solution(mesh):
    rows = P(("fsdp", "blk", "ulysses"), None)
    split, matrix = P("fsdp"), P("fsdp", None)
    return jax.shard_map(
        on_device,
        mesh=mesh,
        in_specs=(
            rows,
            P(("fsdp", "blk", "ulysses")),
            rows,
            split,
            split,
            split,
            split,
            matrix,
            split,
            matrix,
            split,
            matrix,
            split,
            matrix,
            split,
        ),
        out_specs=(
            rows,
            rows,
            split,
            split,
            split,
            split,
            matrix,
            split,
            matrix,
            split,
            matrix,
            split,
            matrix,
            split,
        ),
        check_vma=False,
    )
```

```python
import jax
import jax.numpy as jnp
import numpy as np
from jax import lax
from jax.experimental import pallas as pl
from jax.experimental.pallas import tpu as pltpu
from jax.sharding import PartitionSpec as P

HEAD = 64
ROT = 16
STRETCH = 128
CHUNK = 8
BIG_NEG = -1e30

f32 = jnp.float32
bf16 = jnp.bfloat16


def layer_norm(values, gain, shift):
    center = jnp.mean(values, -1, keepdims=True)
    offset = values - center
    spread = jnp.mean(offset * offset, -1, keepdims=True)
    return offset * lax.rsqrt(spread + 1e-05) * gain + shift


def gelu_exact(values):
    return jax.nn.gelu(values, approximate=False)


def swap(values, axis, bits):
    count = lax.axis_size(axis)
    return lax.ppermute(values, axis, [(i, i ^ bits) for i in range(count)])


def after(values, *earlier):
    return lax.optimization_barrier((values, earlier))[0]


def bit_of(axis, bit):
    return (lax.axis_index(axis) // bit) % 2


def in_order(bit, mine, other, axis=0):
    return jnp.concatenate([jnp.where(bit == 0, mine, other), jnp.where(bit == 0, other, mine)], axis)


def by_device(pieces, index):
    step = 1
    while step < len(pieces):
        odd = (index // step) % 2 == 1
        pieces = [jnp.where(odd, pieces[i ^ step], pieces[i]) for i in range(len(pieces))]
        step *= 2
    return pieces


def add_half(halves, axis, bit):
    which = bit_of(axis, bit)
    got = swap(jnp.where(which == 0, halves[1], halves[0]), axis, bit)
    kept = jnp.where(which == 0, halves[0], halves[1])
    return (kept.astype(f32) + got.astype(f32)).astype(bf16)


def halves_of(values, axis):
    half = values.shape[axis] // 2
    return (
        lax.slice_in_dim(values, 0, half, axis=axis),
        lax.slice_in_dim(values, half, 2 * half, axis=axis),
    )


def share_half(values, axis, bit, dim):
    return in_order(bit_of(axis, bit), values, swap(values, axis, bit), dim)


def gather_small(shard):
    if lax.axis_size("fsdp") != 2:
        return lax.all_gather(shard[None], "fsdp", axis=0, tiled=True)
    return in_order(lax.axis_index("fsdp"), shard[None], swap(shard[None], "fsdp", 1))


def quarter_of(shard):
    quarter = shard.shape[0] // 4
    place = bit_of("blk", 1) * 2 + bit_of("blk", 2)
    return lax.dynamic_slice_in_dim(shard, place * quarter, quarter)


def both_shards(shard, half):
    return in_order(lax.axis_index("fsdp"), shard, share_half(half, "blk", 1, 0))


def attend_kernel(rank, q_ref, g_ref, *refs):
    kv_refs = refs[:-9]
    o_ref, dq_ref, keep_ref, send_ref, rows, lanes, sums, probs, order = refs[-9:]
    heads = range(q_ref.shape[0])
    cols = q_ref.shape[0] * HEAD
    n_keys = rank.shape[0]
    own = q_ref.shape[-1] // STRETCH
    wide = 2 * STRETCH
    span = CHUNK * STRETCH

    for t in range(n_keys):
        i, at = t // own, (t % own) * STRETCH
        place = rank[t]
        for h in heads:
            both = jnp.concatenate(
                [
                    kv_refs[i][first : first + HEAD, at : at + STRETCH]
                    for first in (h * HEAD, cols + h * HEAD)
                ],
                0,
            )
            lanes[h, place] = both
            rows[h, place] = both.T
            sums[h, t] = jnp.zeros((STRETCH, 2 * HEAD), f32)
    for a in range(own):
        before = jnp.int32(0)
        for b in range(own):
            before += (rank[b] < rank[a]).astype(jnp.int32)
        order[before] = a

    def side(h, j, part):
        first = part * HEAD
        return jnp.concatenate(
            [lanes[h, j * CHUNK + i, first : first + HEAD, :] for i in range(CHUNK)], 1
        )

    def keys(h, j):
        return rows[h, pl.ds(j * CHUNK, CHUNK)].reshape(span, 2 * HEAD)

    def pair(p, carry):
        a, b = order[2 * p], order[2 * p + 1]
        ra, rb = rank[a], rank[b]
        at_a = pl.ds(pl.multiple_of(a * STRETCH, STRETCH), STRETCH)
        at_b = pl.ds(pl.multiple_of(b * STRETCH, STRETCH), STRETCH)
        q = [jnp.concatenate([q_ref[h, :, at_a], q_ref[h, :, at_b]], 1) for h in heads]
        g = [jnp.concatenate([g_ref[h, :, at_a], g_ref[h, :, at_b]], 1) for h in heads]
        none = jnp.zeros_like(q[0])
        q_low = [jnp.concatenate([v, none], 0) for v in q]
        g_high = [jnp.concatenate([none, v], 0) for v in g]
        lane = lax.broadcasted_iota(jnp.int32, (1, wide), 1)
        q_place = jnp.where(lane < STRETCH, ra * STRETCH + lane, rb * STRETCH + lane - STRETCH)
        clear = ra // CHUNK
        total = (rb + CHUNK) // CHUNK

        def score(j, tops, masked):
            result = []
            for h in heads:
                s = jnp.dot(keys(h, j), q_low[h], preferred_element_type=f32)
                if masked:
                    k_place = j * span + lax.broadcasted_iota(jnp.int32, (span, 1), 0)
                    s = jnp.where(k_place <= q_place, s, BIG_NEG)
                probs[h, j] = s
                result.append(jnp.maximum(tops[h], jnp.max(s.reshape(span // 8, 8, wide), 0)))
            return tuple(result)

        tops = tuple(jnp.full((8, wide), BIG_NEG, f32) for _ in heads)
        tops = lax.fori_loop(0, clear, lambda j, v: score(j, v, False), tops)
        tops = lax.fori_loop(clear, total, lambda j, v: score(j, v, True), tops)
        tops = [jnp.max(v, 0, keepdims=True) for v in tops]

        def weigh(j, state):
            result = []
            for h in heads:
                count, out = state[h]
                weight = jnp.exp(probs[h, j] - tops[h])
                probs[h, j] = weight
                count = count + jnp.sum(weight.reshape(span // 8, 8, wide), 0)
                out = out + jnp.dot(side(h, j, 1), weight.astype(bf16), preferred_element_type=f32)
                result.append((count, out))
            return tuple(result)

        state = tuple((jnp.zeros((8, wide), f32), jnp.zeros((HEAD, wide), f32)) for _ in heads)
        state = lax.fori_loop(0, total, weigh, state)
        inverse, delta, right = [], [], []
        for h in heads:
            count, out = state[h]
            inverse.append(1.0 / jnp.sum(count, 0, keepdims=True))
            out = out * inverse[h]
            delta.append(jnp.sum(out * g[h].astype(f32), 0, keepdims=True))
            o_ref[h, :, at_a] = out[:, :STRETCH].astype(bf16)
            o_ref[h, :, at_b] = out[:, STRETCH:].astype(bf16)
            top = jnp.concatenate([g[h], none], 0).T
            right.append(jnp.concatenate([top, jnp.concatenate([none, q[h]], 0).T], 0))

        def back(j, d_q):
            result = []
            for h in heads:
                weight = probs[h, j] * inverse[h]
                d_weight = jnp.dot(keys(h, j), g_high[h], preferred_element_type=f32)
                d_score = (weight * (d_weight - delta[h])).astype(bf16)
                left = jnp.concatenate([weight.astype(bf16), d_score], 1)
                sums[h, pl.ds(j * CHUNK, CHUNK)] += jnp.dot(
                    left, right[h], preferred_element_type=f32
                ).reshape(CHUNK, STRETCH, 2 * HEAD)
                result.append(d_q[h] + jnp.dot(side(h, j, 0), d_score, preferred_element_type=f32))
            return tuple(result)

        d_q = lax.fori_loop(0, total, back, tuple(jnp.zeros((HEAD, wide), f32) for _ in heads))
        for h in heads:
            scaled = d_q[h] * HEAD ** (-0.5)
            dq_ref[h, :, at_a] = scaled[:, :STRETCH]
            dq_ref[h, :, at_b] = scaled[:, STRETCH:]
        return carry

    lax.fori_loop(0, own // 2, pair, 0)
    for t in range(n_keys):
        i, at = t // own, (t % own) * STRETCH
        to = keep_ref if i % 2 == 0 else send_ref
        for h in heads:
            turned = sums[h, rank[t]].astype(bf16).T
            first = h * HEAD
            to[i // 2, cols + first : cols + first + HEAD, at : at + STRETCH] = turned[:HEAD]
            to[i // 2, first : first + HEAD, at : at + STRETCH] = turned[HEAD:]


def attend(ranks, q, g, kv):
    heads, _, count = q.shape
    devices = len(kv)
    n_keys = devices * count // STRETCH
    pairs = heads * 4 * HEAD * count * count * devices
    half = (devices // 2, 2 * heads * HEAD, count)
    q_spec = pl.BlockSpec(q.shape, lambda i, *_: (0, 0, 0))
    half_spec = pl.BlockSpec(half, lambda i, *_: (0, 0, 0))
    return pl.pallas_call(
        attend_kernel,
        grid_spec=pltpu.PrefetchScalarGridSpec(
            num_scalar_prefetch=1,
            grid=(1,),
            in_specs=[q_spec, q_spec] + [pl.BlockSpec(v.shape, lambda i, *_: (0, 0)) for v in kv],
            out_specs=[q_spec, q_spec, half_spec, half_spec],
            scratch_shapes=[
                pltpu.VMEM((heads, n_keys, STRETCH, 2 * HEAD), bf16),
                pltpu.VMEM((heads, n_keys, 2 * HEAD, STRETCH), bf16),
                pltpu.VMEM((heads, n_keys, STRETCH, 2 * HEAD), f32),
                pltpu.VMEM((heads, n_keys // CHUNK, CHUNK * STRETCH, 2 * STRETCH), f32),
                pltpu.SMEM((count // STRETCH,), jnp.int32),
            ],
        ),
        out_shape=[
            jax.ShapeDtypeStruct(q.shape, bf16),
            jax.ShapeDtypeStruct(q.shape, f32),
            jax.ShapeDtypeStruct(half, bf16),
            jax.ShapeDtypeStruct(half, bf16),
        ],
        compiler_params=pltpu.CompilerParams(vmem_limit_bytes=56 * 2**20),
        cost_estimate=pl.CostEstimate(
            flops=12 * pairs, bytes_accessed=16 * q.size * devices, transcendentals=pairs // 512
        ),
        name="attend",
    )(ranks, q, g, *kv)


def prepare_kernel(freqs, gain, shift, weight, bias, *refs):
    groups = len(refs) - 5
    x_refs = refs[:groups]
    normed_ref, q_ref, kv_ref, cos_ref, sin_ref = refs[groups:]
    count = normed_ref.shape[0] // groups
    cols = q_ref.shape[0]
    halfway = ROT // 2
    blocks = count // STRETCH
    lane = lax.broadcasted_iota(jnp.int32, (1, STRETCH), 1).astype(f32)
    kv_ref[2 * cols :, :] = jnp.zeros((kv_ref.shape[0] - 2 * cols, kv_ref.shape[1]), bf16)
    spots = lax.broadcasted_iota(jnp.int32, (1, STRETCH), 1)
    table = jnp.zeros((1, STRETCH), f32)
    for i, x_ref in enumerate(x_refs):
        at = i * count
        normed = layer_norm(x_ref[:count].astype(f32), gain[...], shift[...]).astype(bf16)
        normed_ref[at : at + count] = normed
        joined = jnp.dot(normed, weight[...], preferred_element_type=f32) + bias[...]
        joined = joined.T
        ranks = x_ref[count : count + 16, :STRETCH].astype(f32)[:1]
        places = []
        for b in range(blocks):
            rank = jnp.sum(jnp.where(spots == b, ranks, 0.0), 1, keepdims=True)
            places.append(rank * STRETCH + lane)
            table = jnp.where(spots == i * blocks + b, rank, table)
        angles = freqs[...] * jnp.concatenate(places, 1)
        cosine, sine = jnp.cos(angles), jnp.sin(angles)
        cos_ref[:, at : at + count] = cosine
        sin_ref[:, at : at + count] = sine
        for to, first, scale in ((q_ref, 0, HEAD ** (-0.5)), (kv_ref, cols, 1.0)):
            for h in range(cols // HEAD):
                low = first + h * HEAD
                one = joined[low : low + halfway]
                two = joined[low + halfway : low + ROT]
                rest = joined[low + ROT : low + HEAD]
                turned = jnp.concatenate(
                    [one * cosine - two * sine, two * cosine + one * sine, rest], 0
                ).astype(bf16)
                to[h * HEAD : (h + 1) * HEAD, at : at + count] = turned * jnp.bfloat16(scale)
        kv_ref[cols : 2 * cols, at : at + count] = joined[2 * cols :].astype(bf16)
    kv_ref[2 * cols :, :STRETCH] = jnp.broadcast_to(table, (16, STRETCH)).astype(bf16)


def prepare(gain, shift, weight, bias, x_all, count):
    width = weight.shape[0]
    cols = weight.shape[1] // 3
    rows = count * len(x_all)
    halfway = ROT // 2
    freqs = jnp.asarray(10000.0 ** (-np.arange(halfway) * 2.0 / ROT), f32)[:, None]
    return pl.pallas_call(
        prepare_kernel,
        out_shape=[
            jax.ShapeDtypeStruct((rows, width), bf16),
            jax.ShapeDtypeStruct((cols, rows), bf16),
            jax.ShapeDtypeStruct((2 * cols + 16, rows), bf16),
            jax.ShapeDtypeStruct((ROT // 2, rows), f32),
            jax.ShapeDtypeStruct((ROT // 2, rows), f32),
        ],
        compiler_params=pltpu.CompilerParams(vmem_limit_bytes=40 * 2**20),
        cost_estimate=pl.CostEstimate(
            flops=6 * cols * rows * width, bytes_accessed=8 * rows * width, transcendentals=0
        ),
        name="prepare",
    )(freqs, gain[None], shift[None], weight, bias[None], *x_all)


def rotate(heads, cosine, sine):
    halfway = ROT // 2
    first = heads[:, :halfway]
    second = heads[:, halfway:ROT]
    return jnp.concatenate(
        [first * cosine - second * sine, second * cosine + first * sine, heads[:, ROT:]], 1
    )


def around(values):
    return [values] + [swap(values, "ulysses", j) for j in range(1, lax.axis_size("ulysses"))]


def stacked_terms(lists):
    return [jnp.stack(v) for v in zip(*lists)]


def to_tokens(values):
    groups = lax.axis_size("ulysses")
    count = values.shape[1] // groups
    pieces = [values[:, j * count : (j + 1) * count] for j in range(groups)]
    return [pieces[0]] + [swap(pieces[j], "ulysses", j) for j in range(1, groups)]


def units_of(up_weight, side):
    units = up_weight.shape[1] // 2
    return jnp.where(side == 0, up_weight[:, :units], up_weight[:, units:])


def mlp_pair(x_both, e_both, gain, shift, up, up_bias, down_weight, *meanwhile):
    side = lax.axis_index("fsdp")
    rows, width = x_both.shape[0] // 2, x_both.shape[1]
    units = up.shape[1]
    normed = layer_norm(x_both.astype(f32), gain, shift).astype(bf16)
    hidden = jnp.dot(normed, up, preferred_element_type=f32) + up_bias.astype(f32)
    active_f, pull_gelu = jax.vjp(gelu_exact, hidden)
    active = active_f.astype(bf16)
    part = jnp.dot(active, down_weight, preferred_element_type=f32)
    d_active = jnp.einsum("td,fd->tf", e_both, down_weight, preferred_element_type=f32)
    d_hidden = pull_gelu(d_active)[0].astype(bf16)
    g_up_bias = jnp.sum(d_hidden.astype(f32), 0)
    d_part = jnp.einsum("tf,df->td", d_hidden, up, preferred_element_type=f32)
    sent = jnp.concatenate([part[rows:], d_part[rows:]]).astype(bf16)
    active, d_hidden = after((active, d_hidden), *meanwhile)
    g_up = jnp.einsum(
        "td,tcf->cdf", normed, d_hidden.reshape(2 * rows, 2, units // 2), preferred_element_type=f32
    ).astype(bf16)
    g_down = jnp.einsum("tf,td->fd", active, e_both, preferred_element_type=f32).astype(bf16)
    g_down = g_down.reshape(2, units // 2, width)
    pieces = jnp.stack([g_up, g_down], 1).reshape(2, 2, 2, width // 2, width)
    first = add_half((pieces[0], pieces[1]), "blk", 1)
    got = swap(after(sent, first), "fsdp", 1).astype(f32)
    out, d_normed = part[:rows] + got[:rows], d_part[:rows] + got[rows:]
    sums = add_half(halves_of(first, 2), "ulysses", 1)
    side, none = lax.axis_index("fsdp"), jnp.zeros_like(g_up_bias)
    g_up_bias = jnp.concatenate([jnp.where(side == 0, g_up_bias, none), jnp.where(side == 0, none, g_up_bias)])
    return out, d_normed, first, sums, g_up_bias


def finish_pair(sums, earlier, later):
    side = lax.axis_index("fsdp")
    sums = add_half(halves_of(after(sums, earlier), 2), "blk", 2)
    sums = add_half(halves_of(after(sums, later), 2), "ulysses", 2)
    got = swap(jnp.where(side == 0, sums[0, 1], sums[0, 0]), "fsdp", 1)
    kept = jnp.where(side == 0, sums[0, 0], sums[0, 1])
    sums = jnp.concatenate([in_order(side, kept[None], got[None]), sums[1]], 0)
    return share_half(sums, "ulysses", 2, 1)


def spread_pair(sums):
    kinds, rows, width = sums.shape
    sums = share_half(sums[:, None], "ulysses", 1, 1)
    sums = share_half(sums[:, :, None], "blk", 2, 2).reshape(kinds, 4 * rows, width)
    return place_mlp(bit_of("blk", 1), sums, swap(sums, "blk", 1))


def place_mlp_kernel(which, mine, other, up_ref, down_ref):
    width = mine.shape[-1]
    for c, ref in ((which[0], mine), (1 - which[0], other)):
        for f in range(2):
            at = pl.multiple_of((2 * f + c) * width, STRETCH)
            up_ref[:, pl.ds(at, width)] = ref[f].astype(f32)
            down_ref[c, f] = ref[2 + f].astype(f32)


def place_mlp(which, mine, other):
    _, rows, width = mine.shape
    step = rows // 4
    whole = pl.BlockSpec((4, step, width), lambda i, *_: (0, i, 0))
    up, down = pl.pallas_call(
        place_mlp_kernel,
        grid_spec=pltpu.PrefetchScalarGridSpec(
            num_scalar_prefetch=1,
            grid=(4,),
            in_specs=[whole, whole],
            out_specs=[
                pl.BlockSpec((step, 4 * width), lambda i, *_: (i, 0)),
                pl.BlockSpec((2, 2, step, width), lambda i, *_: (0, 0, i, 0)),
            ],
        ),
        out_shape=[
            jax.ShapeDtypeStruct((rows, 4 * width), f32),
            jax.ShapeDtypeStruct((2, 2, rows, width), f32),
        ],
        compiler_params=pltpu.CompilerParams(vmem_limit_bytes=32 * 2**20),
        cost_estimate=pl.CostEstimate(flops=0, bytes_accessed=12 * mine.size, transcendentals=0),
        name="place_mlp",
    )(which[None], mine, other)
    return up, down.reshape(4 * rows, width)


def place_qkv_kernel(which, mine, other, qkv_ref, out_ref):
    first = which[0] == 0
    rows, half = mine.shape[1:]
    width = 2 * half
    groups = mine.shape[0] // 4
    for t in range(3):
        blocks = []
        for z in range(groups):
            a, b = mine[3 * z + t], other[3 * z + t]
            blocks += [jnp.where(first, a, b), jnp.where(first, b, a)]
        qkv_ref[:, t * width : (t + 1) * width] = jnp.concatenate(blocks, 0).astype(f32).T
    for z in range(groups // 2):
        for side in range(2):
            a, b = mine[3 * groups + 2 * z + side], other[3 * groups + 2 * z + side]
            at = 2 * z * rows
            both = jnp.concatenate([jnp.where(first, a, b), jnp.where(first, b, a)], 0)
            out_ref[at : at + 2 * rows, side * half : (side + 1) * half] = both.astype(f32)


def place_qkv(which, mine, other):
    _, rows, half = mine.shape
    groups = mine.shape[0] // 4
    return pl.pallas_call(
        place_qkv_kernel,
        grid_spec=pltpu.PrefetchScalarGridSpec(
            num_scalar_prefetch=1,
            grid=(1,),
            in_specs=[pl.BlockSpec(v.shape, lambda i, *_: (0, 0, 0)) for v in (mine, other)],
            out_specs=[
                pl.BlockSpec((half, 6 * half), lambda i, *_: (0, 0)),
                pl.BlockSpec((groups * rows, 2 * half), lambda i, *_: (0, 0)),
            ],
        ),
        out_shape=[
            jax.ShapeDtypeStruct((half, 6 * half), f32),
            jax.ShapeDtypeStruct((groups * rows, 2 * half), f32),
        ],
        compiler_params=pltpu.CompilerParams(vmem_limit_bytes=40 * 2**20),
        cost_estimate=pl.CostEstimate(flops=0, bytes_accessed=12 * mine.size, transcendentals=0),
        name="place_qkv",
    )(which[None], mine, other)


def mlp_gathered(x, e, gain, shift, up, bias, down, *meanwhile):
    normed = layer_norm(x.astype(f32), gain, shift).astype(bf16)
    hidden = jnp.dot(normed, up, preferred_element_type=f32) + bias.astype(f32)
    active_f, pull_gelu = jax.vjp(gelu_exact, hidden)
    active = active_f.astype(bf16)
    out = jnp.dot(active, down, preferred_element_type=f32)
    g_down = jnp.einsum("tf,td->fd", active, e, preferred_element_type=f32)
    d_active = jnp.einsum("td,fd->tf", e, down, preferred_element_type=f32)
    d_hidden = pull_gelu(d_active)[0].astype(bf16)
    g_up = jnp.einsum("td,tf->df", normed, d_hidden, preferred_element_type=f32)
    d_normed = jnp.einsum("tf,df->td", d_hidden, up, preferred_element_type=f32)
    g_up, g_down = (
        lax.psum(
            lax.psum_scatter(g.astype(bf16), "fsdp", scatter_dimension=0, tiled=True),
            ("blk", "ulysses"),
        ).astype(f32)
        for g in (g_up, g_down)
    )
    return out, d_normed, d_hidden, (g_up, g_down), jnp.sum(d_hidden.astype(f32), 0)


def add_blks(grads):
    if lax.axis_size("fsdp") != 2:
        return lax.psum(grads, "blk")
    return add_half(halves_of(add_half(halves_of(grads, 1), "blk", 1), 1), "blk", 2)


def attention_grads(grads, vector, output, g_up):
    side = lax.axis_index("fsdp")
    group = lax.axis_index("ulysses")
    groups = lax.axis_size("ulysses")
    _, rows, width = grads.shape
    if lax.axis_size("fsdp") != 2:
        total = lax.all_gather(lax.psum(grads, "fsdp"), "ulysses", axis=1, tiled=True)
        part = width // lax.axis_size("fsdp")
        g_qkv = lax.dynamic_slice_in_dim(total[:3], side * part, part, 2)
        g_out = lax.dynamic_slice_in_dim(total[3], side * part, part, 0)
        g_qkv = g_qkv.reshape(3 * width, part).T.astype(f32)
        return g_qkv, g_out.astype(f32), sum_everywhere(vector)
    half = width // 2
    size = vector.shape[0]
    small = jnp.pad(vector.astype(bf16), (0, rows * half - size)).reshape(1, rows, half)
    low, high = grads[:, :, :half], grads[:, :, half:]
    kept = jnp.where(side == 0, low[:3], high[:3])
    sent = jnp.where(side == 0, high[:3], low[:3])
    whole = jnp.stack([low[3], high[3]])
    kept = jnp.concatenate([kept, whole, small])
    got = swap(jnp.concatenate([sent, whole, small]), "fsdp", 1)
    kept = (kept.astype(f32) + got.astype(f32)).astype(bf16)
    kept = by_device(around(kept), group)
    small = sum(v[5:].astype(f32) for v in kept).astype(bf16)
    of_qkv = jnp.concatenate([v[:3] for v in kept])
    of_out = [jnp.where(side == 0, a[3:5], b[3:5]) for a, b in zip(kept[: groups // 2], kept[groups // 2 :])]
    kept = jnp.concatenate([of_qkv] + of_out)
    units = kept.shape[0]
    got = after(swap(jnp.concatenate([kept, small]), "blk", 2), output)
    kept = in_order(bit_of("blk", 2), kept, got[:units], 1)
    small = (small.astype(f32) + got[units:].astype(f32)).astype(bf16)
    wide = jnp.pad(small, ((0, 0), (0, rows), (0, 0)))
    got = after(swap(jnp.concatenate([kept, wide]), "blk", 1), g_up)
    small = small.astype(f32) + got[units:, :rows].astype(f32)
    g_qkv, g_out = place_qkv(bit_of("blk", 1), kept, got)
    return g_qkv, g_out, small.reshape(-1)[:size]


def sum_everywhere(values):
    for axis in ("blk", "ulysses", "fsdp"):
        step = 1
        while step < lax.axis_size(axis):
            values = values + swap(values, axis, step)
            step *= 2
    return values


def on_device(
    tokens,
    positions,
    cotangent,
    ln1_gain,
    ln1_bias,
    ln2_gain,
    ln2_bias,
    qkv_weight,
    qkv_bias,
    out_weight,
    out_bias,
    up_weight,
    up_bias,
    down_weight,
    down_bias,
):
    count, width = tokens.shape
    groups = lax.axis_size("ulysses")
    group = lax.axis_index("ulysses")
    shards = lax.axis_size("fsdp")
    cols = width // groups
    heads = cols // HEAD
    rows = count * groups

    ranks = (positions[::STRETCH] // STRETCH).astype(bf16)[None]
    ranks = jnp.pad(ranks, ((0, 15), (0, width - ranks.shape[1])))
    x_ranks = jnp.concatenate([tokens, ranks])
    if shards == 2:
        side = lax.axis_index("fsdp")
        part_qkv = swap(quarter_of(qkv_weight), "fsdp", 1)
        half_up = jnp.concatenate([units_of(up_weight, 1 - side), out_weight], 1)
        part_up = swap(after(quarter_of(half_up), part_qkv), "fsdp", 1)
        x_e = swap(after(jnp.stack([tokens, cotangent]), part_up), "fsdp", 1)
        half_qkv = share_half(part_qkv, "blk", 2, 0)
        w_qkv = both_shards(qkv_weight, half_qkv)
        half_up = share_half(after(part_up, half_qkv), "blk", 2, 0)
        x_all = around(x_ranks)
        mine = jnp.concatenate([units_of(up_weight, side), out_weight], 1)
        half_up = both_shards(mine, after(half_up, w_qkv))
        w_up, w_out = half_up[:, :-width], half_up[:, -width:]
        x_mlp = jnp.concatenate([tokens, x_e[0]])
        e_mlp = jnp.concatenate([cotangent, x_e[1]])
        b_up, w_down = up_bias, down_weight
        mlp, finish, spread = mlp_pair, finish_pair, spread_pair
    else:
        x_all, part_qkv = around(x_ranks), x_ranks
        w_qkv, w_up, w_out, w_down = (
            lax.all_gather(w, "fsdp", axis=0, tiled=True)
            for w in (qkv_weight, up_weight, out_weight, down_weight)
        )
        b_up = gather_small(up_bias).reshape(-1)
        x_mlp, e_mlp = tokens, cotangent
        mlp, finish, spread = mlp_gathered, lambda v, *_: v, lambda v: v
    small = jnp.concatenate([ln1_gain, ln1_bias, ln2_gain, ln2_bias, out_bias, down_bias, qkv_bias])
    small = gather_small(after(small, part_qkv))
    part = width // shards
    ln1_g, ln1_b, ln2_g, ln2_b, b_out, b_down = (
        small[:, i * part : (i + 1) * part].reshape(width).astype(f32) for i in range(6)
    )
    b_qkv = small[:, 6 * part :].reshape(3 * width).astype(f32)
    starts = [i * width + group * cols for i in range(3)]
    w_mine = jnp.concatenate([lax.dynamic_slice_in_dim(w_qkv, v, cols, 1) for v in starts], 1)
    b_mine = jnp.concatenate([lax.dynamic_slice_in_dim(b_qkv, v, cols, 0) for v in starts])
    x_all = after(x_all, w_mine)
    normed, queries, kv, cosine, sine = prepare(ln1_g, ln1_b, w_mine, b_mine, x_all, count)
    queries = queries.reshape(heads, HEAD, rows)
    pieces = {0: kv}
    step = lax.axis_size("blk") // 2
    while step >= 1:
        for i in list(pieces):
            pieces[i ^ step] = swap(pieces[i], "blk", step)
        step //= 2
    kv_all = [pieces[i] for i in range(len(pieces))]
    ranks = jnp.concatenate([v[2 * cols, : rows // STRETCH] for v in kv_all]).astype(jnp.int32)

    d_mixed = jnp.einsum("ed,td->et", w_out, after(cotangent, kv), preferred_element_type=f32).astype(bf16)
    d_heads = [lax.dynamic_slice_in_dim(d_mixed, (group ^ j) * cols, cols) for j in range(groups)]
    d_heads = [d_heads[0]] + [swap(d_heads[j], "ulysses", j) for j in range(1, groups)]
    d_heads = jnp.concatenate(d_heads, 1).reshape(heads, HEAD, rows)

    x_mlp, w_up = after((x_mlp, w_up), kv, d_mixed)
    mlp_out, d_norm_two, begun, terms, g_up_bias = mlp(
        x_mlp, e_mlp, ln2_g, ln2_b, w_up, b_up, w_down, pieces[lax.axis_size("blk") // 2], pieces[1], d_heads
    )

    e_around = around(after(cotangent, begun))
    d_heads = after(d_heads, begun)
    mixed, d_q, kept, sent = attend(ranks, queries, d_heads, kv_all)

    sent, e_around, terms, mlp_out, d_norm_two = after((sent, e_around, terms, mlp_out, d_norm_two))
    got = swap(sent, "blk", 1)
    step, kept = 1, [[kept[i], got[i]] for i in range(kept.shape[0])]
    while len(kept) > 1:
        step *= 2
        sent = sum(v.astype(f32) for v in stacked_terms(kept[1::2])).astype(bf16)
        got = swap(sent, "blk", step)
        kept = [kept[2 * i] + [got[i]] for i in range(got.shape[0])]
    total = sum(v.astype(f32) for v in kept[0])
    d_q = rotate(d_q, cosine, -sine).astype(bf16).reshape(cols, rows)
    mixed = mixed.reshape(cols, rows)
    back_q = to_tokens(jnp.concatenate([d_q, mixed]))
    terms = finish(terms, sent, back_q)
    e_all = jnp.concatenate(e_around, 0)
    g_out = jnp.dot(mixed, e_all, preferred_element_type=f32).astype(bf16)
    d_k = rotate(total[:cols].reshape(heads, HEAD, rows), cosine, -sine).reshape(cols, rows)
    d_kv = jnp.concatenate([d_k, total[cols:]]).astype(bf16)
    d_joined = jnp.concatenate([d_q, d_kv])
    g_bias_mine = jnp.sum(d_joined.astype(f32), 1)
    g_qkv = jnp.dot(d_joined, normed, preferred_element_type=f32).astype(bf16)
    back_kv = to_tokens(d_kv)
    grads = jnp.concatenate([g_qkv.reshape(3, cols, width), g_out[None]])
    grads = add_blks(grads)
    back_kv = after(back_kv, grads, terms)
    g_up, g_down = spread(terms)
    back_q, back_kv = by_device(back_q, group), by_device(back_kv, group)
    d_mine = jnp.concatenate(
        [v[:cols] for v in back_q] + [v[:cols] for v in back_kv] + [v[cols:] for v in back_kv], 0
    )
    d_norm_one = jnp.einsum("et,de->td", d_mine, w_qkv, preferred_element_type=f32)
    x_float = tokens.astype(f32)
    _, pull_one = jax.vjp(layer_norm, x_float, ln1_g, ln1_b)
    _, pull_two = jax.vjp(layer_norm, x_float, ln2_g, ln2_b)
    d_x_one, g_ln1_g, g_ln1_b = pull_one(d_norm_one)
    d_x_two, g_ln2_g, g_ln2_b = pull_two(d_norm_two)
    e_float = cotangent.astype(f32)

    g_qkv_bias = jnp.zeros((3, groups, cols), f32)
    g_qkv_bias = lax.dynamic_update_slice(g_qkv_bias, g_bias_mine.reshape(3, 1, cols), (0, group, 0))
    vectors = [g_ln1_g, g_ln1_b, g_ln2_g, g_ln2_b, jnp.sum(e_float, 0), g_qkv_bias.reshape(-1), g_up_bias]
    back = jnp.concatenate([v[cols:] for v in back_q], 0)
    attn_out = jnp.einsum("et,ed->td", back, w_out, preferred_element_type=f32)
    output = (x_float + (attn_out + b_out) + (mlp_out + b_down)).astype(bf16)
    input_grad = (e_float + d_x_one + d_x_two).astype(bf16)

    g_qkv, g_out, summed = attention_grads(grads, jnp.concatenate(vectors), output, g_up)
    results, start = [], 0
    for vector in vectors:
        mine = vector.shape[0] // shards
        results.append(lax.dynamic_slice_in_dim(summed, start + lax.axis_index("fsdp") * mine, mine))
        start += vector.shape[0]
    g_ln1_g, g_ln1_b, g_ln2_g, g_ln2_b, g_e, g_qkv_bias, g_up_bias = results
    return (
        output,
        input_grad,
        g_ln1_g,
        g_ln1_b,
        g_ln2_g,
        g_ln2_b,
        g_qkv,
        g_qkv_bias,
        g_out,
        g_e,
        g_up,
        g_up_bias,
        g_down,
        g_e,
    )


def solution(mesh):
    rows = P(("fsdp", "blk", "ulysses"), None)
    split, matrix = P("fsdp"), P("fsdp", None)
    return jax.shard_map(
        on_device,
        mesh=mesh,
        in_specs=(
            rows,
            P(("fsdp", "blk", "ulysses")),
            rows,
            split,
            split,
            split,
            split,
            matrix,
            split,
            matrix,
            split,
            matrix,
            split,
            matrix,
            split,
        ),
        out_specs=(
            rows,
            rows,
            split,
            split,
            split,
            split,
            matrix,
            split,
            matrix,
            split,
            matrix,
            split,
            matrix,
            split,
        ),
        check_vma=False,
    )
```

```python
import jax
import jax.numpy as jnp
import numpy as np
from jax import lax
from jax.experimental import pallas as pl
from jax.experimental.pallas import tpu as pltpu
from jax.sharding import PartitionSpec as P

HEAD = 64
ROT = 16
STRETCH = 128
CHUNK = 8
BIG_NEG = -1e30

f32 = jnp.float32
bf16 = jnp.bfloat16


def layer_norm(values, gain, shift):
    center = jnp.mean(values, -1, keepdims=True)
    offset = values - center
    spread = jnp.mean(offset * offset, -1, keepdims=True)
    return offset * lax.rsqrt(spread + 1e-05) * gain + shift


def gelu_exact(values):
    return jax.nn.gelu(values, approximate=False)


def swap(values, axis, bits):
    count = lax.axis_size(axis)
    return lax.ppermute(values, axis, [(i, i ^ bits) for i in range(count)])


def after(values, *earlier):
    return lax.optimization_barrier((values, earlier))[0]


def bit_of(axis, bit):
    return (lax.axis_index(axis) // bit) % 2


def in_order(bit, mine, other, axis=0):
    return jnp.concatenate([jnp.where(bit == 0, mine, other), jnp.where(bit == 0, other, mine)], axis)


def by_device(pieces, index):
    step = 1
    while step < len(pieces):
        odd = (index // step) % 2 == 1
        pieces = [jnp.where(odd, pieces[i ^ step], pieces[i]) for i in range(len(pieces))]
        step *= 2
    return pieces


def add_half(halves, axis, bit):
    which = bit_of(axis, bit)
    got = swap(jnp.where(which == 0, halves[1], halves[0]), axis, bit)
    kept = jnp.where(which == 0, halves[0], halves[1])
    return (kept.astype(f32) + got.astype(f32)).astype(bf16)


def halves_of(values, axis):
    half = values.shape[axis] // 2
    return (
        lax.slice_in_dim(values, 0, half, axis=axis),
        lax.slice_in_dim(values, half, 2 * half, axis=axis),
    )


def share_half(values, axis, bit, dim):
    return in_order(bit_of(axis, bit), values, swap(values, axis, bit), dim)


def gather_small(shard):
    if lax.axis_size("fsdp") != 2:
        return lax.all_gather(shard[None], "fsdp", axis=0, tiled=True)
    return in_order(lax.axis_index("fsdp"), shard[None], swap(shard[None], "fsdp", 1))


def quarter_of(shard):
    quarter = shard.shape[0] // 4
    place = bit_of("blk", 1) * 2 + bit_of("blk", 2)
    return lax.dynamic_slice_in_dim(shard, place * quarter, quarter)


def both_shards(shard, half):
    return in_order(lax.axis_index("fsdp"), shard, share_half(half, "blk", 1, 0))


def attend_kernel(rank, q_ref, g_ref, *refs):
    kv_refs = refs[:-9]
    o_ref, dq_ref, keep_ref, send_ref, rows, lanes, sums, probs, order = refs[-9:]
    heads = range(q_ref.shape[0])
    cols = q_ref.shape[0] * HEAD
    n_keys = rank.shape[0]
    own = q_ref.shape[-1] // STRETCH
    wide = 2 * STRETCH
    span = CHUNK * STRETCH

    for t in range(n_keys):
        i, at = t // own, (t % own) * STRETCH
        place = rank[t]
        for h in heads:
            both = jnp.concatenate(
                [
                    kv_refs[i][first : first + HEAD, at : at + STRETCH]
                    for first in (h * HEAD, cols + h * HEAD)
                ],
                0,
            )
            lanes[h, place] = both
            rows[h, place] = both.T
            sums[h, t] = jnp.zeros((STRETCH, 2 * HEAD), f32)
    for a in range(own):
        before = jnp.int32(0)
        for b in range(own):
            before += (rank[b] < rank[a]).astype(jnp.int32)
        order[before] = a

    def side(h, j, part):
        first = part * HEAD
        return jnp.concatenate(
            [lanes[h, j * CHUNK + i, first : first + HEAD, :] for i in range(CHUNK)], 1
        )

    def keys(h, j):
        return rows[h, pl.ds(j * CHUNK, CHUNK)].reshape(span, 2 * HEAD)

    def pair(p, carry):
        a, b = order[2 * p], order[2 * p + 1]
        ra, rb = rank[a], rank[b]
        at_a = pl.ds(pl.multiple_of(a * STRETCH, STRETCH), STRETCH)
        at_b = pl.ds(pl.multiple_of(b * STRETCH, STRETCH), STRETCH)
        q = [jnp.concatenate([q_ref[h, :, at_a], q_ref[h, :, at_b]], 1) for h in heads]
        g = [jnp.concatenate([g_ref[h, :, at_a], g_ref[h, :, at_b]], 1) for h in heads]
        none = jnp.zeros_like(q[0])
        q_low = [jnp.concatenate([v, none], 0) for v in q]
        g_high = [jnp.concatenate([none, v], 0) for v in g]
        lane = lax.broadcasted_iota(jnp.int32, (1, wide), 1)
        q_place = jnp.where(lane < STRETCH, ra * STRETCH + lane, rb * STRETCH + lane - STRETCH)
        clear = ra // CHUNK
        total = (rb + CHUNK) // CHUNK

        def score(j, tops, masked):
            result = []
            for h in heads:
                s = jnp.dot(keys(h, j), q_low[h], preferred_element_type=f32)
                if masked:
                    k_place = j * span + lax.broadcasted_iota(jnp.int32, (span, 1), 0)
                    s = jnp.where(k_place <= q_place, s, BIG_NEG)
                probs[h, j] = s
                result.append(jnp.maximum(tops[h], jnp.max(s.reshape(span // 8, 8, wide), 0)))
            return tuple(result)

        tops = tuple(jnp.full((8, wide), BIG_NEG, f32) for _ in heads)
        tops = lax.fori_loop(0, clear, lambda j, v: score(j, v, False), tops)
        tops = lax.fori_loop(clear, total, lambda j, v: score(j, v, True), tops)
        tops = [jnp.max(v, 0, keepdims=True) for v in tops]

        def weigh(j, state):
            result = []
            for h in heads:
                count, out = state[h]
                weight = jnp.exp(probs[h, j] - tops[h])
                probs[h, j] = weight
                count = count + jnp.sum(weight.reshape(span // 8, 8, wide), 0)
                out = out + jnp.dot(side(h, j, 1), weight.astype(bf16), preferred_element_type=f32)
                result.append((count, out))
            return tuple(result)

        state = tuple((jnp.zeros((8, wide), f32), jnp.zeros((HEAD, wide), f32)) for _ in heads)
        state = lax.fori_loop(0, total, weigh, state)
        inverse, delta, right = [], [], []
        for h in heads:
            count, out = state[h]
            inverse.append(1.0 / jnp.sum(count, 0, keepdims=True))
            out = out * inverse[h]
            delta.append(jnp.sum(out * g[h].astype(f32), 0, keepdims=True))
            o_ref[h, :, at_a] = out[:, :STRETCH].astype(bf16)
            o_ref[h, :, at_b] = out[:, STRETCH:].astype(bf16)
            top = jnp.concatenate([g[h], none], 0).T
            right.append(jnp.concatenate([top, jnp.concatenate([none, q[h]], 0).T], 0))

        def back(j, d_q):
            result = []
            for h in heads:
                weight = probs[h, j] * inverse[h]
                d_weight = jnp.dot(keys(h, j), g_high[h], preferred_element_type=f32)
                d_score = (weight * (d_weight - delta[h])).astype(bf16)
                left = jnp.concatenate([weight.astype(bf16), d_score], 1)
                sums[h, pl.ds(j * CHUNK, CHUNK)] += jnp.dot(
                    left, right[h], preferred_element_type=f32
                ).reshape(CHUNK, STRETCH, 2 * HEAD)
                result.append(d_q[h] + jnp.dot(side(h, j, 0), d_score, preferred_element_type=f32))
            return tuple(result)

        d_q = lax.fori_loop(0, total, back, tuple(jnp.zeros((HEAD, wide), f32) for _ in heads))
        for h in heads:
            scaled = d_q[h] * HEAD ** (-0.5)
            dq_ref[h, :, at_a] = scaled[:, :STRETCH]
            dq_ref[h, :, at_b] = scaled[:, STRETCH:]
        return carry

    lax.fori_loop(0, own // 2, pair, 0)
    for t in range(n_keys):
        i, at = t // own, (t % own) * STRETCH
        to = keep_ref if i % 2 == 0 else send_ref
        for h in heads:
            turned = sums[h, rank[t]].astype(bf16).T
            first = h * HEAD
            to[i // 2, cols + first : cols + first + HEAD, at : at + STRETCH] = turned[:HEAD]
            to[i // 2, first : first + HEAD, at : at + STRETCH] = turned[HEAD:]


def attend(ranks, q, g, kv):
    heads, _, count = q.shape
    devices = len(kv)
    n_keys = devices * count // STRETCH
    pairs = heads * 4 * HEAD * count * count * devices
    half = (devices // 2, 2 * heads * HEAD, count)
    q_spec = pl.BlockSpec(q.shape, lambda i, *_: (0, 0, 0))
    half_spec = pl.BlockSpec(half, lambda i, *_: (0, 0, 0))
    return pl.pallas_call(
        attend_kernel,
        grid_spec=pltpu.PrefetchScalarGridSpec(
            num_scalar_prefetch=1,
            grid=(1,),
            in_specs=[q_spec, q_spec] + [pl.BlockSpec(v.shape, lambda i, *_: (0, 0)) for v in kv],
            out_specs=[q_spec, q_spec, half_spec, half_spec],
            scratch_shapes=[
                pltpu.VMEM((heads, n_keys, STRETCH, 2 * HEAD), bf16),
                pltpu.VMEM((heads, n_keys, 2 * HEAD, STRETCH), bf16),
                pltpu.VMEM((heads, n_keys, STRETCH, 2 * HEAD), f32),
                pltpu.VMEM((heads, n_keys // CHUNK, CHUNK * STRETCH, 2 * STRETCH), f32),
                pltpu.SMEM((count // STRETCH,), jnp.int32),
            ],
        ),
        out_shape=[
            jax.ShapeDtypeStruct(q.shape, bf16),
            jax.ShapeDtypeStruct(q.shape, f32),
            jax.ShapeDtypeStruct(half, bf16),
            jax.ShapeDtypeStruct(half, bf16),
        ],
        compiler_params=pltpu.CompilerParams(vmem_limit_bytes=56 * 2**20),
        cost_estimate=pl.CostEstimate(
            flops=12 * pairs, bytes_accessed=16 * q.size * devices, transcendentals=pairs // 512
        ),
        name="attend",
    )(ranks, q, g, *kv)


def prepare_kernel(freqs, gain, shift, weight, bias, *refs):
    groups = len(refs) - 5
    x_refs = refs[:groups]
    normed_ref, q_ref, kv_ref, cos_ref, sin_ref = refs[groups:]
    count = normed_ref.shape[0] // groups
    cols = q_ref.shape[0]
    halfway = ROT // 2
    blocks = count // STRETCH
    lane = lax.broadcasted_iota(jnp.int32, (1, STRETCH), 1).astype(f32)
    kv_ref[2 * cols :, :] = jnp.zeros((kv_ref.shape[0] - 2 * cols, kv_ref.shape[1]), bf16)
    spots = lax.broadcasted_iota(jnp.int32, (1, STRETCH), 1)
    table = jnp.zeros((1, STRETCH), f32)
    for i, x_ref in enumerate(x_refs):
        at = i * count
        normed = layer_norm(x_ref[:count].astype(f32), gain[...], shift[...]).astype(bf16)
        normed_ref[at : at + count] = normed
        joined = jnp.dot(normed, weight[...], preferred_element_type=f32) + bias[...]
        joined = joined.T
        ranks = x_ref[count : count + 16, :STRETCH].astype(f32)[:1]
        places = []
        for b in range(blocks):
            rank = jnp.sum(jnp.where(spots == b, ranks, 0.0), 1, keepdims=True)
            places.append(rank * STRETCH + lane)
            table = jnp.where(spots == i * blocks + b, rank, table)
        angles = freqs[...] * jnp.concatenate(places, 1)
        cosine, sine = jnp.cos(angles), jnp.sin(angles)
        cos_ref[:, at : at + count] = cosine
        sin_ref[:, at : at + count] = sine
        for to, first, scale in ((q_ref, 0, HEAD ** (-0.5)), (kv_ref, cols, 1.0)):
            for h in range(cols // HEAD):
                low = first + h * HEAD
                one = joined[low : low + halfway]
                two = joined[low + halfway : low + ROT]
                rest = joined[low + ROT : low + HEAD]
                turned = jnp.concatenate(
                    [one * cosine - two * sine, two * cosine + one * sine, rest], 0
                ).astype(bf16)
                to[h * HEAD : (h + 1) * HEAD, at : at + count] = turned * jnp.bfloat16(scale)
        kv_ref[cols : 2 * cols, at : at + count] = joined[2 * cols :].astype(bf16)
    kv_ref[2 * cols :, :STRETCH] = jnp.broadcast_to(table, (16, STRETCH)).astype(bf16)


def prepare(gain, shift, weight, bias, x_all, count):
    width = weight.shape[0]
    cols = weight.shape[1] // 3
    rows = count * len(x_all)
    halfway = ROT // 2
    freqs = jnp.asarray(10000.0 ** (-np.arange(halfway) * 2.0 / ROT), f32)[:, None]
    return pl.pallas_call(
        prepare_kernel,
        out_shape=[
            jax.ShapeDtypeStruct((rows, width), bf16),
            jax.ShapeDtypeStruct((cols, rows), bf16),
            jax.ShapeDtypeStruct((2 * cols + 16, rows), bf16),
            jax.ShapeDtypeStruct((ROT // 2, rows), f32),
            jax.ShapeDtypeStruct((ROT // 2, rows), f32),
        ],
        compiler_params=pltpu.CompilerParams(vmem_limit_bytes=40 * 2**20),
        cost_estimate=pl.CostEstimate(
            flops=6 * cols * rows * width, bytes_accessed=8 * rows * width, transcendentals=0
        ),
        name="prepare",
    )(freqs, gain[None], shift[None], weight, bias[None], *x_all)


def rotate(heads, cosine, sine):
    halfway = ROT // 2
    first = heads[:, :halfway]
    second = heads[:, halfway:ROT]
    return jnp.concatenate(
        [first * cosine - second * sine, second * cosine + first * sine, heads[:, ROT:]], 1
    )


def around(values):
    return [values] + [swap(values, "ulysses", j) for j in range(1, lax.axis_size("ulysses"))]


def stacked_terms(lists):
    return [jnp.stack(v) for v in zip(*lists)]


def to_tokens(values):
    groups = lax.axis_size("ulysses")
    count = values.shape[1] // groups
    pieces = [values[:, j * count : (j + 1) * count] for j in range(groups)]
    return [pieces[0]] + [swap(pieces[j], "ulysses", j) for j in range(1, groups)]


def units_of(up_weight, side):
    units = up_weight.shape[1] // 2
    return jnp.where(side == 0, up_weight[:, :units], up_weight[:, units:])


def mlp_pair(x_both, e_both, gain, shift, up, up_bias, down_weight, *meanwhile):
    side = lax.axis_index("fsdp")
    rows, width = x_both.shape[0] // 2, x_both.shape[1]
    units = up.shape[1]
    normed = layer_norm(x_both.astype(f32), gain, shift).astype(bf16)
    hidden = jnp.dot(normed, up, preferred_element_type=f32) + up_bias.astype(f32)
    active_f, pull_gelu = jax.vjp(gelu_exact, hidden)
    active = active_f.astype(bf16)
    part = jnp.dot(active, down_weight, preferred_element_type=f32)
    d_active = jnp.einsum("td,fd->tf", e_both, down_weight, preferred_element_type=f32)
    d_hidden = pull_gelu(d_active)[0].astype(bf16)
    g_up_bias = jnp.sum(d_hidden.astype(f32), 0)
    d_part = jnp.einsum("tf,df->td", d_hidden, up, preferred_element_type=f32)
    sent = jnp.concatenate([part[rows:], d_part[rows:]]).astype(bf16)
    active, d_hidden = after((active, d_hidden), *meanwhile)
    g_up = jnp.einsum(
        "td,tcf->cdf", normed, d_hidden.reshape(2 * rows, 2, units // 2), preferred_element_type=f32
    ).astype(bf16)
    g_down = jnp.einsum("tf,td->fd", active, e_both, preferred_element_type=f32).astype(bf16)
    g_down = g_down.reshape(2, units // 2, width)
    pieces = jnp.stack([g_up, g_down], 1).reshape(2, 2, 2, width // 2, width)
    first = add_half((pieces[0], pieces[1]), "blk", 1)
    got = swap(after(sent, first), "fsdp", 1).astype(f32)
    out, d_normed = part[:rows] + got[:rows], d_part[:rows] + got[rows:]
    sums = add_half(halves_of(first, 2), "blk", 2)
    side, none = lax.axis_index("fsdp"), jnp.zeros_like(g_up_bias)
    g_up_bias = jnp.concatenate([jnp.where(side == 0, g_up_bias, none), jnp.where(side == 0, none, g_up_bias)])
    return out, d_normed, first, sums, g_up_bias


def finish_pair(sums, earlier):
    side = lax.axis_index("fsdp")
    sums = after(sums, earlier)
    sums = add_half(halves_of(sums, 2), "ulysses", 1)
    sums = add_half(halves_of(sums, 2), "ulysses", 2)
    got = swap(jnp.where(side == 0, sums[0, 1], sums[0, 0]), "fsdp", 1)
    kept = jnp.where(side == 0, sums[0, 0], sums[0, 1])
    sums = jnp.concatenate([in_order(side, kept[None], got[None]), sums[1]], 0)
    sums = share_half(sums, "ulysses", 2, 1)
    sums = share_half(sums, "ulysses", 1, 1)
    sums = share_half(sums, "blk", 2, 1)
    return place_mlp(bit_of("blk", 1), sums, swap(sums, "blk", 1))


def place_mlp_kernel(which, mine, other, up_ref, down_ref):
    width = mine.shape[-1]
    for c, ref in ((which[0], mine), (1 - which[0], other)):
        for f in range(2):
            at = pl.multiple_of((2 * f + c) * width, STRETCH)
            up_ref[:, pl.ds(at, width)] = ref[f].astype(f32)
            down_ref[c, f] = ref[2 + f].astype(f32)


def place_mlp(which, mine, other):
    _, rows, width = mine.shape
    step = rows // 4
    whole = pl.BlockSpec((4, step, width), lambda i, *_: (0, i, 0))
    up, down = pl.pallas_call(
        place_mlp_kernel,
        grid_spec=pltpu.PrefetchScalarGridSpec(
            num_scalar_prefetch=1,
            grid=(4,),
            in_specs=[whole, whole],
            out_specs=[
                pl.BlockSpec((step, 4 * width), lambda i, *_: (i, 0)),
                pl.BlockSpec((2, 2, step, width), lambda i, *_: (0, 0, i, 0)),
            ],
        ),
        out_shape=[
            jax.ShapeDtypeStruct((rows, 4 * width), f32),
            jax.ShapeDtypeStruct((2, 2, rows, width), f32),
        ],
        compiler_params=pltpu.CompilerParams(vmem_limit_bytes=32 * 2**20),
        cost_estimate=pl.CostEstimate(flops=0, bytes_accessed=12 * mine.size, transcendentals=0),
        name="place_mlp",
    )(which[None], mine, other)
    return up, down.reshape(4 * rows, width)


def place_qkv_kernel(which, mine, other, qkv_ref, out_ref):
    first = which[0] == 0
    rows, half = mine.shape[1:]
    width = 2 * half
    groups = mine.shape[0] // 4
    for t in range(3):
        blocks = []
        for z in range(groups):
            a, b = mine[3 * z + t], other[3 * z + t]
            blocks += [jnp.where(first, a, b), jnp.where(first, b, a)]
        qkv_ref[:, t * width : (t + 1) * width] = jnp.concatenate(blocks, 0).astype(f32).T
    for z in range(groups // 2):
        for side in range(2):
            a, b = mine[3 * groups + 2 * z + side], other[3 * groups + 2 * z + side]
            at = 2 * z * rows
            both = jnp.concatenate([jnp.where(first, a, b), jnp.where(first, b, a)], 0)
            out_ref[at : at + 2 * rows, side * half : (side + 1) * half] = both.astype(f32)


def place_qkv(which, mine, other):
    _, rows, half = mine.shape
    groups = mine.shape[0] // 4
    return pl.pallas_call(
        place_qkv_kernel,
        grid_spec=pltpu.PrefetchScalarGridSpec(
            num_scalar_prefetch=1,
            grid=(1,),
            in_specs=[pl.BlockSpec(v.shape, lambda i, *_: (0, 0, 0)) for v in (mine, other)],
            out_specs=[
                pl.BlockSpec((half, 6 * half), lambda i, *_: (0, 0)),
                pl.BlockSpec((groups * rows, 2 * half), lambda i, *_: (0, 0)),
            ],
        ),
        out_shape=[
            jax.ShapeDtypeStruct((half, 6 * half), f32),
            jax.ShapeDtypeStruct((groups * rows, 2 * half), f32),
        ],
        compiler_params=pltpu.CompilerParams(vmem_limit_bytes=40 * 2**20),
        cost_estimate=pl.CostEstimate(flops=0, bytes_accessed=12 * mine.size, transcendentals=0),
        name="place_qkv",
    )(which[None], mine, other)


def mlp_gathered(x, e, gain, shift, up, bias, down, *meanwhile):
    normed = layer_norm(x.astype(f32), gain, shift).astype(bf16)
    hidden = jnp.dot(normed, up, preferred_element_type=f32) + bias.astype(f32)
    active_f, pull_gelu = jax.vjp(gelu_exact, hidden)
    active = active_f.astype(bf16)
    out = jnp.dot(active, down, preferred_element_type=f32)
    g_down = jnp.einsum("tf,td->fd", active, e, preferred_element_type=f32)
    d_active = jnp.einsum("td,fd->tf", e, down, preferred_element_type=f32)
    d_hidden = pull_gelu(d_active)[0].astype(bf16)
    g_up = jnp.einsum("td,tf->df", normed, d_hidden, preferred_element_type=f32)
    d_normed = jnp.einsum("tf,df->td", d_hidden, up, preferred_element_type=f32)
    g_up, g_down = (
        lax.psum(
            lax.psum_scatter(g.astype(bf16), "fsdp", scatter_dimension=0, tiled=True),
            ("blk", "ulysses"),
        ).astype(f32)
        for g in (g_up, g_down)
    )
    return out, d_normed, d_hidden, (g_up, g_down), jnp.sum(d_hidden.astype(f32), 0)


def add_blks(grads):
    if lax.axis_size("fsdp") != 2:
        return lax.psum(grads, "blk")
    return add_half(halves_of(add_half(halves_of(grads, 1), "blk", 1), 1), "blk", 2)


def attention_grads(grads, vector, output):
    side = lax.axis_index("fsdp")
    group = lax.axis_index("ulysses")
    groups = lax.axis_size("ulysses")
    _, rows, width = grads.shape
    if lax.axis_size("fsdp") != 2:
        total = lax.all_gather(lax.psum(grads, "fsdp"), "ulysses", axis=1, tiled=True)
        part = width // lax.axis_size("fsdp")
        g_qkv = lax.dynamic_slice_in_dim(total[:3], side * part, part, 2)
        g_out = lax.dynamic_slice_in_dim(total[3], side * part, part, 0)
        g_qkv = g_qkv.reshape(3 * width, part).T.astype(f32)
        return g_qkv, g_out.astype(f32), sum_everywhere(vector)
    half = width // 2
    size = vector.shape[0]
    small = jnp.pad(vector.astype(bf16), (0, rows * half - size)).reshape(1, rows, half)
    low, high = grads[:, :, :half], grads[:, :, half:]
    kept = jnp.where(side == 0, low[:3], high[:3])
    sent = jnp.where(side == 0, high[:3], low[:3])
    whole = jnp.stack([low[3], high[3]])
    kept = jnp.concatenate([kept, whole, small])
    got = swap(jnp.concatenate([sent, whole, small]), "fsdp", 1)
    kept = (kept.astype(f32) + got.astype(f32)).astype(bf16)
    kept = by_device(around(kept), group)
    small = sum(v[5:].astype(f32) for v in kept).astype(bf16)
    of_qkv = jnp.concatenate([v[:3] for v in kept])
    of_out = [jnp.where(side == 0, a[3:5], b[3:5]) for a, b in zip(kept[: groups // 2], kept[groups // 2 :])]
    kept = jnp.concatenate([of_qkv] + of_out)
    units = kept.shape[0]
    got = after(swap(jnp.concatenate([kept, small]), "blk", 2), output)
    kept = in_order(bit_of("blk", 2), kept, got[:units], 1)
    small = (small.astype(f32) + got[units:].astype(f32)).astype(bf16)
    wide = jnp.pad(small, ((0, 0), (0, rows), (0, 0)))
    got = swap(jnp.concatenate([kept, wide]), "blk", 1)
    small = small.astype(f32) + got[units:, :rows].astype(f32)
    g_qkv, g_out = place_qkv(bit_of("blk", 1), kept, got)
    return g_qkv, g_out, small.reshape(-1)[:size]


def sum_everywhere(values):
    for axis in ("blk", "ulysses", "fsdp"):
        step = 1
        while step < lax.axis_size(axis):
            values = values + swap(values, axis, step)
            step *= 2
    return values


def on_device(
    tokens,
    positions,
    cotangent,
    ln1_gain,
    ln1_bias,
    ln2_gain,
    ln2_bias,
    qkv_weight,
    qkv_bias,
    out_weight,
    out_bias,
    up_weight,
    up_bias,
    down_weight,
    down_bias,
):
    count, width = tokens.shape
    groups = lax.axis_size("ulysses")
    group = lax.axis_index("ulysses")
    shards = lax.axis_size("fsdp")
    cols = width // groups
    heads = cols // HEAD
    rows = count * groups

    ranks = (positions[::STRETCH] // STRETCH).astype(bf16)[None]
    ranks = jnp.pad(ranks, ((0, 15), (0, width - ranks.shape[1])))
    x_ranks = jnp.concatenate([tokens, ranks])
    if shards == 2:
        side = lax.axis_index("fsdp")
        part_qkv = swap(quarter_of(qkv_weight), "fsdp", 1)
        half_up = jnp.concatenate([units_of(up_weight, 1 - side), out_weight], 1)
        part_up = swap(after(quarter_of(half_up), part_qkv), "fsdp", 1)
        x_e = swap(after(jnp.stack([tokens, cotangent]), part_up), "fsdp", 1)
        w_qkv = both_shards(qkv_weight, share_half(part_qkv, "blk", 2, 0))
        half_up = share_half(part_up, "blk", 2, 0)
        x_all = around(x_ranks)
        mine = jnp.concatenate([units_of(up_weight, side), out_weight], 1)
        half_up = both_shards(mine, half_up)
        w_up, w_out = half_up[:, :-width], half_up[:, -width:]
        x_mlp = jnp.concatenate([tokens, x_e[0]])
        e_mlp = jnp.concatenate([cotangent, x_e[1]])
        b_up, w_down, mlp, finish = up_bias, down_weight, mlp_pair, finish_pair
    else:
        x_all, part_qkv = around(x_ranks), x_ranks
        w_qkv, w_up, w_out, w_down = (
            lax.all_gather(w, "fsdp", axis=0, tiled=True)
            for w in (qkv_weight, up_weight, out_weight, down_weight)
        )
        b_up = gather_small(up_bias).reshape(-1)
        x_mlp, e_mlp, mlp, finish = tokens, cotangent, mlp_gathered, lambda v, _: v
    small = jnp.concatenate([ln1_gain, ln1_bias, ln2_gain, ln2_bias, out_bias, down_bias, qkv_bias])
    small = gather_small(after(small, part_qkv))
    part = width // shards
    ln1_g, ln1_b, ln2_g, ln2_b, b_out, b_down = (
        small[:, i * part : (i + 1) * part].reshape(width).astype(f32) for i in range(6)
    )
    b_qkv = small[:, 6 * part :].reshape(3 * width).astype(f32)
    starts = [i * width + group * cols for i in range(3)]
    w_mine = jnp.concatenate([lax.dynamic_slice_in_dim(w_qkv, v, cols, 1) for v in starts], 1)
    b_mine = jnp.concatenate([lax.dynamic_slice_in_dim(b_qkv, v, cols, 0) for v in starts])
    x_all = after(x_all, w_mine)
    normed, queries, kv, cosine, sine = prepare(ln1_g, ln1_b, w_mine, b_mine, x_all, count)
    queries = queries.reshape(heads, HEAD, rows)
    pieces = {0: kv}
    step = lax.axis_size("blk") // 2
    while step >= 1:
        for i in list(pieces):
            pieces[i ^ step] = swap(pieces[i], "blk", step)
        step //= 2
    kv_all = [pieces[i] for i in range(len(pieces))]
    ranks = jnp.concatenate([v[2 * cols, : rows // STRETCH] for v in kv_all]).astype(jnp.int32)

    d_mixed = jnp.einsum("ed,td->et", w_out, after(cotangent, kv), preferred_element_type=f32).astype(bf16)
    d_heads = [lax.dynamic_slice_in_dim(d_mixed, (group ^ j) * cols, cols) for j in range(groups)]
    d_heads = [d_heads[0]] + [swap(d_heads[j], "ulysses", j) for j in range(1, groups)]
    d_heads = jnp.concatenate(d_heads, 1).reshape(heads, HEAD, rows)

    x_mlp, w_up = after((x_mlp, w_up), kv, d_mixed)
    mlp_out, d_norm_two, begun, terms, g_up_bias = mlp(
        x_mlp, e_mlp, ln2_g, ln2_b, w_up, b_up, w_down, pieces[lax.axis_size("blk") // 2], pieces[1], d_heads
    )

    e_around = around(after(cotangent, begun))
    d_heads = after(d_heads, begun)
    mixed, d_q, kept, sent = attend(ranks, queries, d_heads, kv_all)

    sent, e_around, terms, mlp_out, d_norm_two = after((sent, e_around, terms, mlp_out, d_norm_two))
    got = swap(sent, "blk", 1)
    step, kept = 1, [[kept[i], got[i]] for i in range(kept.shape[0])]
    while len(kept) > 1:
        step *= 2
        sent = sum(v.astype(f32) for v in stacked_terms(kept[1::2])).astype(bf16)
        got = swap(sent, "blk", step)
        kept = [kept[2 * i] + [got[i]] for i in range(got.shape[0])]
    g_up, g_down = finish(terms, sent)
    total = sum(v.astype(f32) for v in kept[0])
    d_q = rotate(d_q, cosine, -sine).astype(bf16).reshape(cols, rows)
    mixed = mixed.reshape(cols, rows)
    back_q = to_tokens(after(jnp.concatenate([d_q, mixed]), sent))
    e_all = jnp.concatenate(e_around, 0)
    g_out = jnp.dot(mixed, e_all, preferred_element_type=f32).astype(bf16)
    d_k = rotate(total[:cols].reshape(heads, HEAD, rows), cosine, -sine).reshape(cols, rows)
    d_kv = jnp.concatenate([d_k, total[cols:]]).astype(bf16)
    d_joined = jnp.concatenate([d_q, d_kv])
    g_bias_mine = jnp.sum(d_joined.astype(f32), 1)
    g_qkv = jnp.dot(d_joined, normed, preferred_element_type=f32).astype(bf16)
    back_kv = to_tokens(d_kv)
    grads = jnp.concatenate([g_qkv.reshape(3, cols, width), g_out[None]])
    grads = add_blks(grads)
    back_q, back_kv = by_device(back_q, group), by_device(back_kv, group)
    d_mine = jnp.concatenate(
        [v[:cols] for v in back_q] + [v[:cols] for v in back_kv] + [v[cols:] for v in back_kv], 0
    )
    d_norm_one = jnp.einsum("et,de->td", d_mine, w_qkv, preferred_element_type=f32)
    x_float = tokens.astype(f32)
    _, pull_one = jax.vjp(layer_norm, x_float, ln1_g, ln1_b)
    _, pull_two = jax.vjp(layer_norm, x_float, ln2_g, ln2_b)
    d_x_one, g_ln1_g, g_ln1_b = pull_one(d_norm_one)
    d_x_two, g_ln2_g, g_ln2_b = pull_two(d_norm_two)
    e_float = cotangent.astype(f32)

    g_qkv_bias = jnp.zeros((3, groups, cols), f32)
    g_qkv_bias = lax.dynamic_update_slice(g_qkv_bias, g_bias_mine.reshape(3, 1, cols), (0, group, 0))
    vectors = [g_ln1_g, g_ln1_b, g_ln2_g, g_ln2_b, jnp.sum(e_float, 0), g_qkv_bias.reshape(-1), g_up_bias]
    back = jnp.concatenate([v[cols:] for v in back_q], 0)
    attn_out = jnp.einsum("et,ed->td", back, w_out, preferred_element_type=f32)
    output = (x_float + (attn_out + b_out) + (mlp_out + b_down)).astype(bf16)
    input_grad = (e_float + d_x_one + d_x_two).astype(bf16)

    g_qkv, g_out, summed = attention_grads(grads, jnp.concatenate(vectors), output)
    results, start = [], 0
    for vector in vectors:
        mine = vector.shape[0] // shards
        results.append(lax.dynamic_slice_in_dim(summed, start + lax.axis_index("fsdp") * mine, mine))
        start += vector.shape[0]
    g_ln1_g, g_ln1_b, g_ln2_g, g_ln2_b, g_e, g_qkv_bias, g_up_bias = results
    return (
        output,
        input_grad,
        g_ln1_g,
        g_ln1_b,
        g_ln2_g,
        g_ln2_b,
        g_qkv,
        g_qkv_bias,
        g_out,
        g_e,
        g_up,
        g_up_bias,
        g_down,
        g_e,
    )


def solution(mesh):
    rows = P(("fsdp", "blk", "ulysses"), None)
    split, matrix = P("fsdp"), P("fsdp", None)
    return jax.shard_map(
        on_device,
        mesh=mesh,
        in_specs=(
            rows,
            P(("fsdp", "blk", "ulysses")),
            rows,
            split,
            split,
            split,
            split,
            matrix,
            split,
            matrix,
            split,
            matrix,
            split,
            matrix,
            split,
        ),
        out_specs=(
            rows,
            rows,
            split,
            split,
            split,
            split,
            matrix,
            split,
            matrix,
            split,
            matrix,
            split,
            matrix,
            split,
        ),
        check_vma=False,
    )
```

```python
import jax
import jax.numpy as jnp
import numpy as np
from jax import lax
from jax.experimental import pallas as pl
from jax.experimental.pallas import tpu as pltpu
from jax.sharding import PartitionSpec as P

HEAD = 64
ROT = 16
STRETCH = 128
CHUNK = 8
BIG_NEG = -1e30

f32 = jnp.float32
bf16 = jnp.bfloat16


def layer_norm(values, gain, shift):
    center = jnp.mean(values, -1, keepdims=True)
    offset = values - center
    spread = jnp.mean(offset * offset, -1, keepdims=True)
    return offset * lax.rsqrt(spread + 1e-05) * gain + shift


def gelu_exact(values):
    return jax.nn.gelu(values, approximate=False)


def swap(values, axis, bits):
    count = lax.axis_size(axis)
    return lax.ppermute(values, axis, [(i, i ^ bits) for i in range(count)])


def after(values, *earlier):
    return lax.optimization_barrier((values, earlier))[0]


def bit_of(axis, bit):
    return (lax.axis_index(axis) // bit) % 2


def in_order(bit, mine, other, axis=0):
    return jnp.concatenate([jnp.where(bit == 0, mine, other), jnp.where(bit == 0, other, mine)], axis)


def by_device(pieces, index):
    step = 1
    while step < len(pieces):
        odd = (index // step) % 2 == 1
        pieces = [jnp.where(odd, pieces[i ^ step], pieces[i]) for i in range(len(pieces))]
        step *= 2
    return pieces


def add_half(halves, axis, bit):
    which = bit_of(axis, bit)
    got = swap(jnp.where(which == 0, halves[1], halves[0]), axis, bit)
    kept = jnp.where(which == 0, halves[0], halves[1])
    return (kept.astype(f32) + got.astype(f32)).astype(bf16)


def halves_of(values, axis):
    half = values.shape[axis] // 2
    return (
        lax.slice_in_dim(values, 0, half, axis=axis),
        lax.slice_in_dim(values, half, 2 * half, axis=axis),
    )


def share_half(values, axis, bit, dim):
    return in_order(bit_of(axis, bit), values, swap(values, axis, bit), dim)


def gather_small(shard):
    if lax.axis_size("fsdp") != 2:
        return lax.all_gather(shard[None], "fsdp", axis=0, tiled=True)
    return in_order(lax.axis_index("fsdp"), shard[None], swap(shard[None], "fsdp", 1))


def quarter_of(shard):
    quarter = shard.shape[0] // 4
    place = bit_of("blk", 1) * 2 + bit_of("blk", 2)
    return lax.dynamic_slice_in_dim(shard, place * quarter, quarter)


def both_shards(shard, half):
    return in_order(lax.axis_index("fsdp"), shard, share_half(half, "blk", 1, 0))


def attend_kernel(rank, q_ref, g_ref, *refs):
    kv_refs = refs[:-9]
    o_ref, dq_ref, keep_ref, send_ref, rows, lanes, sums, probs, order = refs[-9:]
    heads = range(q_ref.shape[0])
    cols = q_ref.shape[0] * HEAD
    n_keys = rank.shape[0]
    own = q_ref.shape[-1] // STRETCH
    wide = 2 * STRETCH
    span = CHUNK * STRETCH

    for t in range(n_keys):
        i, at = t // own, (t % own) * STRETCH
        place = rank[t]
        for h in heads:
            both = jnp.concatenate(
                [
                    kv_refs[i][first : first + HEAD, at : at + STRETCH]
                    for first in (h * HEAD, cols + h * HEAD)
                ],
                0,
            )
            lanes[h, place] = both
            rows[h, place] = both.T
            sums[h, t] = jnp.zeros((STRETCH, 2 * HEAD), f32)
    for a in range(own):
        before = jnp.int32(0)
        for b in range(own):
            before += (rank[b] < rank[a]).astype(jnp.int32)
        order[before] = a

    def side(h, j, part):
        first = part * HEAD
        return jnp.concatenate(
            [lanes[h, j * CHUNK + i, first : first + HEAD, :] for i in range(CHUNK)], 1
        )

    def keys(h, j):
        return rows[h, pl.ds(j * CHUNK, CHUNK)].reshape(span, 2 * HEAD)

    def pair(p, carry):
        a, b = order[2 * p], order[2 * p + 1]
        ra, rb = rank[a], rank[b]
        at_a = pl.ds(pl.multiple_of(a * STRETCH, STRETCH), STRETCH)
        at_b = pl.ds(pl.multiple_of(b * STRETCH, STRETCH), STRETCH)
        q = [jnp.concatenate([q_ref[h, :, at_a], q_ref[h, :, at_b]], 1) for h in heads]
        g = [jnp.concatenate([g_ref[h, :, at_a], g_ref[h, :, at_b]], 1) for h in heads]
        none = jnp.zeros_like(q[0])
        q_low = [jnp.concatenate([v, none], 0) for v in q]
        g_high = [jnp.concatenate([none, v], 0) for v in g]
        lane = lax.broadcasted_iota(jnp.int32, (1, wide), 1)
        q_place = jnp.where(lane < STRETCH, ra * STRETCH + lane, rb * STRETCH + lane - STRETCH)
        clear = ra // CHUNK
        total = (rb + CHUNK) // CHUNK

        def score(j, tops, masked):
            result = []
            for h in heads:
                s = jnp.dot(keys(h, j), q_low[h], preferred_element_type=f32)
                if masked:
                    k_place = j * span + lax.broadcasted_iota(jnp.int32, (span, 1), 0)
                    s = jnp.where(k_place <= q_place, s, BIG_NEG)
                probs[h, j] = s
                result.append(jnp.maximum(tops[h], jnp.max(s.reshape(span // 8, 8, wide), 0)))
            return tuple(result)

        tops = tuple(jnp.full((8, wide), BIG_NEG, f32) for _ in heads)
        tops = lax.fori_loop(0, clear, lambda j, v: score(j, v, False), tops)
        tops = lax.fori_loop(clear, total, lambda j, v: score(j, v, True), tops)
        tops = [jnp.max(v, 0, keepdims=True) for v in tops]

        def weigh(j, state):
            result = []
            for h in heads:
                count, out = state[h]
                weight = jnp.exp(probs[h, j] - tops[h])
                probs[h, j] = weight
                count = count + jnp.sum(weight.reshape(span // 8, 8, wide), 0)
                out = out + jnp.dot(side(h, j, 1), weight.astype(bf16), preferred_element_type=f32)
                result.append((count, out))
            return tuple(result)

        state = tuple((jnp.zeros((8, wide), f32), jnp.zeros((HEAD, wide), f32)) for _ in heads)
        state = lax.fori_loop(0, total, weigh, state)
        inverse, delta, right = [], [], []
        for h in heads:
            count, out = state[h]
            inverse.append(1.0 / jnp.sum(count, 0, keepdims=True))
            out = out * inverse[h]
            delta.append(jnp.sum(out * g[h].astype(f32), 0, keepdims=True))
            o_ref[h, :, at_a] = out[:, :STRETCH].astype(bf16)
            o_ref[h, :, at_b] = out[:, STRETCH:].astype(bf16)
            top = jnp.concatenate([g[h], none], 0).T
            right.append(jnp.concatenate([top, jnp.concatenate([none, q[h]], 0).T], 0))

        def back(j, d_q):
            result = []
            for h in heads:
                weight = probs[h, j] * inverse[h]
                d_weight = jnp.dot(keys(h, j), g_high[h], preferred_element_type=f32)
                d_score = (weight * (d_weight - delta[h])).astype(bf16)
                left = jnp.concatenate([weight.astype(bf16), d_score], 1)
                sums[h, pl.ds(j * CHUNK, CHUNK)] += jnp.dot(
                    left, right[h], preferred_element_type=f32
                ).reshape(CHUNK, STRETCH, 2 * HEAD)
                result.append(d_q[h] + jnp.dot(side(h, j, 0), d_score, preferred_element_type=f32))
            return tuple(result)

        d_q = lax.fori_loop(0, total, back, tuple(jnp.zeros((HEAD, wide), f32) for _ in heads))
        for h in heads:
            scaled = d_q[h] * HEAD ** (-0.5)
            dq_ref[h, :, at_a] = scaled[:, :STRETCH]
            dq_ref[h, :, at_b] = scaled[:, STRETCH:]
        return carry

    lax.fori_loop(0, own // 2, pair, 0)
    for t in range(n_keys):
        i, at = t // own, (t % own) * STRETCH
        to = keep_ref if i % 2 == 0 else send_ref
        for h in heads:
            turned = sums[h, rank[t]].astype(bf16).T
            first = h * HEAD
            to[i // 2, cols + first : cols + first + HEAD, at : at + STRETCH] = turned[:HEAD]
            to[i // 2, first : first + HEAD, at : at + STRETCH] = turned[HEAD:]


def attend(ranks, q, g, kv):
    heads, _, count = q.shape
    devices = len(kv)
    n_keys = devices * count // STRETCH
    pairs = heads * 4 * HEAD * count * count * devices
    half = (devices // 2, 2 * heads * HEAD, count)
    q_spec = pl.BlockSpec(q.shape, lambda i, *_: (0, 0, 0))
    half_spec = pl.BlockSpec(half, lambda i, *_: (0, 0, 0))
    return pl.pallas_call(
        attend_kernel,
        grid_spec=pltpu.PrefetchScalarGridSpec(
            num_scalar_prefetch=1,
            grid=(1,),
            in_specs=[q_spec, q_spec] + [pl.BlockSpec(v.shape, lambda i, *_: (0, 0)) for v in kv],
            out_specs=[q_spec, q_spec, half_spec, half_spec],
            scratch_shapes=[
                pltpu.VMEM((heads, n_keys, STRETCH, 2 * HEAD), bf16),
                pltpu.VMEM((heads, n_keys, 2 * HEAD, STRETCH), bf16),
                pltpu.VMEM((heads, n_keys, STRETCH, 2 * HEAD), f32),
                pltpu.VMEM((heads, n_keys // CHUNK, CHUNK * STRETCH, 2 * STRETCH), f32),
                pltpu.SMEM((count // STRETCH,), jnp.int32),
            ],
        ),
        out_shape=[
            jax.ShapeDtypeStruct(q.shape, bf16),
            jax.ShapeDtypeStruct(q.shape, f32),
            jax.ShapeDtypeStruct(half, bf16),
            jax.ShapeDtypeStruct(half, bf16),
        ],
        compiler_params=pltpu.CompilerParams(vmem_limit_bytes=56 * 2**20),
        cost_estimate=pl.CostEstimate(
            flops=12 * pairs, bytes_accessed=16 * q.size * devices, transcendentals=pairs // 512
        ),
        name="attend",
    )(ranks, q, g, *kv)


def prepare_kernel(freqs, gain, shift, weight, bias, *refs):
    groups = len(refs) - 5
    x_refs = refs[:groups]
    normed_ref, q_ref, kv_ref, cos_ref, sin_ref = refs[groups:]
    count = normed_ref.shape[0] // groups
    cols = q_ref.shape[0]
    halfway = ROT // 2
    blocks = count // STRETCH
    lane = lax.broadcasted_iota(jnp.int32, (1, STRETCH), 1).astype(f32)
    kv_ref[2 * cols :, :] = jnp.zeros((kv_ref.shape[0] - 2 * cols, kv_ref.shape[1]), bf16)
    spots = lax.broadcasted_iota(jnp.int32, (1, STRETCH), 1)
    table = jnp.zeros((1, STRETCH), f32)
    for i, x_ref in enumerate(x_refs):
        at = i * count
        normed = layer_norm(x_ref[:count].astype(f32), gain[...], shift[...]).astype(bf16)
        normed_ref[at : at + count] = normed
        joined = jnp.dot(normed, weight[...], preferred_element_type=f32) + bias[...]
        joined = joined.T
        ranks = x_ref[count : count + 16, :STRETCH].astype(f32)[:1]
        places = []
        for b in range(blocks):
            rank = jnp.sum(jnp.where(spots == b, ranks, 0.0), 1, keepdims=True)
            places.append(rank * STRETCH + lane)
            table = jnp.where(spots == i * blocks + b, rank, table)
        angles = freqs[...] * jnp.concatenate(places, 1)
        cosine, sine = jnp.cos(angles), jnp.sin(angles)
        cos_ref[:, at : at + count] = cosine
        sin_ref[:, at : at + count] = sine
        for to, first, scale in ((q_ref, 0, HEAD ** (-0.5)), (kv_ref, cols, 1.0)):
            for h in range(cols // HEAD):
                low = first + h * HEAD
                one = joined[low : low + halfway]
                two = joined[low + halfway : low + ROT]
                rest = joined[low + ROT : low + HEAD]
                turned = jnp.concatenate(
                    [one * cosine - two * sine, two * cosine + one * sine, rest], 0
                ).astype(bf16)
                to[h * HEAD : (h + 1) * HEAD, at : at + count] = turned * jnp.bfloat16(scale)
        kv_ref[cols : 2 * cols, at : at + count] = joined[2 * cols :].astype(bf16)
    kv_ref[2 * cols :, :STRETCH] = jnp.broadcast_to(table, (16, STRETCH)).astype(bf16)


def prepare(gain, shift, weight, bias, x_all, count):
    width = weight.shape[0]
    cols = weight.shape[1] // 3
    rows = count * len(x_all)
    halfway = ROT // 2
    freqs = jnp.asarray(10000.0 ** (-np.arange(halfway) * 2.0 / ROT), f32)[:, None]
    return pl.pallas_call(
        prepare_kernel,
        out_shape=[
            jax.ShapeDtypeStruct((rows, width), bf16),
            jax.ShapeDtypeStruct((cols, rows), bf16),
            jax.ShapeDtypeStruct((2 * cols + 16, rows), bf16),
            jax.ShapeDtypeStruct((ROT // 2, rows), f32),
            jax.ShapeDtypeStruct((ROT // 2, rows), f32),
        ],
        compiler_params=pltpu.CompilerParams(vmem_limit_bytes=40 * 2**20),
        cost_estimate=pl.CostEstimate(
            flops=6 * cols * rows * width, bytes_accessed=8 * rows * width, transcendentals=0
        ),
        name="prepare",
    )(freqs, gain[None], shift[None], weight, bias[None], *x_all)


def rotate(heads, cosine, sine):
    halfway = ROT // 2
    first = heads[:, :halfway]
    second = heads[:, halfway:ROT]
    return jnp.concatenate(
        [first * cosine - second * sine, second * cosine + first * sine, heads[:, ROT:]], 1
    )


def around(values):
    return [values] + [swap(values, "ulysses", j) for j in range(1, lax.axis_size("ulysses"))]


def stacked_terms(lists):
    return [jnp.stack(v) for v in zip(*lists)]


def to_tokens(values):
    groups = lax.axis_size("ulysses")
    count = values.shape[1] // groups
    pieces = [values[:, j * count : (j + 1) * count] for j in range(groups)]
    return [pieces[0]] + [swap(pieces[j], "ulysses", j) for j in range(1, groups)]


def units_of(up_weight, side):
    units = up_weight.shape[1] // 2
    return jnp.where(side == 0, up_weight[:, :units], up_weight[:, units:])


def mlp_pair(x_both, e_both, gain, shift, up, up_bias, down_weight, *meanwhile):
    side = lax.axis_index("fsdp")
    rows, width = x_both.shape[0] // 2, x_both.shape[1]
    units = up.shape[1]
    normed = layer_norm(x_both.astype(f32), gain, shift).astype(bf16)
    hidden = jnp.dot(normed, up, preferred_element_type=f32) + up_bias.astype(f32)
    active_f, pull_gelu = jax.vjp(gelu_exact, hidden)
    active = active_f.astype(bf16)
    part = jnp.dot(active, down_weight, preferred_element_type=f32)
    d_active = jnp.einsum("td,fd->tf", e_both, down_weight, preferred_element_type=f32)
    d_hidden = pull_gelu(d_active)[0].astype(bf16)
    g_up_bias = jnp.sum(d_hidden.astype(f32), 0)
    d_part = jnp.einsum("tf,df->td", d_hidden, up, preferred_element_type=f32)
    sent = jnp.concatenate([part[rows:], d_part[rows:]]).astype(bf16)
    active, d_hidden = after((active, d_hidden), *meanwhile)
    g_up = jnp.einsum(
        "td,tcf->cdf", normed, d_hidden.reshape(2 * rows, 2, units // 2), preferred_element_type=f32
    ).astype(bf16)
    g_down = jnp.einsum("tf,td->fd", active, e_both, preferred_element_type=f32).astype(bf16)
    g_down = g_down.reshape(2, units // 2, width)
    pieces = jnp.stack([g_up, g_down], 1).reshape(2, 2, 2, width // 2, width)
    first = add_half((pieces[0], pieces[1]), "blk", 1)
    got = swap(after(sent, first), "fsdp", 1).astype(f32)
    out, d_normed = part[:rows] + got[:rows], d_part[:rows] + got[rows:]
    sums = add_half(halves_of(first, 2), "blk", 2)
    side, none = lax.axis_index("fsdp"), jnp.zeros_like(g_up_bias)
    g_up_bias = jnp.concatenate([jnp.where(side == 0, g_up_bias, none), jnp.where(side == 0, none, g_up_bias)])
    return out, d_normed, first, sums, g_up_bias


def finish_pair(sums, earlier):
    side = lax.axis_index("fsdp")
    sums = after(sums, earlier)
    sums = add_half(halves_of(sums, 2), "ulysses", 1)
    sums = add_half(halves_of(sums, 2), "ulysses", 2)
    got = swap(jnp.where(side == 0, sums[0, 1], sums[0, 0]), "fsdp", 1)
    kept = jnp.where(side == 0, sums[0, 0], sums[0, 1])
    sums = jnp.concatenate([in_order(side, kept[None], got[None]), sums[1]], 0)
    sums = share_half(sums, "ulysses", 2, 1)
    return share_half(sums, "ulysses", 1, 1)


def spread_pair(sums, *earlier):
    sums = after(share_half(sums, "blk", 2, 1), *earlier)
    return place_mlp(bit_of("blk", 1), sums, swap(sums, "blk", 1))


def place_mlp_kernel(which, mine, other, up_ref, down_ref):
    width = mine.shape[-1]
    for c, ref in ((which[0], mine), (1 - which[0], other)):
        for f in range(2):
            at = pl.multiple_of((2 * f + c) * width, STRETCH)
            up_ref[:, pl.ds(at, width)] = ref[f].astype(f32)
            down_ref[c, f] = ref[2 + f].astype(f32)


def place_mlp(which, mine, other):
    _, rows, width = mine.shape
    step = rows // 4
    whole = pl.BlockSpec((4, step, width), lambda i, *_: (0, i, 0))
    up, down = pl.pallas_call(
        place_mlp_kernel,
        grid_spec=pltpu.PrefetchScalarGridSpec(
            num_scalar_prefetch=1,
            grid=(4,),
            in_specs=[whole, whole],
            out_specs=[
                pl.BlockSpec((step, 4 * width), lambda i, *_: (i, 0)),
                pl.BlockSpec((2, 2, step, width), lambda i, *_: (0, 0, i, 0)),
            ],
        ),
        out_shape=[
            jax.ShapeDtypeStruct((rows, 4 * width), f32),
            jax.ShapeDtypeStruct((2, 2, rows, width), f32),
        ],
        compiler_params=pltpu.CompilerParams(vmem_limit_bytes=32 * 2**20),
        cost_estimate=pl.CostEstimate(flops=0, bytes_accessed=12 * mine.size, transcendentals=0),
        name="place_mlp",
    )(which[None], mine, other)
    return up, down.reshape(4 * rows, width)


def place_qkv_kernel(which, mine, other, qkv_ref, out_ref):
    first = which[0] == 0
    rows, half = mine.shape[1:]
    width = 2 * half
    groups = mine.shape[0] // 4
    for t in range(3):
        blocks = []
        for z in range(groups):
            a, b = mine[3 * z + t], other[3 * z + t]
            blocks += [jnp.where(first, a, b), jnp.where(first, b, a)]
        qkv_ref[:, t * width : (t + 1) * width] = jnp.concatenate(blocks, 0).astype(f32).T
    for z in range(groups // 2):
        for side in range(2):
            a, b = mine[3 * groups + 2 * z + side], other[3 * groups + 2 * z + side]
            at = 2 * z * rows
            both = jnp.concatenate([jnp.where(first, a, b), jnp.where(first, b, a)], 0)
            out_ref[at : at + 2 * rows, side * half : (side + 1) * half] = both.astype(f32)


def place_qkv(which, mine, other):
    _, rows, half = mine.shape
    groups = mine.shape[0] // 4
    return pl.pallas_call(
        place_qkv_kernel,
        grid_spec=pltpu.PrefetchScalarGridSpec(
            num_scalar_prefetch=1,
            grid=(1,),
            in_specs=[pl.BlockSpec(v.shape, lambda i, *_: (0, 0, 0)) for v in (mine, other)],
            out_specs=[
                pl.BlockSpec((half, 6 * half), lambda i, *_: (0, 0)),
                pl.BlockSpec((groups * rows, 2 * half), lambda i, *_: (0, 0)),
            ],
        ),
        out_shape=[
            jax.ShapeDtypeStruct((half, 6 * half), f32),
            jax.ShapeDtypeStruct((groups * rows, 2 * half), f32),
        ],
        compiler_params=pltpu.CompilerParams(vmem_limit_bytes=40 * 2**20),
        cost_estimate=pl.CostEstimate(flops=0, bytes_accessed=12 * mine.size, transcendentals=0),
        name="place_qkv",
    )(which[None], mine, other)


def mlp_gathered(x, e, gain, shift, up, bias, down, *meanwhile):
    normed = layer_norm(x.astype(f32), gain, shift).astype(bf16)
    hidden = jnp.dot(normed, up, preferred_element_type=f32) + bias.astype(f32)
    active_f, pull_gelu = jax.vjp(gelu_exact, hidden)
    active = active_f.astype(bf16)
    out = jnp.dot(active, down, preferred_element_type=f32)
    g_down = jnp.einsum("tf,td->fd", active, e, preferred_element_type=f32)
    d_active = jnp.einsum("td,fd->tf", e, down, preferred_element_type=f32)
    d_hidden = pull_gelu(d_active)[0].astype(bf16)
    g_up = jnp.einsum("td,tf->df", normed, d_hidden, preferred_element_type=f32)
    d_normed = jnp.einsum("tf,df->td", d_hidden, up, preferred_element_type=f32)
    g_up, g_down = (
        lax.psum(
            lax.psum_scatter(g.astype(bf16), "fsdp", scatter_dimension=0, tiled=True),
            ("blk", "ulysses"),
        ).astype(f32)
        for g in (g_up, g_down)
    )
    return out, d_normed, d_hidden, (g_up, g_down), jnp.sum(d_hidden.astype(f32), 0)


def add_blks(grads):
    if lax.axis_size("fsdp") != 2:
        return lax.psum(grads, "blk")
    return add_half(halves_of(add_half(halves_of(grads, 1), "blk", 1), 1), "blk", 2)


def attention_grads(grads, vector, output):
    side = lax.axis_index("fsdp")
    group = lax.axis_index("ulysses")
    groups = lax.axis_size("ulysses")
    _, rows, width = grads.shape
    if lax.axis_size("fsdp") != 2:
        total = lax.all_gather(lax.psum(grads, "fsdp"), "ulysses", axis=1, tiled=True)
        part = width // lax.axis_size("fsdp")
        g_qkv = lax.dynamic_slice_in_dim(total[:3], side * part, part, 2)
        g_out = lax.dynamic_slice_in_dim(total[3], side * part, part, 0)
        g_qkv = g_qkv.reshape(3 * width, part).T.astype(f32)
        return g_qkv, g_out.astype(f32), sum_everywhere(vector)
    half = width // 2
    size = vector.shape[0]
    small = jnp.pad(vector.astype(bf16), (0, rows * half - size)).reshape(1, rows, half)
    low, high = grads[:, :, :half], grads[:, :, half:]
    kept = jnp.where(side == 0, low[:3], high[:3])
    sent = jnp.where(side == 0, high[:3], low[:3])
    whole = jnp.stack([low[3], high[3]])
    kept = jnp.concatenate([kept, whole, small])
    got = swap(jnp.concatenate([sent, whole, small]), "fsdp", 1)
    kept = (kept.astype(f32) + got.astype(f32)).astype(bf16)
    kept = by_device(around(kept), group)
    small = sum(v[5:].astype(f32) for v in kept).astype(bf16)
    of_qkv = jnp.concatenate([v[:3] for v in kept])
    of_out = [jnp.where(side == 0, a[3:5], b[3:5]) for a, b in zip(kept[: groups // 2], kept[groups // 2 :])]
    kept = jnp.concatenate([of_qkv] + of_out)
    units = kept.shape[0]
    got = after(swap(jnp.concatenate([kept, small]), "blk", 2), output)
    kept = in_order(bit_of("blk", 2), kept, got[:units], 1)
    small = (small.astype(f32) + got[units:].astype(f32)).astype(bf16)
    wide = jnp.pad(small, ((0, 0), (0, rows), (0, 0)))
    got = swap(jnp.concatenate([kept, wide]), "blk", 1)
    small = small.astype(f32) + got[units:, :rows].astype(f32)
    g_qkv, g_out = place_qkv(bit_of("blk", 1), kept, got)
    return g_qkv, g_out, small.reshape(-1)[:size]


def sum_everywhere(values):
    for axis in ("blk", "ulysses", "fsdp"):
        step = 1
        while step < lax.axis_size(axis):
            values = values + swap(values, axis, step)
            step *= 2
    return values


def on_device(
    tokens,
    positions,
    cotangent,
    ln1_gain,
    ln1_bias,
    ln2_gain,
    ln2_bias,
    qkv_weight,
    qkv_bias,
    out_weight,
    out_bias,
    up_weight,
    up_bias,
    down_weight,
    down_bias,
):
    count, width = tokens.shape
    groups = lax.axis_size("ulysses")
    group = lax.axis_index("ulysses")
    shards = lax.axis_size("fsdp")
    cols = width // groups
    heads = cols // HEAD
    rows = count * groups

    ranks = (positions[::STRETCH] // STRETCH).astype(bf16)[None]
    ranks = jnp.pad(ranks, ((0, 15), (0, width - ranks.shape[1])))
    x_ranks = jnp.concatenate([tokens, ranks])
    if shards == 2:
        side = lax.axis_index("fsdp")
        part_qkv = swap(quarter_of(qkv_weight), "fsdp", 1)
        half_up = jnp.concatenate([units_of(up_weight, 1 - side), out_weight], 1)
        part_up = swap(after(quarter_of(half_up), part_qkv), "fsdp", 1)
        x_e = swap(after(jnp.stack([tokens, cotangent]), part_up), "fsdp", 1)
        w_qkv = both_shards(qkv_weight, share_half(part_qkv, "blk", 2, 0))
        half_up = share_half(part_up, "blk", 2, 0)
        x_all = around(x_ranks)
        mine = jnp.concatenate([units_of(up_weight, side), out_weight], 1)
        half_up = both_shards(mine, half_up)
        w_up, w_out = half_up[:, :-width], half_up[:, -width:]
        x_mlp = jnp.concatenate([tokens, x_e[0]])
        e_mlp = jnp.concatenate([cotangent, x_e[1]])
        b_up, w_down = up_bias, down_weight
        mlp, finish, spread = mlp_pair, finish_pair, spread_pair
    else:
        x_all, part_qkv = around(x_ranks), x_ranks
        w_qkv, w_up, w_out, w_down = (
            lax.all_gather(w, "fsdp", axis=0, tiled=True)
            for w in (qkv_weight, up_weight, out_weight, down_weight)
        )
        b_up = gather_small(up_bias).reshape(-1)
        x_mlp, e_mlp = tokens, cotangent
        mlp, finish, spread = mlp_gathered, lambda v, _: v, lambda v, *_: v
    small = jnp.concatenate([ln1_gain, ln1_bias, ln2_gain, ln2_bias, out_bias, down_bias, qkv_bias])
    small = gather_small(after(small, part_qkv))
    part = width // shards
    ln1_g, ln1_b, ln2_g, ln2_b, b_out, b_down = (
        small[:, i * part : (i + 1) * part].reshape(width).astype(f32) for i in range(6)
    )
    b_qkv = small[:, 6 * part :].reshape(3 * width).astype(f32)
    starts = [i * width + group * cols for i in range(3)]
    w_mine = jnp.concatenate([lax.dynamic_slice_in_dim(w_qkv, v, cols, 1) for v in starts], 1)
    b_mine = jnp.concatenate([lax.dynamic_slice_in_dim(b_qkv, v, cols, 0) for v in starts])
    x_all = after(x_all, w_mine)
    normed, queries, kv, cosine, sine = prepare(ln1_g, ln1_b, w_mine, b_mine, x_all, count)
    queries = queries.reshape(heads, HEAD, rows)
    pieces = {0: kv}
    step = lax.axis_size("blk") // 2
    while step >= 1:
        for i in list(pieces):
            pieces[i ^ step] = swap(pieces[i], "blk", step)
        step //= 2
    kv_all = [pieces[i] for i in range(len(pieces))]
    ranks = jnp.concatenate([v[2 * cols, : rows // STRETCH] for v in kv_all]).astype(jnp.int32)

    d_mixed = jnp.einsum("ed,td->et", w_out, after(cotangent, kv), preferred_element_type=f32).astype(bf16)
    d_heads = [lax.dynamic_slice_in_dim(d_mixed, (group ^ j) * cols, cols) for j in range(groups)]
    d_heads = [d_heads[0]] + [swap(d_heads[j], "ulysses", j) for j in range(1, groups)]
    d_heads = jnp.concatenate(d_heads, 1).reshape(heads, HEAD, rows)

    x_mlp, w_up = after((x_mlp, w_up), kv, d_mixed)
    mlp_out, d_norm_two, begun, terms, g_up_bias = mlp(
        x_mlp, e_mlp, ln2_g, ln2_b, w_up, b_up, w_down, pieces[lax.axis_size("blk") // 2], pieces[1], d_heads
    )

    e_around = around(after(cotangent, begun))
    d_heads = after(d_heads, begun)
    mixed, d_q, kept, sent = attend(ranks, queries, d_heads, kv_all)

    sent, e_around, terms, mlp_out, d_norm_two = after((sent, e_around, terms, mlp_out, d_norm_two))
    d_q = rotate(d_q, cosine, -sine).astype(bf16).reshape(cols, rows)
    mixed = mixed.reshape(cols, rows)
    back_q = to_tokens(jnp.concatenate([d_q, mixed]))
    got = swap(sent, "blk", 1)
    step, kept = 1, [[kept[i], got[i]] for i in range(kept.shape[0])]
    while len(kept) > 1:
        step *= 2
        sent = sum(v.astype(f32) for v in stacked_terms(kept[1::2])).astype(bf16)
        if step == 2:
            terms = finish(terms, sent)
        sent, back_q = after((sent, back_q))
        got = swap(sent, "blk", step)
        kept = [kept[2 * i] + [got[i]] for i in range(got.shape[0])]
    total = sum(v.astype(f32) for v in kept[0])
    e_all = jnp.concatenate(e_around, 0)
    g_out = jnp.dot(mixed, e_all, preferred_element_type=f32).astype(bf16)
    d_k = rotate(total[:cols].reshape(heads, HEAD, rows), cosine, -sine).reshape(cols, rows)
    d_kv = jnp.concatenate([d_k, total[cols:]]).astype(bf16)
    d_joined = jnp.concatenate([d_q, d_kv])
    g_bias_mine = jnp.sum(d_joined.astype(f32), 1)
    g_qkv = jnp.dot(d_joined, normed, preferred_element_type=f32).astype(bf16)
    back_kv = to_tokens(d_kv)
    grads = jnp.concatenate([g_qkv.reshape(3, cols, width), g_out[None]])
    grads = add_blks(grads)
    back_kv = after(back_kv, grads)
    back_q, back_kv = by_device(back_q, group), by_device(back_kv, group)
    d_mine = jnp.concatenate(
        [v[:cols] for v in back_q] + [v[:cols] for v in back_kv] + [v[cols:] for v in back_kv], 0
    )
    d_norm_one = jnp.einsum("et,de->td", d_mine, w_qkv, preferred_element_type=f32)
    x_float = tokens.astype(f32)
    _, pull_one = jax.vjp(layer_norm, x_float, ln1_g, ln1_b)
    _, pull_two = jax.vjp(layer_norm, x_float, ln2_g, ln2_b)
    d_x_one, g_ln1_g, g_ln1_b = pull_one(d_norm_one)
    d_x_two, g_ln2_g, g_ln2_b = pull_two(d_norm_two)
    e_float = cotangent.astype(f32)

    g_qkv_bias = jnp.zeros((3, groups, cols), f32)
    g_qkv_bias = lax.dynamic_update_slice(g_qkv_bias, g_bias_mine.reshape(3, 1, cols), (0, group, 0))
    vectors = [g_ln1_g, g_ln1_b, g_ln2_g, g_ln2_b, jnp.sum(e_float, 0), g_qkv_bias.reshape(-1), g_up_bias]
    back = jnp.concatenate([v[cols:] for v in back_q], 0)
    attn_out = jnp.einsum("et,ed->td", back, w_out, preferred_element_type=f32)
    output = (x_float + (attn_out + b_out) + (mlp_out + b_down)).astype(bf16)
    input_grad = (e_float + d_x_one + d_x_two).astype(bf16)

    g_qkv, g_out, summed = attention_grads(grads, jnp.concatenate(vectors), output)
    g_up, g_down = spread(terms, output, input_grad)
    results, start = [], 0
    for vector in vectors:
        mine = vector.shape[0] // shards
        results.append(lax.dynamic_slice_in_dim(summed, start + lax.axis_index("fsdp") * mine, mine))
        start += vector.shape[0]
    g_ln1_g, g_ln1_b, g_ln2_g, g_ln2_b, g_e, g_qkv_bias, g_up_bias = results
    return (
        output,
        input_grad,
        g_ln1_g,
        g_ln1_b,
        g_ln2_g,
        g_ln2_b,
        g_qkv,
        g_qkv_bias,
        g_out,
        g_e,
        g_up,
        g_up_bias,
        g_down,
        g_e,
    )


def solution(mesh):
    rows = P(("fsdp", "blk", "ulysses"), None)
    split, matrix = P("fsdp"), P("fsdp", None)
    return jax.shard_map(
        on_device,
        mesh=mesh,
        in_specs=(
            rows,
            P(("fsdp", "blk", "ulysses")),
            rows,
            split,
            split,
            split,
            split,
            matrix,
            split,
            matrix,
            split,
            matrix,
            split,
            matrix,
            split,
        ),
        out_specs=(
            rows,
            rows,
            split,
            split,
            split,
            split,
            matrix,
            split,
            matrix,
            split,
            matrix,
            split,
            matrix,
            split,
        ),
        check_vma=False,
    )
```

```python
import jax
import jax.numpy as jnp
import numpy as np
from jax import lax
from jax.experimental import pallas as pl
from jax.experimental.pallas import tpu as pltpu
from jax.sharding import PartitionSpec as P

HEAD = 64
ROT = 16
STRETCH = 128
CHUNK = 8
BIG_NEG = -1e30

f32 = jnp.float32
bf16 = jnp.bfloat16


def layer_norm(values, gain, shift):
    center = jnp.mean(values, -1, keepdims=True)
    offset = values - center
    spread = jnp.mean(offset * offset, -1, keepdims=True)
    return offset * lax.rsqrt(spread + 1e-05) * gain + shift


def gelu_exact(values):
    return jax.nn.gelu(values, approximate=False)


def swap(values, axis, bits):
    count = lax.axis_size(axis)
    return lax.ppermute(values, axis, [(i, i ^ bits) for i in range(count)])


def after(values, *earlier):
    return lax.optimization_barrier((values, earlier))[0]


def bit_of(axis, bit):
    return (lax.axis_index(axis) // bit) % 2


def in_order(bit, mine, other, axis=0):
    return jnp.concatenate([jnp.where(bit == 0, mine, other), jnp.where(bit == 0, other, mine)], axis)


def by_device(pieces, index):
    step = 1
    while step < len(pieces):
        odd = (index // step) % 2 == 1
        pieces = [jnp.where(odd, pieces[i ^ step], pieces[i]) for i in range(len(pieces))]
        step *= 2
    return pieces


def add_half(halves, axis, bit):
    which = bit_of(axis, bit)
    got = swap(jnp.where(which == 0, halves[1], halves[0]), axis, bit)
    kept = jnp.where(which == 0, halves[0], halves[1])
    return (kept.astype(f32) + got.astype(f32)).astype(bf16)


def halves_of(values, axis):
    half = values.shape[axis] // 2
    return (
        lax.slice_in_dim(values, 0, half, axis=axis),
        lax.slice_in_dim(values, half, 2 * half, axis=axis),
    )


def share_half(values, axis, bit, dim):
    return in_order(bit_of(axis, bit), values, swap(values, axis, bit), dim)


def gather_small(shard):
    if lax.axis_size("fsdp") != 2:
        return lax.all_gather(shard[None], "fsdp", axis=0, tiled=True)
    return in_order(lax.axis_index("fsdp"), shard[None], swap(shard[None], "fsdp", 1))


def quarter_of(shard):
    quarter = shard.shape[0] // 4
    place = bit_of("blk", 1) * 2 + bit_of("blk", 2)
    return lax.dynamic_slice_in_dim(shard, place * quarter, quarter)


def both_shards(shard, half):
    return in_order(lax.axis_index("fsdp"), shard, share_half(half, "blk", 1, 0))


def attend_kernel(rank, q_ref, g_ref, *refs):
    kv_refs = refs[:-9]
    o_ref, dq_ref, keep_ref, send_ref, rows, lanes, sums, probs, order = refs[-9:]
    heads = range(q_ref.shape[0])
    cols = q_ref.shape[0] * HEAD
    n_keys = rank.shape[0]
    own = q_ref.shape[-1] // STRETCH
    wide = 2 * STRETCH
    span = CHUNK * STRETCH

    for t in range(n_keys):
        i, at = t // own, (t % own) * STRETCH
        place = rank[t]
        for h in heads:
            both = jnp.concatenate(
                [
                    kv_refs[i][first : first + HEAD, at : at + STRETCH]
                    for first in (h * HEAD, cols + h * HEAD)
                ],
                0,
            )
            lanes[h, place] = both
            rows[h, place] = both.T
            sums[h, t] = jnp.zeros((STRETCH, 2 * HEAD), f32)
    for a in range(own):
        before = jnp.int32(0)
        for b in range(own):
            before += (rank[b] < rank[a]).astype(jnp.int32)
        order[before] = a

    def side(h, j, part):
        first = part * HEAD
        return jnp.concatenate(
            [lanes[h, j * CHUNK + i, first : first + HEAD, :] for i in range(CHUNK)], 1
        )

    def keys(h, j):
        return rows[h, pl.ds(j * CHUNK, CHUNK)].reshape(span, 2 * HEAD)

    def pair(p, carry):
        a, b = order[2 * p], order[2 * p + 1]
        ra, rb = rank[a], rank[b]
        at_a = pl.ds(pl.multiple_of(a * STRETCH, STRETCH), STRETCH)
        at_b = pl.ds(pl.multiple_of(b * STRETCH, STRETCH), STRETCH)
        q = [jnp.concatenate([q_ref[h, :, at_a], q_ref[h, :, at_b]], 1) for h in heads]
        g = [jnp.concatenate([g_ref[h, :, at_a], g_ref[h, :, at_b]], 1) for h in heads]
        none = jnp.zeros_like(q[0])
        q_low = [jnp.concatenate([v, none], 0) for v in q]
        g_high = [jnp.concatenate([none, v], 0) for v in g]
        lane = lax.broadcasted_iota(jnp.int32, (1, wide), 1)
        q_place = jnp.where(lane < STRETCH, ra * STRETCH + lane, rb * STRETCH + lane - STRETCH)
        clear = ra // CHUNK
        total = (rb + CHUNK) // CHUNK

        def score(j, tops, masked):
            result = []
            for h in heads:
                s = jnp.dot(keys(h, j), q_low[h], preferred_element_type=f32)
                if masked:
                    k_place = j * span + lax.broadcasted_iota(jnp.int32, (span, 1), 0)
                    s = jnp.where(k_place <= q_place, s, BIG_NEG)
                probs[h, j] = s
                result.append(jnp.maximum(tops[h], jnp.max(s.reshape(span // 8, 8, wide), 0)))
            return tuple(result)

        tops = tuple(jnp.full((8, wide), BIG_NEG, f32) for _ in heads)
        tops = lax.fori_loop(0, clear, lambda j, v: score(j, v, False), tops)
        tops = lax.fori_loop(clear, total, lambda j, v: score(j, v, True), tops)
        tops = [jnp.max(v, 0, keepdims=True) for v in tops]

        def weigh(j, state):
            result = []
            for h in heads:
                count, out = state[h]
                weight = jnp.exp(probs[h, j] - tops[h])
                probs[h, j] = weight
                count = count + jnp.sum(weight.reshape(span // 8, 8, wide), 0)
                out = out + jnp.dot(side(h, j, 1), weight.astype(bf16), preferred_element_type=f32)
                result.append((count, out))
            return tuple(result)

        state = tuple((jnp.zeros((8, wide), f32), jnp.zeros((HEAD, wide), f32)) for _ in heads)
        state = lax.fori_loop(0, total, weigh, state)
        inverse, delta, right = [], [], []
        for h in heads:
            count, out = state[h]
            inverse.append(1.0 / jnp.sum(count, 0, keepdims=True))
            out = out * inverse[h]
            delta.append(jnp.sum(out * g[h].astype(f32), 0, keepdims=True))
            o_ref[h, :, at_a] = out[:, :STRETCH].astype(bf16)
            o_ref[h, :, at_b] = out[:, STRETCH:].astype(bf16)
            top = jnp.concatenate([g[h], none], 0).T
            right.append(jnp.concatenate([top, jnp.concatenate([none, q[h]], 0).T], 0))

        def back(j, d_q):
            result = []
            for h in heads:
                weight = probs[h, j] * inverse[h]
                d_weight = jnp.dot(keys(h, j), g_high[h], preferred_element_type=f32)
                d_score = (weight * (d_weight - delta[h])).astype(bf16)
                left = jnp.concatenate([weight.astype(bf16), d_score], 1)
                sums[h, pl.ds(j * CHUNK, CHUNK)] += jnp.dot(
                    left, right[h], preferred_element_type=f32
                ).reshape(CHUNK, STRETCH, 2 * HEAD)
                result.append(d_q[h] + jnp.dot(side(h, j, 0), d_score, preferred_element_type=f32))
            return tuple(result)

        d_q = lax.fori_loop(0, total, back, tuple(jnp.zeros((HEAD, wide), f32) for _ in heads))
        for h in heads:
            scaled = d_q[h] * HEAD ** (-0.5)
            dq_ref[h, :, at_a] = scaled[:, :STRETCH]
            dq_ref[h, :, at_b] = scaled[:, STRETCH:]
        return carry

    lax.fori_loop(0, own // 2, pair, 0)
    for t in range(n_keys):
        i, at = t // own, (t % own) * STRETCH
        to = keep_ref if i % 2 == 0 else send_ref
        for h in heads:
            turned = sums[h, rank[t]].astype(bf16).T
            first = h * HEAD
            to[i // 2, cols + first : cols + first + HEAD, at : at + STRETCH] = turned[:HEAD]
            to[i // 2, first : first + HEAD, at : at + STRETCH] = turned[HEAD:]


def attend(ranks, q, g, kv):
    heads, _, count = q.shape
    devices = len(kv)
    n_keys = devices * count // STRETCH
    pairs = heads * 4 * HEAD * count * count * devices
    half = (devices // 2, 2 * heads * HEAD, count)
    q_spec = pl.BlockSpec(q.shape, lambda i, *_: (0, 0, 0))
    half_spec = pl.BlockSpec(half, lambda i, *_: (0, 0, 0))
    return pl.pallas_call(
        attend_kernel,
        grid_spec=pltpu.PrefetchScalarGridSpec(
            num_scalar_prefetch=1,
            grid=(1,),
            in_specs=[q_spec, q_spec] + [pl.BlockSpec(v.shape, lambda i, *_: (0, 0)) for v in kv],
            out_specs=[q_spec, q_spec, half_spec, half_spec],
            scratch_shapes=[
                pltpu.VMEM((heads, n_keys, STRETCH, 2 * HEAD), bf16),
                pltpu.VMEM((heads, n_keys, 2 * HEAD, STRETCH), bf16),
                pltpu.VMEM((heads, n_keys, STRETCH, 2 * HEAD), f32),
                pltpu.VMEM((heads, n_keys // CHUNK, CHUNK * STRETCH, 2 * STRETCH), f32),
                pltpu.SMEM((count // STRETCH,), jnp.int32),
            ],
        ),
        out_shape=[
            jax.ShapeDtypeStruct(q.shape, bf16),
            jax.ShapeDtypeStruct(q.shape, f32),
            jax.ShapeDtypeStruct(half, bf16),
            jax.ShapeDtypeStruct(half, bf16),
        ],
        compiler_params=pltpu.CompilerParams(vmem_limit_bytes=56 * 2**20),
        cost_estimate=pl.CostEstimate(
            flops=12 * pairs, bytes_accessed=16 * q.size * devices, transcendentals=pairs // 512
        ),
        name="attend",
    )(ranks, q, g, *kv)


def prepare_kernel(freqs, gain, shift, weight, bias, *refs):
    groups = len(refs) - 5
    x_refs = refs[:groups]
    normed_ref, q_ref, kv_ref, cos_ref, sin_ref = refs[groups:]
    count = normed_ref.shape[0] // groups
    cols = q_ref.shape[0]
    halfway = ROT // 2
    blocks = count // STRETCH
    lane = lax.broadcasted_iota(jnp.int32, (1, STRETCH), 1).astype(f32)
    kv_ref[2 * cols :, :] = jnp.zeros((kv_ref.shape[0] - 2 * cols, kv_ref.shape[1]), bf16)
    spots = lax.broadcasted_iota(jnp.int32, (1, STRETCH), 1)
    table = jnp.zeros((1, STRETCH), f32)
    for i, x_ref in enumerate(x_refs):
        at = i * count
        normed = layer_norm(x_ref[:count].astype(f32), gain[...], shift[...]).astype(bf16)
        normed_ref[at : at + count] = normed
        joined = jnp.dot(normed, weight[...], preferred_element_type=f32) + bias[...]
        joined = joined.T
        ranks = x_ref[count : count + 16, :STRETCH].astype(f32)[:1]
        places = []
        for b in range(blocks):
            rank = jnp.sum(jnp.where(spots == b, ranks, 0.0), 1, keepdims=True)
            places.append(rank * STRETCH + lane)
            table = jnp.where(spots == i * blocks + b, rank, table)
        angles = freqs[...] * jnp.concatenate(places, 1)
        cosine, sine = jnp.cos(angles), jnp.sin(angles)
        cos_ref[:, at : at + count] = cosine
        sin_ref[:, at : at + count] = sine
        for to, first, scale in ((q_ref, 0, HEAD ** (-0.5)), (kv_ref, cols, 1.0)):
            for h in range(cols // HEAD):
                low = first + h * HEAD
                one = joined[low : low + halfway]
                two = joined[low + halfway : low + ROT]
                rest = joined[low + ROT : low + HEAD]
                turned = jnp.concatenate(
                    [one * cosine - two * sine, two * cosine + one * sine, rest], 0
                ).astype(bf16)
                to[h * HEAD : (h + 1) * HEAD, at : at + count] = turned * jnp.bfloat16(scale)
        kv_ref[cols : 2 * cols, at : at + count] = joined[2 * cols :].astype(bf16)
    kv_ref[2 * cols :, :STRETCH] = jnp.broadcast_to(table, (16, STRETCH)).astype(bf16)


def prepare(gain, shift, weight, bias, x_all, count):
    width = weight.shape[0]
    cols = weight.shape[1] // 3
    rows = count * len(x_all)
    halfway = ROT // 2
    freqs = jnp.asarray(10000.0 ** (-np.arange(halfway) * 2.0 / ROT), f32)[:, None]
    return pl.pallas_call(
        prepare_kernel,
        out_shape=[
            jax.ShapeDtypeStruct((rows, width), bf16),
            jax.ShapeDtypeStruct((cols, rows), bf16),
            jax.ShapeDtypeStruct((2 * cols + 16, rows), bf16),
            jax.ShapeDtypeStruct((ROT // 2, rows), f32),
            jax.ShapeDtypeStruct((ROT // 2, rows), f32),
        ],
        compiler_params=pltpu.CompilerParams(vmem_limit_bytes=40 * 2**20),
        cost_estimate=pl.CostEstimate(
            flops=6 * cols * rows * width, bytes_accessed=8 * rows * width, transcendentals=0
        ),
        name="prepare",
    )(freqs, gain[None], shift[None], weight, bias[None], *x_all)


def rotate(heads, cosine, sine):
    halfway = ROT // 2
    first = heads[:, :halfway]
    second = heads[:, halfway:ROT]
    return jnp.concatenate(
        [first * cosine - second * sine, second * cosine + first * sine, heads[:, ROT:]], 1
    )


def around(values):
    return [values] + [swap(values, "ulysses", j) for j in range(1, lax.axis_size("ulysses"))]


def stacked_terms(lists):
    return [jnp.stack(v) for v in zip(*lists)]


def to_tokens(values):
    groups = lax.axis_size("ulysses")
    count = values.shape[1] // groups
    pieces = [values[:, j * count : (j + 1) * count] for j in range(groups)]
    return [pieces[0]] + [swap(pieces[j], "ulysses", j) for j in range(1, groups)]


def units_of(up_weight, side):
    units = up_weight.shape[1] // 2
    return jnp.where(side == 0, up_weight[:, :units], up_weight[:, units:])


def mlp_pair(x_both, e_both, gain, shift, up, up_bias, down_weight, *meanwhile):
    side = lax.axis_index("fsdp")
    rows, width = x_both.shape[0] // 2, x_both.shape[1]
    units = up.shape[1]
    normed = layer_norm(x_both.astype(f32), gain, shift).astype(bf16)
    hidden = jnp.dot(normed, up, preferred_element_type=f32) + up_bias.astype(f32)
    active_f, pull_gelu = jax.vjp(gelu_exact, hidden)
    active = active_f.astype(bf16)
    part = jnp.dot(active, down_weight, preferred_element_type=f32)
    d_active = jnp.einsum("td,fd->tf", e_both, down_weight, preferred_element_type=f32)
    d_hidden = pull_gelu(d_active)[0].astype(bf16)
    g_up_bias = jnp.sum(d_hidden.astype(f32), 0)
    d_part = jnp.einsum("tf,df->td", d_hidden, up, preferred_element_type=f32)
    sent = jnp.concatenate([part[rows:], d_part[rows:]]).astype(bf16)
    active, d_hidden = after((active, d_hidden), *meanwhile)
    g_up = jnp.einsum(
        "td,tcf->cdf", normed, d_hidden.reshape(2 * rows, 2, units // 2), preferred_element_type=f32
    ).astype(bf16)
    g_down = jnp.einsum("tf,td->fd", active, e_both, preferred_element_type=f32).astype(bf16)
    g_down = g_down.reshape(2, units // 2, width)
    pieces = jnp.stack([g_up, g_down], 1).reshape(2, 2, 2, width // 2, width)
    first = add_half((pieces[0], pieces[1]), "blk", 1)
    got = swap(after(sent, first), "fsdp", 1).astype(f32)
    out, d_normed = part[:rows] + got[:rows], d_part[:rows] + got[rows:]
    sums = add_half(halves_of(first, 2), "blk", 2)
    side, none = lax.axis_index("fsdp"), jnp.zeros_like(g_up_bias)
    g_up_bias = jnp.concatenate([jnp.where(side == 0, g_up_bias, none), jnp.where(side == 0, none, g_up_bias)])
    return out, d_normed, first, sums, g_up_bias


def finish_pair(sums, earlier):
    side = lax.axis_index("fsdp")
    sums = after(sums, earlier)
    sums = add_half(halves_of(sums, 2), "ulysses", 1)
    sums = add_half(halves_of(sums, 2), "ulysses", 2)
    got = swap(jnp.where(side == 0, sums[0, 1], sums[0, 0]), "fsdp", 1)
    kept = jnp.where(side == 0, sums[0, 0], sums[0, 1])
    sums = jnp.concatenate([in_order(side, kept[None], got[None]), sums[1]], 0)
    sums = share_half(sums, "ulysses", 2, 1)
    return sums


def spread_pair(sums, near, *earlier):
    mine, other = [], []
    sums = after(sums, near)
    for part in (sums[:2], sums[2:]):
        part = share_half(share_half(part, "ulysses", 1, 1), "blk", 2, 1)
        mine.append(after(part, *earlier))
        other.append(swap(mine[-1], "blk", 1))
    return place_mlp(bit_of("blk", 1), mine, other)


def place_mlp_kernel(which, mine_up, mine_down, other_up, other_down, up_ref, down_ref):
    width = mine_up.shape[-1]
    for c, up, down in ((which[0], mine_up, mine_down), (1 - which[0], other_up, other_down)):
        for f in range(2):
            at = pl.multiple_of((2 * f + c) * width, STRETCH)
            up_ref[:, pl.ds(at, width)] = up[f].astype(f32)
            down_ref[c, f] = down[f].astype(f32)


def place_mlp(which, mine, other):
    _, rows, width = mine[0].shape
    step = rows // 4
    whole = pl.BlockSpec((2, step, width), lambda i, *_: (0, i, 0))
    up, down = pl.pallas_call(
        place_mlp_kernel,
        grid_spec=pltpu.PrefetchScalarGridSpec(
            num_scalar_prefetch=1,
            grid=(4,),
            in_specs=[whole] * 4,
            out_specs=[
                pl.BlockSpec((step, 4 * width), lambda i, *_: (i, 0)),
                pl.BlockSpec((2, 2, step, width), lambda i, *_: (0, 0, i, 0)),
            ],
        ),
        out_shape=[
            jax.ShapeDtypeStruct((rows, 4 * width), f32),
            jax.ShapeDtypeStruct((2, 2, rows, width), f32),
        ],
        compiler_params=pltpu.CompilerParams(vmem_limit_bytes=32 * 2**20),
        cost_estimate=pl.CostEstimate(flops=0, bytes_accessed=24 * mine[0].size, transcendentals=0),
        name="place_mlp",
    )(which[None], *mine, *other)
    return up, down.reshape(4 * rows, width)


def place_qkv_kernel(which, mine, other, qkv_ref, out_ref):
    first = which[0] == 0
    rows, half = mine.shape[1:]
    width = 2 * half
    groups = mine.shape[0] // 4
    for t in range(3):
        blocks = []
        for z in range(groups):
            a, b = mine[3 * z + t], other[3 * z + t]
            blocks += [jnp.where(first, a, b), jnp.where(first, b, a)]
        qkv_ref[:, t * width : (t + 1) * width] = jnp.concatenate(blocks, 0).astype(f32).T
    for z in range(groups // 2):
        for side in range(2):
            a, b = mine[3 * groups + 2 * z + side], other[3 * groups + 2 * z + side]
            at = 2 * z * rows
            both = jnp.concatenate([jnp.where(first, a, b), jnp.where(first, b, a)], 0)
            out_ref[at : at + 2 * rows, side * half : (side + 1) * half] = both.astype(f32)


def place_qkv(which, mine, other):
    _, rows, half = mine.shape
    groups = mine.shape[0] // 4
    return pl.pallas_call(
        place_qkv_kernel,
        grid_spec=pltpu.PrefetchScalarGridSpec(
            num_scalar_prefetch=1,
            grid=(1,),
            in_specs=[pl.BlockSpec(v.shape, lambda i, *_: (0, 0, 0)) for v in (mine, other)],
            out_specs=[
                pl.BlockSpec((half, 6 * half), lambda i, *_: (0, 0)),
                pl.BlockSpec((groups * rows, 2 * half), lambda i, *_: (0, 0)),
            ],
        ),
        out_shape=[
            jax.ShapeDtypeStruct((half, 6 * half), f32),
            jax.ShapeDtypeStruct((groups * rows, 2 * half), f32),
        ],
        compiler_params=pltpu.CompilerParams(vmem_limit_bytes=40 * 2**20),
        cost_estimate=pl.CostEstimate(flops=0, bytes_accessed=12 * mine.size, transcendentals=0),
        name="place_qkv",
    )(which[None], mine, other)


def mlp_gathered(x, e, gain, shift, up, bias, down, *meanwhile):
    normed = layer_norm(x.astype(f32), gain, shift).astype(bf16)
    hidden = jnp.dot(normed, up, preferred_element_type=f32) + bias.astype(f32)
    active_f, pull_gelu = jax.vjp(gelu_exact, hidden)
    active = active_f.astype(bf16)
    out = jnp.dot(active, down, preferred_element_type=f32)
    g_down = jnp.einsum("tf,td->fd", active, e, preferred_element_type=f32)
    d_active = jnp.einsum("td,fd->tf", e, down, preferred_element_type=f32)
    d_hidden = pull_gelu(d_active)[0].astype(bf16)
    g_up = jnp.einsum("td,tf->df", normed, d_hidden, preferred_element_type=f32)
    d_normed = jnp.einsum("tf,df->td", d_hidden, up, preferred_element_type=f32)
    g_up, g_down = (
        lax.psum(
            lax.psum_scatter(g.astype(bf16), "fsdp", scatter_dimension=0, tiled=True),
            ("blk", "ulysses"),
        ).astype(f32)
        for g in (g_up, g_down)
    )
    return out, d_normed, d_hidden, (g_up, g_down), jnp.sum(d_hidden.astype(f32), 0)


def add_blks(grads):
    if lax.axis_size("fsdp") != 2:
        return lax.psum(grads, "blk")
    return add_half(halves_of(add_half(halves_of(grads, 1), "blk", 1), 1), "blk", 2)


def attention_grads(grads, vector, output, g_up):
    side = lax.axis_index("fsdp")
    group = lax.axis_index("ulysses")
    groups = lax.axis_size("ulysses")
    _, rows, width = grads.shape
    if lax.axis_size("fsdp") != 2:
        total = lax.all_gather(lax.psum(grads, "fsdp"), "ulysses", axis=1, tiled=True)
        part = width // lax.axis_size("fsdp")
        g_qkv = lax.dynamic_slice_in_dim(total[:3], side * part, part, 2)
        g_out = lax.dynamic_slice_in_dim(total[3], side * part, part, 0)
        g_qkv = g_qkv.reshape(3 * width, part).T.astype(f32)
        return g_qkv, g_out.astype(f32), sum_everywhere(vector)
    half = width // 2
    size = vector.shape[0]
    small = jnp.pad(vector.astype(bf16), (0, rows * half - size)).reshape(1, rows, half)
    low, high = grads[:, :, :half], grads[:, :, half:]
    kept = jnp.where(side == 0, low[:3], high[:3])
    sent = jnp.where(side == 0, high[:3], low[:3])
    whole = jnp.stack([low[3], high[3]])
    kept = jnp.concatenate([kept, whole, small])
    got = swap(jnp.concatenate([sent, whole, small]), "fsdp", 1)
    kept = (kept.astype(f32) + got.astype(f32)).astype(bf16)
    kept = by_device(around(kept), group)
    small = sum(v[5:].astype(f32) for v in kept).astype(bf16)
    of_qkv = jnp.concatenate([v[:3] for v in kept])
    of_out = [jnp.where(side == 0, a[3:5], b[3:5]) for a, b in zip(kept[: groups // 2], kept[groups // 2 :])]
    kept = jnp.concatenate([of_qkv] + of_out)
    units = kept.shape[0]
    got = after(swap(jnp.concatenate([kept, small]), "blk", 2), output)
    kept = in_order(bit_of("blk", 2), kept, got[:units], 1)
    small = (small.astype(f32) + got[units:].astype(f32)).astype(bf16)
    wide = jnp.pad(small, ((0, 0), (0, rows), (0, 0)))
    got = after(swap(jnp.concatenate([kept, wide]), "blk", 1), g_up)
    small = small.astype(f32) + got[units:, :rows].astype(f32)
    g_qkv, g_out = place_qkv(bit_of("blk", 1), kept, got)
    return g_qkv, g_out, small.reshape(-1)[:size]


def sum_everywhere(values):
    for axis in ("blk", "ulysses", "fsdp"):
        step = 1
        while step < lax.axis_size(axis):
            values = values + swap(values, axis, step)
            step *= 2
    return values


def on_device(
    tokens,
    positions,
    cotangent,
    ln1_gain,
    ln1_bias,
    ln2_gain,
    ln2_bias,
    qkv_weight,
    qkv_bias,
    out_weight,
    out_bias,
    up_weight,
    up_bias,
    down_weight,
    down_bias,
):
    count, width = tokens.shape
    groups = lax.axis_size("ulysses")
    group = lax.axis_index("ulysses")
    shards = lax.axis_size("fsdp")
    cols = width // groups
    heads = cols // HEAD
    rows = count * groups

    ranks = (positions[::STRETCH] // STRETCH).astype(bf16)[None]
    ranks = jnp.pad(ranks, ((0, 15), (0, width - ranks.shape[1])))
    x_ranks = jnp.concatenate([tokens, ranks])
    if shards == 2:
        side = lax.axis_index("fsdp")
        part_qkv = swap(quarter_of(qkv_weight), "fsdp", 1)
        half_up = jnp.concatenate([units_of(up_weight, 1 - side), out_weight], 1)
        part_up = swap(after(quarter_of(half_up), part_qkv), "fsdp", 1)
        x_e = swap(after(jnp.stack([tokens, cotangent]), part_up), "fsdp", 1)
        w_qkv = both_shards(qkv_weight, share_half(part_qkv, "blk", 2, 0))
        half_up = share_half(part_up, "blk", 2, 0)
        x_all = around(x_ranks)
        mine = jnp.concatenate([units_of(up_weight, side), out_weight], 1)
        half_up = both_shards(mine, half_up)
        w_up, w_out = half_up[:, :-width], half_up[:, -width:]
        x_mlp = jnp.concatenate([tokens, x_e[0]])
        e_mlp = jnp.concatenate([cotangent, x_e[1]])
        b_up, w_down = up_bias, down_weight
        mlp, finish, spread = mlp_pair, finish_pair, spread_pair
    else:
        x_all, part_qkv = around(x_ranks), x_ranks
        w_qkv, w_up, w_out, w_down = (
            lax.all_gather(w, "fsdp", axis=0, tiled=True)
            for w in (qkv_weight, up_weight, out_weight, down_weight)
        )
        b_up = gather_small(up_bias).reshape(-1)
        x_mlp, e_mlp = tokens, cotangent
        mlp, finish, spread = mlp_gathered, lambda v, _: v, lambda v, *_: v
    small = jnp.concatenate([ln1_gain, ln1_bias, ln2_gain, ln2_bias, out_bias, down_bias, qkv_bias])
    small = gather_small(after(small, part_qkv))
    part = width // shards
    ln1_g, ln1_b, ln2_g, ln2_b, b_out, b_down = (
        small[:, i * part : (i + 1) * part].reshape(width).astype(f32) for i in range(6)
    )
    b_qkv = small[:, 6 * part :].reshape(3 * width).astype(f32)
    starts = [i * width + group * cols for i in range(3)]
    w_mine = jnp.concatenate([lax.dynamic_slice_in_dim(w_qkv, v, cols, 1) for v in starts], 1)
    b_mine = jnp.concatenate([lax.dynamic_slice_in_dim(b_qkv, v, cols, 0) for v in starts])
    x_all = after(x_all, w_mine)
    normed, queries, kv, cosine, sine = prepare(ln1_g, ln1_b, w_mine, b_mine, x_all, count)
    queries = queries.reshape(heads, HEAD, rows)
    pieces = {0: kv}
    step = lax.axis_size("blk") // 2
    while step >= 1:
        for i in list(pieces):
            pieces[i ^ step] = swap(pieces[i], "blk", step)
        step //= 2
    kv_all = [pieces[i] for i in range(len(pieces))]
    ranks = jnp.concatenate([v[2 * cols, : rows // STRETCH] for v in kv_all]).astype(jnp.int32)

    d_mixed = jnp.einsum("ed,td->et", w_out, after(cotangent, kv), preferred_element_type=f32).astype(bf16)
    d_heads = [lax.dynamic_slice_in_dim(d_mixed, (group ^ j) * cols, cols) for j in range(groups)]
    d_heads = [d_heads[0]] + [swap(d_heads[j], "ulysses", j) for j in range(1, groups)]
    d_heads = jnp.concatenate(d_heads, 1).reshape(heads, HEAD, rows)

    x_mlp, w_up = after((x_mlp, w_up), kv, d_mixed)
    mlp_out, d_norm_two, begun, terms, g_up_bias = mlp(
        x_mlp, e_mlp, ln2_g, ln2_b, w_up, b_up, w_down, pieces[lax.axis_size("blk") // 2], pieces[1], d_heads
    )

    e_around = around(after(cotangent, begun))
    d_heads = after(d_heads, begun)
    mixed, d_q, kept, sent = attend(ranks, queries, d_heads, kv_all)

    sent, e_around, terms, mlp_out, d_norm_two = after((sent, e_around, terms, mlp_out, d_norm_two))
    d_q = rotate(d_q, cosine, -sine).astype(bf16).reshape(cols, rows)
    mixed = mixed.reshape(cols, rows)
    back_q = to_tokens(jnp.concatenate([d_q, mixed]))
    got = swap(sent, "blk", 1)
    step, kept = 1, [[kept[i], got[i]] for i in range(kept.shape[0])]
    while len(kept) > 1:
        step *= 2
        sent = sum(v.astype(f32) for v in stacked_terms(kept[1::2])).astype(bf16)
        if step == 2:
            terms = finish(terms, sent)
        sent, back_q = after((sent, back_q))
        got = swap(sent, "blk", step)
        kept = [kept[2 * i] + [got[i]] for i in range(got.shape[0])]
    total = sum(v.astype(f32) for v in kept[0])
    e_all = jnp.concatenate(e_around, 0)
    g_out = jnp.dot(mixed, e_all, preferred_element_type=f32).astype(bf16)
    d_k = rotate(total[:cols].reshape(heads, HEAD, rows), cosine, -sine).reshape(cols, rows)
    d_kv = jnp.concatenate([d_k, total[cols:]]).astype(bf16)
    d_joined = jnp.concatenate([d_q, d_kv])
    g_bias_mine = jnp.sum(d_joined.astype(f32), 1)
    g_qkv = jnp.dot(d_joined, normed, preferred_element_type=f32).astype(bf16)
    back_kv = to_tokens(d_kv)
    grads = jnp.concatenate([g_qkv.reshape(3, cols, width), g_out[None]])
    grads = add_blks(grads)
    back_kv = after(back_kv, grads)
    back_q, back_kv = by_device(back_q, group), by_device(back_kv, group)
    d_mine = jnp.concatenate(
        [v[:cols] for v in back_q] + [v[:cols] for v in back_kv] + [v[cols:] for v in back_kv], 0
    )
    d_norm_one = jnp.einsum("et,de->td", d_mine, w_qkv, preferred_element_type=f32)
    x_float = tokens.astype(f32)
    _, pull_one = jax.vjp(layer_norm, x_float, ln1_g, ln1_b)
    _, pull_two = jax.vjp(layer_norm, x_float, ln2_g, ln2_b)
    d_x_one, g_ln1_g, g_ln1_b = pull_one(d_norm_one)
    d_x_two, g_ln2_g, g_ln2_b = pull_two(d_norm_two)
    e_float = cotangent.astype(f32)

    g_qkv_bias = jnp.zeros((3, groups, cols), f32)
    g_qkv_bias = lax.dynamic_update_slice(g_qkv_bias, g_bias_mine.reshape(3, 1, cols), (0, group, 0))
    vectors = [g_ln1_g, g_ln1_b, g_ln2_g, g_ln2_b, jnp.sum(e_float, 0), g_qkv_bias.reshape(-1), g_up_bias]
    back = jnp.concatenate([v[cols:] for v in back_q], 0)
    attn_out = jnp.einsum("et,ed->td", back, w_out, preferred_element_type=f32)
    output = (x_float + (attn_out + b_out) + (mlp_out + b_down)).astype(bf16)
    input_grad = (e_float + d_x_one + d_x_two).astype(bf16)

    vector = jnp.concatenate(vectors)
    g_up, g_down = spread(terms, vector, output, input_grad)
    g_qkv, g_out, summed = attention_grads(grads, vector, output, g_up)
    results, start = [], 0
    for vector in vectors:
        mine = vector.shape[0] // shards
        results.append(lax.dynamic_slice_in_dim(summed, start + lax.axis_index("fsdp") * mine, mine))
        start += vector.shape[0]
    g_ln1_g, g_ln1_b, g_ln2_g, g_ln2_b, g_e, g_qkv_bias, g_up_bias = results
    return (
        output,
        input_grad,
        g_ln1_g,
        g_ln1_b,
        g_ln2_g,
        g_ln2_b,
        g_qkv,
        g_qkv_bias,
        g_out,
        g_e,
        g_up,
        g_up_bias,
        g_down,
        g_e,
    )


def solution(mesh):
    rows = P(("fsdp", "blk", "ulysses"), None)
    split, matrix = P("fsdp"), P("fsdp", None)
    return jax.shard_map(
        on_device,
        mesh=mesh,
        in_specs=(
            rows,
            P(("fsdp", "blk", "ulysses")),
            rows,
            split,
            split,
            split,
            split,
            matrix,
            split,
            matrix,
            split,
            matrix,
            split,
            matrix,
            split,
        ),
        out_specs=(
            rows,
            rows,
            split,
            split,
            split,
            split,
            matrix,
            split,
            matrix,
            split,
            matrix,
            split,
            matrix,
            split,
        ),
        check_vma=False,
    )
```

```python
import jax
import jax.numpy as jnp
import numpy as np
from jax import lax
from jax.experimental import pallas as pl
from jax.experimental.pallas import tpu as pltpu
from jax.sharding import PartitionSpec as P

HEAD = 64
ROT = 16
STRETCH = 128
CHUNK = 8
BIG_NEG = -1e30

f32 = jnp.float32
bf16 = jnp.bfloat16


def layer_norm(values, gain, shift):
    center = jnp.mean(values, -1, keepdims=True)
    offset = values - center
    spread = jnp.mean(offset * offset, -1, keepdims=True)
    return offset * lax.rsqrt(spread + 1e-05) * gain + shift


def gelu_exact(values):
    return jax.nn.gelu(values, approximate=False)


def swap(values, axis, bits):
    count = lax.axis_size(axis)
    return lax.ppermute(values, axis, [(i, i ^ bits) for i in range(count)])


def after(values, *earlier):
    return lax.optimization_barrier((values, earlier))[0]


def bit_of(axis, bit):
    return (lax.axis_index(axis) // bit) % 2


def in_order(bit, mine, other, axis=0):
    return jnp.concatenate([jnp.where(bit == 0, mine, other), jnp.where(bit == 0, other, mine)], axis)


def by_device(pieces, index):
    step = 1
    while step < len(pieces):
        odd = (index // step) % 2 == 1
        pieces = [jnp.where(odd, pieces[i ^ step], pieces[i]) for i in range(len(pieces))]
        step *= 2
    return pieces


def add_half(halves, axis, bit):
    which = bit_of(axis, bit)
    got = swap(jnp.where(which == 0, halves[1], halves[0]), axis, bit)
    kept = jnp.where(which == 0, halves[0], halves[1])
    return (kept.astype(f32) + got.astype(f32)).astype(bf16)


def halves_of(values, axis):
    half = values.shape[axis] // 2
    return (
        lax.slice_in_dim(values, 0, half, axis=axis),
        lax.slice_in_dim(values, half, 2 * half, axis=axis),
    )


def share_half(values, axis, bit, dim):
    return in_order(bit_of(axis, bit), values, swap(values, axis, bit), dim)


def gather_small(shard):
    if lax.axis_size("fsdp") != 2:
        return lax.all_gather(shard[None], "fsdp", axis=0, tiled=True)
    return in_order(lax.axis_index("fsdp"), shard[None], swap(shard[None], "fsdp", 1))


def quarter_of(shard):
    quarter = shard.shape[0] // 4
    place = bit_of("blk", 1) * 2 + bit_of("blk", 2)
    return lax.dynamic_slice_in_dim(shard, place * quarter, quarter)


def both_shards(shard, half):
    return in_order(lax.axis_index("fsdp"), shard, share_half(half, "blk", 1, 0))


def attend_kernel(rank, q_ref, g_ref, *refs):
    kv_refs = refs[:-9]
    o_ref, dq_ref, keep_ref, send_ref, rows, lanes, sums, probs, order = refs[-9:]
    heads = range(q_ref.shape[0])
    cols = q_ref.shape[0] * HEAD
    n_keys = rank.shape[0]
    own = q_ref.shape[-1] // STRETCH
    wide = 2 * STRETCH
    span = CHUNK * STRETCH

    for t in range(n_keys):
        i, at = t // own, (t % own) * STRETCH
        place = rank[t]
        for h in heads:
            both = jnp.concatenate(
                [
                    kv_refs[i][first : first + HEAD, at : at + STRETCH]
                    for first in (h * HEAD, cols + h * HEAD)
                ],
                0,
            )
            lanes[h, place] = both
            rows[h, place] = both.T
            sums[h, t] = jnp.zeros((STRETCH, 2 * HEAD), f32)
    for a in range(own):
        before = jnp.int32(0)
        for b in range(own):
            before += (rank[b] < rank[a]).astype(jnp.int32)
        order[before] = a

    def side(h, j, part):
        first = part * HEAD
        return jnp.concatenate(
            [lanes[h, j * CHUNK + i, first : first + HEAD, :] for i in range(CHUNK)], 1
        )

    def keys(h, j):
        return rows[h, pl.ds(j * CHUNK, CHUNK)].reshape(span, 2 * HEAD)

    def pair(p, carry):
        a, b = order[2 * p], order[2 * p + 1]
        ra, rb = rank[a], rank[b]
        at_a = pl.ds(pl.multiple_of(a * STRETCH, STRETCH), STRETCH)
        at_b = pl.ds(pl.multiple_of(b * STRETCH, STRETCH), STRETCH)
        q = [jnp.concatenate([q_ref[h, :, at_a], q_ref[h, :, at_b]], 1) for h in heads]
        g = [jnp.concatenate([g_ref[h, :, at_a], g_ref[h, :, at_b]], 1) for h in heads]
        none = jnp.zeros_like(q[0])
        q_low = [jnp.concatenate([v, none], 0) for v in q]
        g_high = [jnp.concatenate([none, v], 0) for v in g]
        lane = lax.broadcasted_iota(jnp.int32, (1, wide), 1)
        q_place = jnp.where(lane < STRETCH, ra * STRETCH + lane, rb * STRETCH + lane - STRETCH)
        clear = ra // CHUNK
        total = (rb + CHUNK) // CHUNK

        def score(j, tops, masked):
            result = []
            for h in heads:
                s = jnp.dot(keys(h, j), q_low[h], preferred_element_type=f32)
                if masked:
                    k_place = j * span + lax.broadcasted_iota(jnp.int32, (span, 1), 0)
                    s = jnp.where(k_place <= q_place, s, BIG_NEG)
                probs[h, j] = s
                result.append(jnp.maximum(tops[h], jnp.max(s.reshape(span // 8, 8, wide), 0)))
            return tuple(result)

        tops = tuple(jnp.full((8, wide), BIG_NEG, f32) for _ in heads)
        tops = lax.fori_loop(0, clear, lambda j, v: score(j, v, False), tops)
        tops = lax.fori_loop(clear, total, lambda j, v: score(j, v, True), tops)
        tops = [jnp.max(v, 0, keepdims=True) for v in tops]

        def weigh(j, state):
            result = []
            for h in heads:
                count, out = state[h]
                weight = jnp.exp(probs[h, j] - tops[h])
                probs[h, j] = weight
                count = count + jnp.sum(weight.reshape(span // 8, 8, wide), 0)
                out = out + jnp.dot(side(h, j, 1), weight.astype(bf16), preferred_element_type=f32)
                result.append((count, out))
            return tuple(result)

        state = tuple((jnp.zeros((8, wide), f32), jnp.zeros((HEAD, wide), f32)) for _ in heads)
        state = lax.fori_loop(0, total, weigh, state)
        inverse, delta, right = [], [], []
        for h in heads:
            count, out = state[h]
            inverse.append(1.0 / jnp.sum(count, 0, keepdims=True))
            out = out * inverse[h]
            delta.append(jnp.sum(out * g[h].astype(f32), 0, keepdims=True))
            o_ref[h, :, at_a] = out[:, :STRETCH].astype(bf16)
            o_ref[h, :, at_b] = out[:, STRETCH:].astype(bf16)
            top = jnp.concatenate([g[h], none], 0).T
            right.append(jnp.concatenate([top, jnp.concatenate([none, q[h]], 0).T], 0))

        def back(j, d_q):
            result = []
            for h in heads:
                weight = probs[h, j] * inverse[h]
                d_weight = jnp.dot(keys(h, j), g_high[h], preferred_element_type=f32)
                d_score = (weight * (d_weight - delta[h])).astype(bf16)
                left = jnp.concatenate([weight.astype(bf16), d_score], 1)
                sums[h, pl.ds(j * CHUNK, CHUNK)] += jnp.dot(
                    left, right[h], preferred_element_type=f32
                ).reshape(CHUNK, STRETCH, 2 * HEAD)
                result.append(d_q[h] + jnp.dot(side(h, j, 0), d_score, preferred_element_type=f32))
            return tuple(result)

        d_q = lax.fori_loop(0, total, back, tuple(jnp.zeros((HEAD, wide), f32) for _ in heads))
        for h in heads:
            scaled = d_q[h] * HEAD ** (-0.5)
            dq_ref[h, :, at_a] = scaled[:, :STRETCH]
            dq_ref[h, :, at_b] = scaled[:, STRETCH:]
        return carry

    lax.fori_loop(0, own // 2, pair, 0)
    for t in range(n_keys):
        i, at = t // own, (t % own) * STRETCH
        to = keep_ref if i % 2 == 0 else send_ref
        for h in heads:
            turned = sums[h, rank[t]].astype(bf16).T
            first = h * HEAD
            to[i // 2, cols + first : cols + first + HEAD, at : at + STRETCH] = turned[:HEAD]
            to[i // 2, first : first + HEAD, at : at + STRETCH] = turned[HEAD:]


def attend(ranks, q, g, kv):
    heads, _, count = q.shape
    devices = len(kv)
    n_keys = devices * count // STRETCH
    pairs = heads * 4 * HEAD * count * count * devices
    half = (devices // 2, 2 * heads * HEAD, count)
    q_spec = pl.BlockSpec(q.shape, lambda i, *_: (0, 0, 0))
    half_spec = pl.BlockSpec(half, lambda i, *_: (0, 0, 0))
    return pl.pallas_call(
        attend_kernel,
        grid_spec=pltpu.PrefetchScalarGridSpec(
            num_scalar_prefetch=1,
            grid=(1,),
            in_specs=[q_spec, q_spec] + [pl.BlockSpec(v.shape, lambda i, *_: (0, 0)) for v in kv],
            out_specs=[q_spec, q_spec, half_spec, half_spec],
            scratch_shapes=[
                pltpu.VMEM((heads, n_keys, STRETCH, 2 * HEAD), bf16),
                pltpu.VMEM((heads, n_keys, 2 * HEAD, STRETCH), bf16),
                pltpu.VMEM((heads, n_keys, STRETCH, 2 * HEAD), f32),
                pltpu.VMEM((heads, n_keys // CHUNK, CHUNK * STRETCH, 2 * STRETCH), f32),
                pltpu.SMEM((count // STRETCH,), jnp.int32),
            ],
        ),
        out_shape=[
            jax.ShapeDtypeStruct(q.shape, bf16),
            jax.ShapeDtypeStruct(q.shape, f32),
            jax.ShapeDtypeStruct(half, bf16),
            jax.ShapeDtypeStruct(half, bf16),
        ],
        compiler_params=pltpu.CompilerParams(vmem_limit_bytes=56 * 2**20),
        cost_estimate=pl.CostEstimate(
            flops=12 * pairs, bytes_accessed=16 * q.size * devices, transcendentals=pairs // 512
        ),
        name="attend",
    )(ranks, q, g, *kv)


def prepare_kernel(freqs, gain, shift, weight, bias, *refs):
    groups = len(refs) - 5
    x_refs = refs[:groups]
    normed_ref, q_ref, kv_ref, cos_ref, sin_ref = refs[groups:]
    count = normed_ref.shape[0] // groups
    cols = q_ref.shape[0]
    halfway = ROT // 2
    blocks = count // STRETCH
    lane = lax.broadcasted_iota(jnp.int32, (1, STRETCH), 1).astype(f32)
    kv_ref[2 * cols :, :] = jnp.zeros((kv_ref.shape[0] - 2 * cols, kv_ref.shape[1]), bf16)
    spots = lax.broadcasted_iota(jnp.int32, (1, STRETCH), 1)
    table = jnp.zeros((1, STRETCH), f32)
    for i, x_ref in enumerate(x_refs):
        at = i * count
        normed = layer_norm(x_ref[:count].astype(f32), gain[...], shift[...]).astype(bf16)
        normed_ref[at : at + count] = normed
        joined = jnp.dot(normed, weight[...], preferred_element_type=f32) + bias[...]
        joined = joined.T
        ranks = x_ref[count : count + 16, :STRETCH].astype(f32)[:1]
        places = []
        for b in range(blocks):
            rank = jnp.sum(jnp.where(spots == b, ranks, 0.0), 1, keepdims=True)
            places.append(rank * STRETCH + lane)
            table = jnp.where(spots == i * blocks + b, rank, table)
        angles = freqs[...] * jnp.concatenate(places, 1)
        cosine, sine = jnp.cos(angles), jnp.sin(angles)
        cos_ref[:, at : at + count] = cosine
        sin_ref[:, at : at + count] = sine
        for to, first, scale in ((q_ref, 0, HEAD ** (-0.5)), (kv_ref, cols, 1.0)):
            for h in range(cols // HEAD):
                low = first + h * HEAD
                one = joined[low : low + halfway]
                two = joined[low + halfway : low + ROT]
                rest = joined[low + ROT : low + HEAD]
                turned = jnp.concatenate(
                    [one * cosine - two * sine, two * cosine + one * sine, rest], 0
                ).astype(bf16)
                to[h * HEAD : (h + 1) * HEAD, at : at + count] = turned * jnp.bfloat16(scale)
        kv_ref[cols : 2 * cols, at : at + count] = joined[2 * cols :].astype(bf16)
    kv_ref[2 * cols :, :STRETCH] = jnp.broadcast_to(table, (16, STRETCH)).astype(bf16)


def prepare(gain, shift, weight, bias, x_all, count):
    width = weight.shape[0]
    cols = weight.shape[1] // 3
    rows = count * len(x_all)
    halfway = ROT // 2
    freqs = jnp.asarray(10000.0 ** (-np.arange(halfway) * 2.0 / ROT), f32)[:, None]
    return pl.pallas_call(
        prepare_kernel,
        out_shape=[
            jax.ShapeDtypeStruct((rows, width), bf16),
            jax.ShapeDtypeStruct((cols, rows), bf16),
            jax.ShapeDtypeStruct((2 * cols + 16, rows), bf16),
            jax.ShapeDtypeStruct((ROT // 2, rows), f32),
            jax.ShapeDtypeStruct((ROT // 2, rows), f32),
        ],
        compiler_params=pltpu.CompilerParams(vmem_limit_bytes=40 * 2**20),
        cost_estimate=pl.CostEstimate(
            flops=6 * cols * rows * width, bytes_accessed=8 * rows * width, transcendentals=0
        ),
        name="prepare",
    )(freqs, gain[None], shift[None], weight, bias[None], *x_all)


def rotate(heads, cosine, sine):
    halfway = ROT // 2
    first = heads[:, :halfway]
    second = heads[:, halfway:ROT]
    return jnp.concatenate(
        [first * cosine - second * sine, second * cosine + first * sine, heads[:, ROT:]], 1
    )


def around(values):
    return [values] + [swap(values, "ulysses", j) for j in range(1, lax.axis_size("ulysses"))]


def stacked_terms(lists):
    return [jnp.stack(v) for v in zip(*lists)]


def to_tokens(values):
    groups = lax.axis_size("ulysses")
    count = values.shape[1] // groups
    pieces = [values[:, j * count : (j + 1) * count] for j in range(groups)]
    return [pieces[0]] + [swap(pieces[j], "ulysses", j) for j in range(1, groups)]


def units_of(up_weight, side):
    units = up_weight.shape[1] // 2
    return jnp.where(side == 0, up_weight[:, :units], up_weight[:, units:])


def mlp_pair(x_both, e_both, gain, shift, up, up_bias, down_weight, *meanwhile):
    side = lax.axis_index("fsdp")
    rows, width = x_both.shape[0] // 2, x_both.shape[1]
    units = up.shape[1]
    normed = layer_norm(x_both.astype(f32), gain, shift).astype(bf16)
    hidden = jnp.dot(normed, up, preferred_element_type=f32) + up_bias.astype(f32)
    active_f, pull_gelu = jax.vjp(gelu_exact, hidden)
    active = active_f.astype(bf16)
    part = jnp.dot(active, down_weight, preferred_element_type=f32)
    d_active = jnp.einsum("td,fd->tf", e_both, down_weight, preferred_element_type=f32)
    d_hidden = pull_gelu(d_active)[0].astype(bf16)
    g_up_bias = jnp.sum(d_hidden.astype(f32), 0)
    d_part = jnp.einsum("tf,df->td", d_hidden, up, preferred_element_type=f32)
    sent = jnp.concatenate([part[rows:], d_part[rows:]]).astype(bf16)
    active, d_hidden = after((active, d_hidden), *meanwhile)
    g_up = jnp.einsum(
        "td,tcf->cdf", normed, d_hidden.reshape(2 * rows, 2, units // 2), preferred_element_type=f32
    ).astype(bf16)
    g_down = jnp.einsum("tf,td->fd", active, e_both, preferred_element_type=f32).astype(bf16)
    g_down = g_down.reshape(2, units // 2, width)
    pieces = jnp.stack([g_up, g_down], 1).reshape(2, 2, 2, width // 2, width)
    first = add_half((pieces[0], pieces[1]), "blk", 1)
    got = swap(after(sent, first), "fsdp", 1).astype(f32)
    out, d_normed = part[:rows] + got[:rows], d_part[:rows] + got[rows:]
    sums = add_half(halves_of(first, 2), "blk", 2)
    side, none = lax.axis_index("fsdp"), jnp.zeros_like(g_up_bias)
    g_up_bias = jnp.concatenate([jnp.where(side == 0, g_up_bias, none), jnp.where(side == 0, none, g_up_bias)])
    return out, d_normed, first, sums, g_up_bias


def finish_pair(sums, earlier):
    side = lax.axis_index("fsdp")
    sums = after(sums, earlier)
    sums = add_half(halves_of(sums, 2), "ulysses", 1)
    sums = add_half(halves_of(sums, 2), "ulysses", 2)
    got = swap(jnp.where(side == 0, sums[0, 1], sums[0, 0]), "fsdp", 1)
    kept = jnp.where(side == 0, sums[0, 0], sums[0, 1])
    sums = jnp.concatenate([in_order(side, kept[None], got[None]), sums[1]], 0)
    sums = share_half(sums, "ulysses", 2, 1)
    return sums


def spread_pair(sums, *earlier):
    mine, other = [], []
    for part in (sums[:2], sums[2:]):
        part = share_half(share_half(part, "ulysses", 1, 1), "blk", 2, 1)
        mine.append(after(part, *earlier))
        other.append(swap(mine[-1], "blk", 1))
    return place_mlp(bit_of("blk", 1), mine, other)


def place_mlp_kernel(which, mine_up, mine_down, other_up, other_down, up_ref, down_ref):
    width = mine_up.shape[-1]
    for c, up, down in ((which[0], mine_up, mine_down), (1 - which[0], other_up, other_down)):
        for f in range(2):
            at = pl.multiple_of((2 * f + c) * width, STRETCH)
            up_ref[:, pl.ds(at, width)] = up[f].astype(f32)
            down_ref[c, f] = down[f].astype(f32)


def place_mlp(which, mine, other):
    _, rows, width = mine[0].shape
    step = rows // 4
    whole = pl.BlockSpec((2, step, width), lambda i, *_: (0, i, 0))
    up, down = pl.pallas_call(
        place_mlp_kernel,
        grid_spec=pltpu.PrefetchScalarGridSpec(
            num_scalar_prefetch=1,
            grid=(4,),
            in_specs=[whole] * 4,
            out_specs=[
                pl.BlockSpec((step, 4 * width), lambda i, *_: (i, 0)),
                pl.BlockSpec((2, 2, step, width), lambda i, *_: (0, 0, i, 0)),
            ],
        ),
        out_shape=[
            jax.ShapeDtypeStruct((rows, 4 * width), f32),
            jax.ShapeDtypeStruct((2, 2, rows, width), f32),
        ],
        compiler_params=pltpu.CompilerParams(vmem_limit_bytes=32 * 2**20),
        cost_estimate=pl.CostEstimate(flops=0, bytes_accessed=24 * mine[0].size, transcendentals=0),
        name="place_mlp",
    )(which[None], *mine, *other)
    return up, down.reshape(4 * rows, width)


def place_qkv_kernel(which, mine, other, qkv_ref, out_ref):
    first = which[0] == 0
    rows, half = mine.shape[1:]
    width = 2 * half
    groups = mine.shape[0] // 4
    for t in range(3):
        blocks = []
        for z in range(groups):
            a, b = mine[3 * z + t], other[3 * z + t]
            blocks += [jnp.where(first, a, b), jnp.where(first, b, a)]
        qkv_ref[:, t * width : (t + 1) * width] = jnp.concatenate(blocks, 0).astype(f32).T
    for z in range(groups // 2):
        for side in range(2):
            a, b = mine[3 * groups + 2 * z + side], other[3 * groups + 2 * z + side]
            at = 2 * z * rows
            both = jnp.concatenate([jnp.where(first, a, b), jnp.where(first, b, a)], 0)
            out_ref[at : at + 2 * rows, side * half : (side + 1) * half] = both.astype(f32)


def place_qkv(which, mine, other):
    _, rows, half = mine.shape
    groups = mine.shape[0] // 4
    return pl.pallas_call(
        place_qkv_kernel,
        grid_spec=pltpu.PrefetchScalarGridSpec(
            num_scalar_prefetch=1,
            grid=(1,),
            in_specs=[pl.BlockSpec(v.shape, lambda i, *_: (0, 0, 0)) for v in (mine, other)],
            out_specs=[
                pl.BlockSpec((half, 6 * half), lambda i, *_: (0, 0)),
                pl.BlockSpec((groups * rows, 2 * half), lambda i, *_: (0, 0)),
            ],
        ),
        out_shape=[
            jax.ShapeDtypeStruct((half, 6 * half), f32),
            jax.ShapeDtypeStruct((groups * rows, 2 * half), f32),
        ],
        compiler_params=pltpu.CompilerParams(vmem_limit_bytes=40 * 2**20),
        cost_estimate=pl.CostEstimate(flops=0, bytes_accessed=12 * mine.size, transcendentals=0),
        name="place_qkv",
    )(which[None], mine, other)


def mlp_gathered(x, e, gain, shift, up, bias, down, *meanwhile):
    normed = layer_norm(x.astype(f32), gain, shift).astype(bf16)
    hidden = jnp.dot(normed, up, preferred_element_type=f32) + bias.astype(f32)
    active_f, pull_gelu = jax.vjp(gelu_exact, hidden)
    active = active_f.astype(bf16)
    out = jnp.dot(active, down, preferred_element_type=f32)
    g_down = jnp.einsum("tf,td->fd", active, e, preferred_element_type=f32)
    d_active = jnp.einsum("td,fd->tf", e, down, preferred_element_type=f32)
    d_hidden = pull_gelu(d_active)[0].astype(bf16)
    g_up = jnp.einsum("td,tf->df", normed, d_hidden, preferred_element_type=f32)
    d_normed = jnp.einsum("tf,df->td", d_hidden, up, preferred_element_type=f32)
    g_up, g_down = (
        lax.psum(
            lax.psum_scatter(g.astype(bf16), "fsdp", scatter_dimension=0, tiled=True),
            ("blk", "ulysses"),
        ).astype(f32)
        for g in (g_up, g_down)
    )
    return out, d_normed, d_hidden, (g_up, g_down), jnp.sum(d_hidden.astype(f32), 0)


def add_blks(grads):
    if lax.axis_size("fsdp") != 2:
        return lax.psum(grads, "blk")
    return add_half(halves_of(add_half(halves_of(grads, 1), "blk", 1), 1), "blk", 2)


def attention_grads(grads, vector, output, g_up):
    side = lax.axis_index("fsdp")
    group = lax.axis_index("ulysses")
    groups = lax.axis_size("ulysses")
    _, rows, width = grads.shape
    if lax.axis_size("fsdp") != 2:
        total = lax.all_gather(lax.psum(grads, "fsdp"), "ulysses", axis=1, tiled=True)
        part = width // lax.axis_size("fsdp")
        g_qkv = lax.dynamic_slice_in_dim(total[:3], side * part, part, 2)
        g_out = lax.dynamic_slice_in_dim(total[3], side * part, part, 0)
        g_qkv = g_qkv.reshape(3 * width, part).T.astype(f32)
        return g_qkv, g_out.astype(f32), sum_everywhere(vector)
    half = width // 2
    size = vector.shape[0]
    small = jnp.pad(vector.astype(bf16), (0, rows * half - size)).reshape(1, rows, half)
    low, high = grads[:, :, :half], grads[:, :, half:]
    kept = jnp.where(side == 0, low[:3], high[:3])
    sent = jnp.where(side == 0, high[:3], low[:3])
    whole = jnp.stack([low[3], high[3]])
    kept = jnp.concatenate([kept, whole, small])
    got = swap(jnp.concatenate([sent, whole, small]), "fsdp", 1)
    kept = (kept.astype(f32) + got.astype(f32)).astype(bf16)
    kept = by_device(around(kept), group)
    small = sum(v[5:].astype(f32) for v in kept).astype(bf16)
    of_qkv = jnp.concatenate([v[:3] for v in kept])
    of_out = [jnp.where(side == 0, a[3:5], b[3:5]) for a, b in zip(kept[: groups // 2], kept[groups // 2 :])]
    kept = jnp.concatenate([of_qkv] + of_out)
    units = kept.shape[0]
    got = after(swap(jnp.concatenate([kept, small]), "blk", 2), output)
    kept = in_order(bit_of("blk", 2), kept, got[:units], 1)
    small = (small.astype(f32) + got[units:].astype(f32)).astype(bf16)
    wide = jnp.pad(small, ((0, 0), (0, rows), (0, 0)))
    got = after(swap(jnp.concatenate([kept, wide]), "blk", 1), g_up)
    small = small.astype(f32) + got[units:, :rows].astype(f32)
    g_qkv, g_out = place_qkv(bit_of("blk", 1), kept, got)
    return g_qkv, g_out, small.reshape(-1)[:size]


def sum_everywhere(values):
    for axis in ("blk", "ulysses", "fsdp"):
        step = 1
        while step < lax.axis_size(axis):
            values = values + swap(values, axis, step)
            step *= 2
    return values


def on_device(
    tokens,
    positions,
    cotangent,
    ln1_gain,
    ln1_bias,
    ln2_gain,
    ln2_bias,
    qkv_weight,
    qkv_bias,
    out_weight,
    out_bias,
    up_weight,
    up_bias,
    down_weight,
    down_bias,
):
    count, width = tokens.shape
    groups = lax.axis_size("ulysses")
    group = lax.axis_index("ulysses")
    shards = lax.axis_size("fsdp")
    cols = width // groups
    heads = cols // HEAD
    rows = count * groups

    ranks = (positions[::STRETCH] // STRETCH).astype(bf16)[None]
    ranks = jnp.pad(ranks, ((0, 15), (0, width - ranks.shape[1])))
    x_ranks = jnp.concatenate([tokens, ranks])
    if shards == 2:
        side = lax.axis_index("fsdp")
        part_qkv = swap(quarter_of(qkv_weight), "fsdp", 1)
        half_up = jnp.concatenate([units_of(up_weight, 1 - side), out_weight], 1)
        part_up = swap(after(quarter_of(half_up), part_qkv), "fsdp", 1)
        x_e = swap(after(jnp.stack([tokens, cotangent]), part_up), "fsdp", 1)
        w_qkv = both_shards(qkv_weight, share_half(part_qkv, "blk", 2, 0))
        half_up = share_half(part_up, "blk", 2, 0)
        x_all = around(x_ranks)
        mine = jnp.concatenate([units_of(up_weight, side), out_weight], 1)
        half_up = both_shards(mine, half_up)
        w_up, w_out = half_up[:, :-width], half_up[:, -width:]
        x_mlp = jnp.concatenate([tokens, x_e[0]])
        e_mlp = jnp.concatenate([cotangent, x_e[1]])
        b_up, w_down = up_bias, down_weight
        mlp, finish, spread = mlp_pair, finish_pair, spread_pair
    else:
        x_all, part_qkv = around(x_ranks), x_ranks
        w_qkv, w_up, w_out, w_down = (
            lax.all_gather(w, "fsdp", axis=0, tiled=True)
            for w in (qkv_weight, up_weight, out_weight, down_weight)
        )
        b_up = gather_small(up_bias).reshape(-1)
        x_mlp, e_mlp = tokens, cotangent
        mlp, finish, spread = mlp_gathered, lambda v, _: v, lambda v, *_: v
    small = jnp.concatenate([ln1_gain, ln1_bias, ln2_gain, ln2_bias, out_bias, down_bias, qkv_bias])
    small = gather_small(after(small, part_qkv))
    part = width // shards
    ln1_g, ln1_b, ln2_g, ln2_b, b_out, b_down = (
        small[:, i * part : (i + 1) * part].reshape(width).astype(f32) for i in range(6)
    )
    b_qkv = small[:, 6 * part :].reshape(3 * width).astype(f32)
    starts = [i * width + group * cols for i in range(3)]
    w_mine = jnp.concatenate([lax.dynamic_slice_in_dim(w_qkv, v, cols, 1) for v in starts], 1)
    b_mine = jnp.concatenate([lax.dynamic_slice_in_dim(b_qkv, v, cols, 0) for v in starts])
    x_all = after(x_all, w_mine)
    normed, queries, kv, cosine, sine = prepare(ln1_g, ln1_b, w_mine, b_mine, x_all, count)
    queries = queries.reshape(heads, HEAD, rows)
    pieces = {0: kv}
    step = lax.axis_size("blk") // 2
    while step >= 1:
        for i in list(pieces):
            pieces[i ^ step] = swap(pieces[i], "blk", step)
        step //= 2
    kv_all = [pieces[i] for i in range(len(pieces))]
    ranks = jnp.concatenate([v[2 * cols, : rows // STRETCH] for v in kv_all]).astype(jnp.int32)

    d_mixed = jnp.einsum("ed,td->et", w_out, after(cotangent, kv), preferred_element_type=f32).astype(bf16)
    d_heads = [lax.dynamic_slice_in_dim(d_mixed, (group ^ j) * cols, cols) for j in range(groups)]
    d_heads = [d_heads[0]] + [swap(d_heads[j], "ulysses", j) for j in range(1, groups)]
    d_heads = jnp.concatenate(d_heads, 1).reshape(heads, HEAD, rows)

    x_mlp, w_up = after((x_mlp, w_up), kv, d_mixed)
    mlp_out, d_norm_two, begun, terms, g_up_bias = mlp(
        x_mlp, e_mlp, ln2_g, ln2_b, w_up, b_up, w_down, pieces[lax.axis_size("blk") // 2], pieces[1], d_heads
    )

    e_around = around(after(cotangent, begun))
    d_heads = after(d_heads, begun)
    mixed, d_q, kept, sent = attend(ranks, queries, d_heads, kv_all)

    sent, e_around, terms, mlp_out, d_norm_two = after((sent, e_around, terms, mlp_out, d_norm_two))
    d_q = rotate(d_q, cosine, -sine).astype(bf16).reshape(cols, rows)
    mixed = mixed.reshape(cols, rows)
    back_q = to_tokens(jnp.concatenate([d_q, mixed]))
    got = swap(sent, "blk", 1)
    step, kept = 1, [[kept[i], got[i]] for i in range(kept.shape[0])]
    while len(kept) > 1:
        step *= 2
        sent = sum(v.astype(f32) for v in stacked_terms(kept[1::2])).astype(bf16)
        if step == 2:
            terms = finish(terms, sent)
        sent, back_q = after((sent, back_q))
        got = swap(sent, "blk", step)
        kept = [kept[2 * i] + [got[i]] for i in range(got.shape[0])]
    total = sum(v.astype(f32) for v in kept[0])
    e_all = jnp.concatenate(e_around, 0)
    g_out = jnp.dot(mixed, e_all, preferred_element_type=f32).astype(bf16)
    d_k = rotate(total[:cols].reshape(heads, HEAD, rows), cosine, -sine).reshape(cols, rows)
    d_kv = jnp.concatenate([d_k, total[cols:]]).astype(bf16)
    d_joined = jnp.concatenate([d_q, d_kv])
    g_bias_mine = jnp.sum(d_joined.astype(f32), 1)
    g_qkv = jnp.dot(d_joined, normed, preferred_element_type=f32).astype(bf16)
    back_kv = to_tokens(d_kv)
    grads = jnp.concatenate([g_qkv.reshape(3, cols, width), g_out[None]])
    grads = add_blks(grads)
    back_kv = after(back_kv, grads)
    back_q, back_kv = by_device(back_q, group), by_device(back_kv, group)
    d_mine = jnp.concatenate(
        [v[:cols] for v in back_q] + [v[:cols] for v in back_kv] + [v[cols:] for v in back_kv], 0
    )
    d_norm_one = jnp.einsum("et,de->td", d_mine, w_qkv, preferred_element_type=f32)
    x_float = tokens.astype(f32)
    _, pull_one = jax.vjp(layer_norm, x_float, ln1_g, ln1_b)
    _, pull_two = jax.vjp(layer_norm, x_float, ln2_g, ln2_b)
    d_x_one, g_ln1_g, g_ln1_b = pull_one(d_norm_one)
    d_x_two, g_ln2_g, g_ln2_b = pull_two(d_norm_two)
    e_float = cotangent.astype(f32)

    g_qkv_bias = jnp.zeros((3, groups, cols), f32)
    g_qkv_bias = lax.dynamic_update_slice(g_qkv_bias, g_bias_mine.reshape(3, 1, cols), (0, group, 0))
    vectors = [g_ln1_g, g_ln1_b, g_ln2_g, g_ln2_b, jnp.sum(e_float, 0), g_qkv_bias.reshape(-1), g_up_bias]
    back = jnp.concatenate([v[cols:] for v in back_q], 0)
    attn_out = jnp.einsum("et,ed->td", back, w_out, preferred_element_type=f32)
    output = (x_float + (attn_out + b_out) + (mlp_out + b_down)).astype(bf16)
    input_grad = (e_float + d_x_one + d_x_two).astype(bf16)

    vector = jnp.concatenate(vectors)
    g_up, g_down = spread(terms, output, input_grad)
    g_qkv, g_out, summed = attention_grads(grads, vector, output, g_up)
    results, start = [], 0
    for vector in vectors:
        mine = vector.shape[0] // shards
        results.append(lax.dynamic_slice_in_dim(summed, start + lax.axis_index("fsdp") * mine, mine))
        start += vector.shape[0]
    g_ln1_g, g_ln1_b, g_ln2_g, g_ln2_b, g_e, g_qkv_bias, g_up_bias = results
    return (
        output,
        input_grad,
        g_ln1_g,
        g_ln1_b,
        g_ln2_g,
        g_ln2_b,
        g_qkv,
        g_qkv_bias,
        g_out,
        g_e,
        g_up,
        g_up_bias,
        g_down,
        g_e,
    )


def solution(mesh):
    rows = P(("fsdp", "blk", "ulysses"), None)
    split, matrix = P("fsdp"), P("fsdp", None)
    return jax.shard_map(
        on_device,
        mesh=mesh,
        in_specs=(
            rows,
            P(("fsdp", "blk", "ulysses")),
            rows,
            split,
            split,
            split,
            split,
            matrix,
            split,
            matrix,
            split,
            matrix,
            split,
            matrix,
            split,
        ),
        out_specs=(
            rows,
            rows,
            split,
            split,
            split,
            split,
            matrix,
            split,
            matrix,
            split,
            matrix,
            split,
            matrix,
            split,
        ),
        check_vma=False,
    )
```
